128 devices in a mesh: section: 2 (over x_hi), dp: 64 (over z, x_lo, y, core).
Axes of the slice: x: 4 (x_hi: 2, x_lo: 2; x = x_hi * 2 + x_lo), y: 4, z: 4, core: 2. Of those that a mesh axis runs over, the one named last changes fastest.
Arguments:
- tokens: bfloat16 [2, 4096, 768], P(None, 'dp'), may hold values from -6 to 6
- cotangent: bfloat16 [2, 4096, 768], P(None, 'dp'), may hold values from -6 to 6
- lengths: int32 [2, 64, 2], P(None, 'dp'), may hold values from 16 to 48, as said below
- routes: int32 [2, 2, 4096, 2], P('section', None, 'dp'), may hold values from 0 to 31, all different within a row; in each aligned block of 64 rows (0 to 63, 64 to 127, ..., all dimensions but the last counted through in order) at most 8 rows name the same one
- buckets: int32 [64], replicated, may hold values from 0 to 31, as said below
- qkv_weight: bfloat16 [2, 768, 2304], P('section', 'dp'), may hold values from -0.21875 to 0.21875
- out_weight: bfloat16 [2, 768, 768], P('section', 'dp'), may hold values from -0.625 to 0.625
- router_weight: bfloat16 [2, 768, 32], P('section', 'dp'), may hold values from -0.15625 to 0.15625
- norm1_gain: bfloat16 [2, 768], P('section', 'dp'), may hold values from 0.5 to 1.5
- norm2_gain: bfloat16 [2, 768], P('section', 'dp'), may hold values from 0.5 to 1.5
- rel_bias: bfloat16 [2, 384], P('section', 'dp'), may hold values from -4 to 4
- expert_in: bfloat16 [2, 64, 768, 1536], P('section', 'dp'), may hold values from -0.21875 to 0.21875
- expert_out: bfloat16 [2, 64, 1536, 768], P('section', 'dp'), may hold values from -0.21875 to 0.21875
Outputs:
- layer_outputs: bfloat16 [2, 2, 4096, 768], P('section', None, 'dp')
- input_grads: float32 [2, 2, 4096, 768], P('section', None, 'dp')
- qkv_grad: float32 [2, 768, 2304], P('section', 'dp')
- out_grad: float32 [2, 768, 768], P('section', 'dp')
- router_grad: float32 [2, 768, 32], P('section', 'dp')
- norm1_grad: float32 [2, 768], P('section', 'dp')
- norm2_grad: float32 [2, 768], P('section', 'dp')
- rel_bias_grad: float32 [2, 384], P('section', 'dp')
- expert_in_grad: float32 [2, 64, 768, 1536], P('section', 'dp')
- expert_out_grad: float32 [2, 64, 1536, 768], P('section', 'dp')
The draws below stay inside these ranges and needn't reach their ends.
Inputs may be any that keep to these rules, and one draw needn't show every extreme that they name: Each row holds the lengths 48 and 16, in either order. `routes`: a token's two experts differ; within the 64 rows of one device for one layer and micro-batch no expert is named more than 8 times, and 8 is reached. `buckets`: never falling; 0 at distance 0 and 31 at distance 64 - 1.
All inputs are finite; a program needn't handle non-finite values.
Results may differ from the reference program's by a relative error of at most 0.034.
Values may be sent and summed in bfloat16 or wider, within the bound.
No kernel may reach another device: no remote copies, remote signals or barrier semaphores. Data moves between devices by JAX's collectives and lax.ppermute only.
A program may use at most 192 MiB of HBM per device.

```python
import math
import jax
import jax.numpy as jnp
import numpy as np
from jax import lax

D = 768
H = 12
HD = 64
FF = 3072
TOK = 64
MB = 2
SEGS = 2
NB = 32
SPLIT = 2
TOP = 2
FFH = 1536
EXPERTS = 32
CAP = 8
MOST = 48
TOKENS = 4096
N_SECTION = 2
N_DP = 64


def draw_buckets(key, part):
    key = jax.random.fold_in(key, 7)
    distance = jnp.arange(TOK, dtype=jnp.int32)
    coins = jax.random.randint(key, (TOK,), 0, 4)
    steps_up = jnp.where(distance < NB // 4, 1, (coins == 0).astype(jnp.int32))
    steps_up = jnp.where(distance == 0, 0, steps_up)
    bucket_ids = jnp.minimum(jnp.cumsum(steps_up, dtype=jnp.int32), NB - 1)
    return jnp.where(distance == TOK - 1, NB - 1, bucket_ids).astype(jnp.int32)


def draw_lengths(key, part):
    key = jax.random.fold_in(key, 11)
    coins = jax.random.randint(key, (MB, N_DP, 1), 0, 2)
    first_len = jnp.where(coins == 1, MOST, TOK - MOST).astype(jnp.int32)
    return jnp.concatenate([first_len, TOK - first_len], axis=-1).astype(jnp.int32)


def levels(rng, shape, pieces, low, high):
    level, own = 1.0, jax.random.fold_in(rng, 6)
    for dim, shards_of in pieces:
        heights = jnp.exp(jax.random.uniform(jax.random.fold_in(own, dim), (shards_of,), jnp.float32, low / len(pieces), high / len(pieces)))
        level = level * jnp.repeat(heights, shape[dim] // shards_of).reshape([-1 if axis == dim else 1 for axis in range(len(shape))])
    return level


def routed_block(rng, own, number, rows, count, top, most, slope):
    sequence = jax.random.permutation(rng, count)
    packed, ordinary = load_shares(count, rows * top, most, slope, True), load_shares(count, rows * top, most, slope, False)
    places = jnp.arange(count)

    def named(tallies, offset_by):
        used = int((tallies > 0).sum())
        fixed = max(1, used // 4)
        shifted = fixed + (places - fixed + offset_by * (used - fixed)) % max(1, count - fixed)
        return jnp.zeros((count,), jnp.int32).at[sequence[jnp.where(places < fixed, places, shifted)]].set(jnp.asarray(tallies, jnp.int32))

    tallies = jnp.where(number % 4 == 0, named(packed, number // 4), named(ordinary, number - number // 4 - 1))
    mixed = jax.random.permutation(jax.random.fold_in(own, 3), count)
    source_of, receiver = mixed[0:count // 2 * 2:2], mixed[1:count // 2 * 2:2]
    margin = jnp.minimum(tallies[source_of] - 1, most - tallies[receiver]) // 2
    margin = jnp.where((source_of == sequence[0]) | (receiver == sequence[0]) | (tallies[receiver] == 0), 0, jnp.maximum(margin, 0))
    shifted = jax.random.randint(jax.random.fold_in(own, 4), (count // 2,), 0, 1 << 20) % (margin + 1)
    tallies = tallies.at[source_of].add(-shifted).at[receiver].add(shifted)
    members = jnp.searchsorted(jnp.cumsum(tallies), jnp.arange(rows * top), side="right").astype(jnp.int32)
    table = members.reshape(top, rows).T
    table = table[jax.random.permutation(jax.random.fold_in(own, 1), rows)]
    offset_by = jax.random.randint(jax.random.fold_in(own, 2), (rows, 1), 0, top)
    return jnp.take_along_axis(table, (jnp.arange(top)[None, :] + offset_by) % top, axis=1)


def load_shares(amount, total, most, lean, full):
    weights = [(1 << 20) // math.isqrt(rank ** lean) + 1 for rank in range(1, amount + 1)]
    largest = most if full else min(most, max(-(-total // amount), total * weights[0] // sum(weights)))
    least = 1 if total - largest >= amount - 1 else 0
    given, spare = [largest] + [least] * (amount - 1), total - largest - least * (amount - 1)
    while spare > 0:
        movable = [i for i in range(1, amount) if given[i] < largest] or [i for i in range(1, amount) if given[i] < most]
        pool, remaining = sum([weights[i] for i in movable]), spare
        for i in movable:
            extra = min(most - given[i], max(1, remaining * weights[i] // pool), spare)
            given[i] = given[i] + extra
            spare = spare - extra
    return np.array(given)


def gaussian(own_key, extent, deviation, reach, split=(), kind=jnp.bfloat16):
    result = jax.random.normal(own_key, extent, jnp.float32) * deviation
    if len(split) > 0:
        result = levels(own_key, extent, split, -0.22, 0.18) * result
    return jnp.clip(result, min=-reach, max=reach).astype(kind)


def setup_inputs(seed: int = 0) -> dict:
    key_list = jax.random.split(jax.random.key(seed), 14)
    tokens = gaussian(key_list[0], (MB, TOKENS, D), 1.0, 6.0, ((1, 64),))
    cotangent = gaussian(key_list[1], (MB, TOKENS, D), 1.0, 6.0, ((1, 64),))
    lengths = draw_lengths(jax.random.fold_in(key_list[13], 71), 0)
    routes_keys = jax.random.split(jax.random.fold_in(key_list[3], 1), N_SECTION * MB * TOKENS // TOK)
    routes_turns = jax.random.permutation(jax.random.fold_in(key_list[3], 3), N_SECTION * MB * TOKENS // TOK)
    routes = jax.vmap(lambda own, number: routed_block(jax.random.fold_in(key_list[3], 2), own, number, TOK, EXPERTS, TOP, CAP, 2))(routes_keys, routes_turns).reshape((N_SECTION, MB, TOKENS, TOP))
    buckets = draw_buckets(jax.random.fold_in(key_list[13], 71), 0)
    qkv_weight = gaussian(key_list[5], (N_SECTION, D, 3 * D), D ** -0.5, 0.21875, ((0, 2), (1, 64)))
    out_weight = gaussian(key_list[6], (N_SECTION, D, D), (D // 8) ** -0.5, 0.625, ((0, 2), (1, 64)))
    router_weight = gaussian(key_list[7], (N_SECTION, D, EXPERTS), (2 * D) ** -0.5, 0.15625, ((0, 2), (1, 64)))
    norm1_gain = jnp.clip(1.0 + 0.1 * jax.random.normal(key_list[8], (N_SECTION, D), jnp.float32), 0.5, 1.5).astype(jnp.bfloat16)
    norm2_gain = jnp.clip(1.0 + 0.1 * jax.random.normal(key_list[9], (N_SECTION, D), jnp.float32), 0.5, 1.5).astype(jnp.bfloat16)
    rel_bias = gaussian(key_list[10], (N_SECTION, NB * H), 1.0, 4.0, ((0, 2), (1, 64)))
    expert_in = gaussian(key_list[11], (N_SECTION, N_DP, D, FFH), D ** -0.5, 0.21875, ((0, 2), (1, 64)))
    expert_out = gaussian(key_list[12], (N_SECTION, N_DP, FFH, D), (FF // 4) ** -0.5, 0.21875, ((0, 2), (1, 64)))
    return {"tokens": tokens, "cotangent": cotangent, "lengths": lengths, "routes": routes, "buckets": buckets, "qkv_weight": qkv_weight, "out_weight": out_weight, "router_weight": router_weight, "norm1_gain": norm1_gain, "norm2_gain": norm2_gain, "rel_bias": rel_bias, "expert_in": expert_in, "expert_out": expert_out}


@jax.custom_vjp
def low(v):
    return lax.optimization_barrier(v.astype(jnp.bfloat16)).astype(jnp.float32)

@jax.custom_vjp
def low_back(v):
    return v

def low_keep(v):
    return (low(v), None)

def low_pass(kept, grad):
    return (grad,)

def back_keep(v):
    return (v, None)

def back_low(kept, grad):
    return (low(grad),)
low.defvjp(low_keep, low_pass)
low_back.defvjp(back_keep, back_low)
EPSILON = 1e-06
PRECISE = lax.Precision.HIGHEST

def norm_rows(values, gain):
    return values * lax.rsqrt(lax.optimization_barrier(jnp.mean(values * values, axis=-1, keepdims=True)) + EPSILON) * gain

def smooth_gate(pre_value):
    return jax.nn.gelu(pre_value, approximate=True)

def seq_visible(seg_lengths):
    positions = jnp.arange(TOK, dtype=jnp.int32)
    seg_ends = jnp.cumsum(seg_lengths, axis=-1, dtype=jnp.int32)
    segment = lax.optimization_barrier(jnp.sum((positions[None, :, None] >= seg_ends[:, None, :]).astype(jnp.int32), axis=-1, dtype=jnp.int32))
    causal = positions[:, None] >= positions[None, :]
    return (segment[:, :, None] == segment[:, None, :]) & causal[None]

def bucket_table(buckets):
    span_length = buckets.shape[0]
    positions = jnp.arange(span_length, dtype=jnp.int32)
    distance = jnp.clip(positions[:, None] - positions[None, :], 0, span_length - 1).astype(jnp.int32)
    bucket_of = jnp.take(buckets, distance, axis=0)
    return (bucket_of[:, :, None] == jnp.arange(NB, dtype=jnp.int32)[None, None, :]).astype(jnp.float32)

def slot_table(route_ids, experts, capacity):
    blocks = route_ids.shape[0]
    flat_ids = route_ids.reshape(blocks, -1)
    onehot = (flat_ids[..., None] == jnp.arange(experts, dtype=jnp.int32)).astype(jnp.int32)
    earlier = jnp.cumsum(onehot, axis=1, dtype=jnp.int32) - onehot
    rank_in = lax.optimization_barrier(jnp.sum(earlier * onehot, axis=-1, dtype=jnp.int32))
    return ((flat_ids * capacity + rank_in).astype(jnp.int32), onehot)

def expert_pair(operands):
    rows_in, first_matrix, second_matrix = operands
    total = jnp.zeros(rows_in.shape, jnp.float32)
    for half_index in range(SPLIT):
        arriving = low_back(rows_in)
        pre_act = low_back(jnp.matmul(arriving, first_matrix[half_index], precision=PRECISE))
        hidden = low(smooth_gate(pre_act))
        total = total + low_back(low(jnp.matmul(hidden, second_matrix[half_index], precision=PRECISE)))
    return total

def layer_fn(layer_in, qkv_matrix, out_matrix, router_matrix, gain_one, gain_two, rel_matrix, first_matrix, second_matrix, visible, bias_table, slot_ids, onehot):
    blocks, row_count, model_width = layer_in.shape
    normed = low(norm_rows(layer_in, gain_one))
    projected = low_back(low(jnp.matmul(normed, qkv_matrix, precision=PRECISE)))
    heads_all = projected.reshape(blocks, row_count, 3, H, HD)
    bias_heads = jnp.einsum('ijn,nh->hij', bias_table, rel_matrix.reshape(NB, H), precision=PRECISE)
    scores = jnp.einsum('bihd,bjhd->bhij', heads_all[:, :, 0], heads_all[:, :, 1], precision=PRECISE) * HD ** (-0.5) + bias_heads[None]
    scores = low_back(scores)
    scores = jnp.where(visible[:, None], scores, -1e+30)
    probabilities = low(jax.nn.softmax(scores, axis=-1))
    attended = jnp.einsum('bhij,bjhd->bihd', probabilities, heads_all[:, :, 2], precision=PRECISE).reshape(blocks, row_count, model_width)
    attended = low_back(low(attended))
    middle = layer_in + low_back(jnp.matmul(attended, out_matrix, precision=PRECISE))
    moe_in = low(norm_rows(middle, gain_two))
    logits = jnp.matmul(moe_in, router_matrix, precision=PRECISE)
    chosen = onehot.reshape(blocks, row_count, TOP, EXPERTS).astype(jnp.float32)
    picked = jnp.einsum('btke,bte->btk', chosen, logits, precision=PRECISE)
    gate_weights = jax.nn.softmax(picked, axis=-1)
    dispatch = (slot_ids[..., None] == jnp.arange(EXPERTS * CAP, dtype=jnp.int32)).astype(jnp.float32)
    doubled = jnp.repeat(moe_in, TOP, axis=1)
    buffer = jnp.einsum('brs,brd->bsd', dispatch, doubled, precision=PRECISE)
    per_expert = buffer.reshape(blocks, EXPERTS, CAP, model_width).transpose(1, 0, 2, 3).reshape(EXPERTS, blocks * CAP, model_width)
    made = lax.map(jax.checkpoint(expert_pair), (per_expert, first_matrix.reshape(EXPERTS, SPLIT, model_width, FFH), second_matrix.reshape(EXPERTS, SPLIT, FFH, model_width)))
    back_rows = made.reshape(EXPERTS, blocks, CAP, model_width).transpose(1, 0, 2, 3).reshape(blocks, EXPERTS * CAP, model_width)
    picked_rows = jnp.einsum('brs,bsd->brd', dispatch, back_rows, precision=PRECISE).reshape(blocks, row_count, TOP, model_width)
    return middle + lax.optimization_barrier(jnp.sum(gate_weights[..., None] * picked_rows, axis=2))

def reference(tokens, cotangent, lengths, routes, buckets, qkv_weight, out_weight, router_weight, norm1_gain, norm2_gain, rel_bias, expert_in, expert_out):
    blocks = MB * N_DP
    visible = seq_visible(lengths.reshape(blocks, SEGS))
    bias_table = bucket_table(buckets)
    route_blocks = routes.reshape(N_SECTION, blocks, TOK, TOP)
    tables = [slot_table(route_blocks[layer_index], EXPERTS, CAP) for layer_index in range(N_SECTION)]
    start = tokens.astype(jnp.float32).reshape(blocks, TOK, D)
    shifts = jnp.zeros((N_SECTION, blocks, TOK, D), jnp.float32)
    params = tuple((member.astype(jnp.float32) for member in (qkv_weight, out_weight, router_weight, norm1_gain, norm2_gain, rel_bias, expert_in, expert_out)))

    def forward(start_rows, shift_rows, qkv_all, out_all, router_all, gain_one_all, gain_two_all, rel_all, first_all, second_all):
        current = start_rows
        outputs = []
        for layer_index in range(N_SECTION):
            if layer_index > 0:
                current = low_back(low(current)) + shift_rows[layer_index]
            current = layer_fn(current, qkv_all[layer_index], out_all[layer_index], router_all[layer_index], gain_one_all[layer_index], gain_two_all[layer_index], rel_all[layer_index], first_all[layer_index], second_all[layer_index], visible, bias_table, tables[layer_index][0], tables[layer_index][1])
            outputs.append(current)
        return (current, jnp.stack(outputs))
    final_rows, pullback, outputs = jax.vjp(forward, start, shifts, *params, has_aux=True)
    gradients = pullback(cotangent.astype(jnp.float32).reshape(blocks, TOK, D))
    input_grads = gradients[1].at[0].set(gradients[0]).reshape(N_SECTION, MB, TOKENS, D)
    layer_outputs = outputs.astype(jnp.bfloat16).reshape(N_SECTION, MB, TOKENS, D)
    return (layer_outputs, input_grads, gradients[2], gradients[3], gradients[4], gradients[5], gradients[6], gradients[7], gradients[8], gradients[9])
```

```python
import jax
import jax.numpy as jnp
from jax import lax
from jax.sharding import Mesh, PartitionSpec as P

D = 768
H = 12
HD = 64
TOK = 64
MB = 2
NB = 32
TOP = 2
CAP = 8
ROWS = MB * TOK
LANES = 128

EPSILON = 1e-06
PRECISE = lax.Precision.HIGHEST
BF = jnp.bfloat16
F32 = jnp.float32


def mm(a, b):
    return jnp.dot(a, b, preferred_element_type=F32)


def mm_nt(a, b):
    return lax.dot_general(a, b, (((1,), (1,)), ((), ())), preferred_element_type=F32)


def mm_tn(a, b):
    return lax.dot_general(a, b, (((0,), (0,)), ((), ())), preferred_element_type=F32)


def core_swap(value):
    return lax.ppermute(value, "core", [(0, 1), (1, 0)])


def chip_exchange(value):
    return lax.all_to_all(value, "chip", split_axis=0, concat_axis=0, tiled=True)


def norm_rows(values, gain):
    return values * lax.rsqrt(jnp.mean(values * values, axis=-1, keepdims=True) + EPSILON) * gain


def norm_back(values, gain, grad_in):
    factor = lax.rsqrt(jnp.mean(values * values, axis=-1, keepdims=True) + EPSILON)
    normed = values * factor
    weighted = grad_in * gain
    value_grad = factor * (weighted - normed * jnp.mean(weighted * normed, axis=-1, keepdims=True))
    return (value_grad, jnp.sum(grad_in * normed, axis=0))


def smooth_gate(pre_value):
    return jax.nn.gelu(pre_value, approximate=True)


def seq_visible(seg_lengths):
    positions = jnp.arange(TOK, dtype=jnp.int32)
    seg_ends = jnp.cumsum(seg_lengths, axis=-1, dtype=jnp.int32)
    segment = jnp.sum(
        (positions[None, :, None] >= seg_ends[:, None, :]).astype(jnp.int32),
        axis=-1,
        dtype=jnp.int32,
    )
    causal = positions[:, None] >= positions[None, :]
    return (segment[:, :, None] == segment[:, None, :]) & causal[None]


def bucket_table(buckets):
    positions = jnp.arange(TOK, dtype=jnp.int32)
    distance = jnp.clip(positions[:, None] - positions[None, :], 0, TOK - 1)
    steps = (distance[:, :, None] == positions).astype(BF).reshape(TOK * TOK, TOK)
    chosen = (buckets[:, None] == jnp.arange(NB, dtype=jnp.int32)[None, :]).astype(BF)
    return mm(steps, chosen).astype(BF).reshape(TOK, TOK, NB)


def slot_table(routes, experts):
    flat = routes.reshape(MB, TOK * TOP)
    onehot = (flat[..., None] == jnp.arange(experts, dtype=jnp.int32)).astype(jnp.int32)
    earlier = jnp.cumsum(onehot, axis=1, dtype=jnp.int32) - onehot
    rank = jnp.sum(earlier * onehot, axis=-1, dtype=jnp.int32)
    micro = jnp.arange(MB, dtype=jnp.int32)[:, None]
    slots = flat * (MB * CAP) + micro * CAP + rank
    return slots.reshape(ROWS, TOP), onehot.reshape(ROWS, TOP, experts).astype(F32)


def pack_columns(qkv, out, router, gain_one, gain_two, rel):
    rows = qkv.shape[0]
    rel_column = jnp.pad(rel, (0, rows - rel.shape[0]))
    extras = jnp.concatenate(
        [router, gain_one[:, None], gain_two[:, None], rel_column[:, None]], axis=1
    )
    extras = jnp.pad(extras, ((0, 0), (0, LANES - extras.shape[1])))
    return jnp.concatenate([qkv, out, extras], axis=1)


def gather_dense(shard, core, chips):
    rows, width = shard.shape
    offset = width // LANES // 2 * LANES
    piece = width - offset
    other = core_swap(shard)
    pair = jnp.concatenate(
        [jnp.where(core == 0, shard, other), jnp.where(core == 0, other, shard)], axis=0
    )
    half = lax.dynamic_slice(pair, (0, core * offset), (2 * rows, piece))
    spread = jnp.broadcast_to(half[None], (chips, 2 * rows, piece))
    mine = chip_exchange(spread).reshape(chips * 2 * rows, piece)
    theirs = core_swap(mine)
    low = jnp.where(core == 0, mine, theirs)
    high = jnp.where(core == 0, theirs, mine)
    return jnp.concatenate([low[:, :offset], high], axis=1)


def scatter_dense(total, core, chips):
    depth, width = total.shape
    rows = depth // chips // 2
    offset = width // LANES // 2 * LANES
    piece = width - offset
    mine = lax.dynamic_slice(total, (0, core * offset), (depth, piece))
    theirs = lax.dynamic_slice(total, (0, (1 - core) * offset), (depth, piece)).astype(BF)
    mine = (mine + core_swap(theirs).astype(F32)).astype(BF)
    arrived = chip_exchange(mine.reshape(chips, 2 * rows, piece))
    summed = jnp.sum(arrived.astype(F32), axis=0)
    own = lax.dynamic_slice(summed, (core * rows, 0), (rows, piece))
    given = lax.dynamic_slice(summed, ((1 - core) * rows, 0), (rows, piece))
    other = core_swap(given)
    low = jnp.where(core == 0, own, other)
    high = jnp.where(core == 0, other, own)
    return jnp.concatenate([low[:, :offset], high], axis=1)


def to_experts(rows, chips):
    mine = chip_exchange(rows.reshape(chips, -1, rows.shape[-1])).reshape(rows.shape)
    return mine, core_swap(mine)


def from_experts(mine, theirs, chips):
    total = (mine.astype(F32) + core_swap(theirs).astype(F32)).astype(BF)
    return chip_exchange(total.reshape(chips, -1, total.shape[-1])).reshape(total.shape)


def heads(values):
    return values.reshape(MB, TOK, H, HD)


def attention_scores(query, key, bias_heads, visible):
    scores = (
        jnp.einsum("bihd,bjhd->bhij", query, key, preferred_element_type=F32) * HD ** (-0.5)
        + bias_heads[None]
    )
    return jnp.where(visible[:, None], scores, -1e30)


def split_heads(projected):
    return tuple(heads(projected[:, part * D : (part + 1) * D]) for part in range(3))


def forward_layer(layer_in, weights, bias_heads, visible, picks, first, second, chips):
    qkv, out, router, gain_one, gain_two = weights
    pick_list, spread, chosen = picks
    normed = norm_rows(layer_in, gain_one).astype(BF)
    projected = mm(normed, qkv).astype(BF)
    query, key, value = split_heads(projected)
    scores = attention_scores(query, key, bias_heads, visible)
    probabilities = jax.nn.softmax(scores, axis=-1)
    attended = jnp.einsum(
        "bhij,bjhd->bihd", probabilities.astype(BF), value, preferred_element_type=F32
    )
    attended = attended.reshape(ROWS, D).astype(BF)
    middle = layer_in + mm(attended, out)
    moe_in = norm_rows(middle, gain_two).astype(BF)
    logits = mm(moe_in, router)
    gates = jax.nn.softmax(jnp.sum(chosen * logits[:, None, :], axis=-1), axis=-1)
    buffer = mm_tn(spread, moe_in).astype(BF)
    arrived = to_experts(buffer, chips)
    pre = tuple(mm(rows, first) for rows in arrived)
    made = tuple(mm(smooth_gate(value).astype(BF), second).astype(BF) for value in pre)
    returned = from_experts(made[0], made[1], chips)
    picked = tuple(mm(table, returned) for table in pick_list)
    result = middle + gates[:, :1] * picked[0] + gates[:, 1:] * picked[1]
    saved = (layer_in, normed, projected, probabilities, attended, middle, moe_in, gates, picked, arrived, pre)
    return result, saved


def backward_layer(grad_out, weights, bias_table, picks, first, second, saved, chips, totals):
    qkv, out, router, gain_one, gain_two = weights
    pick_list, spread, chosen = picks
    layer_in, normed, projected, probabilities, attended, middle, moe_in, gates, picked, arrived, pre = saved
    gate_grad = jnp.stack([jnp.sum(rows * grad_out, axis=-1) for rows in picked], axis=-1)
    slot_grad = [(gates[:, k : k + 1] * grad_out).astype(BF) for k in range(TOP)]
    buffer_grad = (mm_tn(pick_list[0], slot_grad[0]) + mm_tn(pick_list[1], slot_grad[1])).astype(BF)
    grads = to_experts(buffer_grad, chips)
    row_grad, first_total, second_total = [], 0.0, 0.0
    for rows, pre_value, rows_grad in zip(arrived, pre, grads):
        hidden, gelu_back = jax.vjp(smooth_gate, pre_value)
        pre_grad = gelu_back(mm_nt(rows_grad, second))[0].astype(BF)
        row_grad.append(mm_nt(pre_grad, first).astype(BF))
        if totals:
            second_total = second_total + mm_tn(hidden.astype(BF), rows_grad)
            first_total = first_total + mm_tn(rows, pre_grad)
    returned = from_experts(row_grad[0], row_grad[1], chips)
    moe_grad = mm(spread, returned)
    picked_grad = gates * (gate_grad - jnp.sum(gates * gate_grad, axis=-1, keepdims=True))
    logit_grad = jnp.sum(chosen * picked_grad[..., None], axis=1)
    moe_grad = moe_grad + lax.dot_general(
        logit_grad, router.astype(F32), (((1,), (1,)), ((), ())), precision=PRECISE
    )
    middle_grad, gain_two_total = norm_back(middle, gain_two, moe_grad)
    middle_grad = middle_grad + grad_out
    branch_grad = middle_grad.astype(BF)
    attended_grad = heads(mm_nt(branch_grad, out).astype(BF))
    query, key, value = split_heads(projected)
    value_grad = jnp.einsum(
        "bhij,bihd->bjhd", probabilities.astype(BF), attended_grad, preferred_element_type=F32
    )
    prob_grad = jnp.einsum("bihd,bjhd->bhij", attended_grad, value, preferred_element_type=F32)
    score_grad = (
        probabilities * (prob_grad - jnp.sum(probabilities * prob_grad, axis=-1, keepdims=True))
    ).astype(BF)
    scale = HD ** (-0.5)
    query_grad = jnp.einsum("bhij,bjhd->bihd", score_grad, key, preferred_element_type=F32) * scale
    key_grad = jnp.einsum("bhij,bihd->bjhd", score_grad, query, preferred_element_type=F32) * scale
    projected_grad = jnp.concatenate(
        [value.reshape(ROWS, D).astype(BF) for value in (query_grad, key_grad, value_grad)], axis=1
    )
    normed_grad = mm_nt(projected_grad, qkv)
    input_grad, gain_one_total = norm_back(layer_in, gain_one, normed_grad)
    input_grad = input_grad + middle_grad
    if not totals:
        return input_grad, None, None
    qkv_total = mm_tn(normed, projected_grad)
    out_total = mm_tn(attended, branch_grad)
    router_total = lax.dot_general(
        moe_in.astype(F32), logit_grad, (((0,), (0,)), ((), ())), precision=PRECISE
    )
    rel_total = jnp.einsum(
        "ijn,hij->nh", bias_table.astype(F32), jnp.sum(score_grad.astype(F32), axis=0), precision=PRECISE
    ).reshape(-1)
    dense = (qkv_total, out_total, router_total, gain_one_total, gain_two_total, rel_total)
    return input_grad, dense, (first_total, second_total)


def per_device(
    tokens,
    cotangent,
    lengths,
    routes,
    buckets,
    qkv_weight,
    out_weight,
    router_weight,
    norm1_gain,
    norm2_gain,
    rel_bias,
    expert_in,
    expert_out,
):
    chips = lax.axis_size("chip")
    core = lax.axis_index("core")
    section = lax.axis_index("section")
    last = lax.axis_size("section") - 1
    experts = router_weight.shape[2]
    first, second = expert_in[0, 0], expert_out[0, 0]
    shard = pack_columns(
        qkv_weight[0], out_weight[0], router_weight[0], norm1_gain[0], norm2_gain[0], rel_bias[0]
    )
    dense = gather_dense(shard, core, chips)
    qkv, out = dense[:, : 3 * D], dense[:, 3 * D : 4 * D]
    extras = dense[:, 4 * D :]
    router = extras[:, :experts]
    gain_one = extras[:, experts].astype(F32)
    gain_two = extras[:, experts + 1].astype(F32)
    own_rel = NB * H // (2 * chips)
    rel = extras[:, experts + 2].reshape(2 * chips, -1)[:, :own_rel].reshape(NB, H)
    weights = (qkv, out, router, gain_one, gain_two)
    visible = seq_visible(lengths[:, 0, :])
    slots, chosen = slot_table(routes[0], experts)
    slot_iota = jnp.arange(experts * MB * CAP, dtype=jnp.int32)[None, :]
    pick_list = tuple((slots[:, k : k + 1] == slot_iota).astype(BF) for k in range(TOP))
    picks = (pick_list, pick_list[0] + pick_list[1], chosen)
    bias_table = bucket_table(buckets)
    bias_heads = jnp.einsum("ijn,nh->hij", bias_table, rel, preferred_element_type=F32)

    begin = tokens.reshape(ROWS, D).astype(F32)
    result, _ = forward_layer(begin, weights, bias_heads, visible, picks, first, second, chips)
    passed = lax.ppermute(result.astype(BF), "section", [(0, 1)]).astype(F32)
    layer_in = jnp.where(section == 0, begin, passed)
    result, saved = forward_layer(layer_in, weights, bias_heads, visible, picks, first, second, chips)
    layer_outputs = result.astype(BF)

    ending = cotangent.reshape(ROWS, D).astype(F32)
    input_grad, _, _ = backward_layer(
        ending, weights, bias_table, picks, first, second, saved, chips, False
    )
    passed = lax.ppermute(input_grad.astype(BF), "section", [(1, 0)]).astype(F32)
    grad_out = jnp.where(section == last, ending, passed)
    input_grad, totals, expert_totals = backward_layer(
        grad_out, weights, bias_table, picks, first, second, saved, chips, True
    )
    qkv_total, out_total, router_total, one_total, two_total, rel_total = totals
    rows = qkv_weight.shape[1]
    rel_column = jnp.pad(rel_total.reshape(2 * chips, own_rel), ((0, 0), (0, rows - own_rel)))
    small = jnp.concatenate(
        [router_total, one_total[:, None], two_total[:, None], rel_column.reshape(-1, 1)], axis=1
    )
    count = small.shape[1]
    exact = lax.reduce_precision(small, 8, 7)
    small = jnp.pad(
        jnp.concatenate([exact, small - exact], axis=1), ((0, 0), (0, LANES - 2 * count))
    )
    own = scatter_dense(jnp.concatenate([qkv_total, out_total, small], axis=1), core, chips)
    small = own[:, 4 * D : 4 * D + count] + own[:, 4 * D + count : 4 * D + 2 * count]
    return (
        layer_outputs.reshape(1, MB, TOK, D),
        input_grad.reshape(1, MB, TOK, D),
        own[None, :, : 3 * D],
        own[None, :, 3 * D : 4 * D],
        small[None, :, :experts],
        small[None, :, experts],
        small[None, :, experts + 1],
        small[None, :own_rel, experts + 2],
        expert_totals[0][None, None],
        expert_totals[1][None, None],
    )


def solution(mesh):
    sections, members = mesh.devices.shape
    fine = Mesh(mesh.devices.reshape(sections, members // 2, 2), ("section", "chip", "core"))
    dp = ("chip", "core")
    return jax.shard_map(
        per_device,
        mesh=fine,
        in_specs=(
            P(None, dp, None),
            P(None, dp, None),
            P(None, dp, None),
            P("section", None, dp, None),
            P(),
            P("section", dp, None),
            P("section", dp, None),
            P("section", dp, None),
            P("section", dp),
            P("section", dp),
            P("section", dp),
            P("section", dp, None, None),
            P("section", dp, None, None),
        ),
        out_specs=(
            P("section", None, dp, None),
            P("section", None, dp, None),
            P("section", dp, None),
            P("section", dp, None),
            P("section", dp, None),
            P("section", dp),
            P("section", dp),
            P("section", dp),
            P("section", dp, None, None),
            P("section", dp, None, None),
        ),
        check_vma=False,
    )
```

```python
import functools

import jax
import jax.numpy as jnp
from jax import lax
from jax.experimental import pallas as pl
from jax.experimental.pallas import tpu as pltpu
from jax.sharding import Mesh, PartitionSpec as P

D = 768
H = 12
HD = 64
TOK = 64
MB = 2
NB = 32
TOP = 2
CAP = 8
ROWS = MB * TOK
LANES = 128
EXPERTS = 32
SLOTS = MB * CAP
FFH = 1536
QH = 3 * D // 2
OH = D // 2
WIDE = QH + OH + LANES
GAIN_AT = EXPERTS
REL_AT = EXPERTS + 2
REL_OWN = 6
OWN = 12
BLOCKS = 4
BLOCK = FFH // BLOCKS

EPSILON = 1e-06
SCALE = HD ** (-0.5)
BF = jnp.bfloat16
F32 = jnp.float32
VMEM = pl.BlockSpec(memory_space=pltpu.VMEM)
SMEM = pl.BlockSpec(memory_space=pltpu.SMEM)
LIMIT = 48 * 1024 * 1024


def mm(a, b):
    return jnp.dot(a, b, preferred_element_type=F32)


def mm_nt(a, b):
    return lax.dot_general(a, b, (((1,), (1,)), ((), ())), preferred_element_type=F32)


def mm_tn(a, b):
    return lax.dot_general(a, b, (((0,), (0,)), ((), ())), preferred_element_type=F32)


def halves(value):
    high = value.astype(BF)
    return high, (value - high.astype(F32)).astype(BF)


def core_swap(value):
    return lax.ppermute(value, "core", [(0, 1), (1, 0)])


def chip_exchange(value):
    return lax.all_to_all(value, "chip", split_axis=0, concat_axis=0, tiled=True)


def iota(shape, axis):
    return lax.broadcasted_iota(jnp.int32, shape, axis)


def places(core, width):
    mine = pl.multiple_of(core * width, LANES)
    theirs = pl.multiple_of((1 - core) * width, LANES)
    return pl.ds(mine, width), pl.ds(theirs, width)


def gain_rows(mine_ref):
    chosen = (iota((16, LANES), 1) == iota((16, LANES), 0) + GAIN_AT).astype(BF)
    return mm_nt(chosen, mine_ref[:, QH + OH :])


def norm_factor(values):
    return lax.rsqrt(jnp.mean(values * values, axis=-1, keepdims=True) + EPSILON)


def norm_back(values, gain, grad_in):
    factor = norm_factor(values)
    normed = values * factor
    weighted = grad_in * gain
    value_grad = factor * (weighted - normed * jnp.mean(weighted * normed, axis=-1, keepdims=True))
    return value_grad, grad_in * normed


def gelu_parts(pre):
    outer = 0.7978845608028654
    inner = outer * 0.044715
    square = pre * pre
    share = 0.5 + 0.5 * jnp.tanh(pre * (outer + inner * square))
    hidden = pre * share
    return share, hidden, square


def gelu_slope(share, hidden, square):
    outer = 0.7978845608028654
    inner = outer * 0.044715
    return share + hidden * (1.0 - share) * (2.0 * outer + 6.0 * inner * square)


def slot_rows(slots_t_ref, k):
    return iota((EXPERTS * SLOTS, ROWS), 0) == slots_t_ref[k : k + 1, :]


def slot_columns(slots_ref, k):
    return iota((ROWS, EXPERTS * SLOTS), 1) == slots_ref[:, k : k + 1]


def bucket_rows(target_ref, part):
    return (iota((D, LANES), 0) == target_ref[...] + OWN * part).astype(BF)


def front(saving, core_ref, x_ref, mine_ref, theirs_ref, mask_ref, target_ref, slots_ref, slots_t_ref, *refs):
    if saving:
        grad_ref, normed_ref, projected_ref, probs_ref, attended_ref, middle_ref, moe_ref, gates_ref, buffer_ref = refs
    else:
        middle_ref, gates_ref, buffer_ref, projected_ref, attended_ref = refs
    core = core_ref[0]
    x = x_ref[...].astype(F32)
    gains = gain_rows(mine_ref)
    normed = (x * norm_factor(x) * gains[0:1]).astype(BF)
    if saving:
        normed_ref[...] = normed
    own, other = places(core, QH)
    projected_ref[:, own] = mm(normed, mine_ref[:, :QH]).astype(BF)
    projected_ref[:, other] = mm(normed, theirs_ref[:, :QH]).astype(BF)
    extras = mine_ref[:, QH + OH :]
    rel = [mm_tn(extras, bucket_rows(target_ref, part)) for part in range(2)]
    mask = mask_ref[...]
    low_lanes = iota((1, LANES), 1) < HD
    for pair in range(H // 2):
        at = pair * LANES
        query = projected_ref[:, at : at + LANES]
        key = projected_ref[:, D + at : D + at + LANES]
        value = projected_ref[:, 2 * D + at : 2 * D + at + LANES]
        result = jnp.zeros((ROWS, LANES), F32)
        for side in range(2):
            head = 2 * pair + side
            chosen = low_lanes if side == 0 else jnp.logical_not(low_lanes)
            row = REL_AT + head % REL_OWN
            spread = jnp.broadcast_to(rel[head // REL_OWN][row : row + 1, :], (ROWS, LANES))
            bias = pltpu.roll(spread, 0, 1, stride=1, stride_axis=0)
            scores = mm_nt(jnp.where(chosen, query, jnp.zeros_like(query)), key) * SCALE + bias + mask
            raised = jnp.exp(scores - jnp.max(scores, axis=-1, keepdims=True))
            probs = raised / jnp.sum(raised, axis=-1, keepdims=True)
            if saving:
                probs_ref[head] = probs
            result = result + mm(probs.astype(BF), jnp.where(chosen, value, jnp.zeros_like(value)))
        attended_ref[:, at : at + LANES] = result.astype(BF)
    attended = attended_ref[...]
    own, other = places(core, OH)
    middle_ref[:, own] = mm(attended, mine_ref[:, QH : QH + OH])
    middle_ref[:, other] = mm(attended, theirs_ref[:, QH : QH + OH])
    middle = x + middle_ref[...]
    middle_ref[...] = middle
    moe_in = (middle * norm_factor(middle) * gains[1:2]).astype(BF)
    logits = mm(moe_in, extras)
    lane = iota((ROWS, LANES), 1)
    picked = [
        jnp.sum(jnp.where(lane == slots_ref[:, k : k + 1] // SLOTS, logits, 0.0), axis=-1, keepdims=True)
        for k in range(TOP)
    ]
    peak = jnp.maximum(picked[0], picked[1])
    raised = [jnp.exp(value - peak) for value in picked]
    gates = [value / (raised[0] + raised[1]) for value in raised]
    gates_ref[...] = jnp.where(lane == 0, gates[0], jnp.where(lane == 1, gates[1], 0.0))
    tables = [slot_rows(slots_t_ref, k) for k in range(TOP)]
    buffer = mm((tables[0] | tables[1]).astype(BF), moe_in).astype(BF)
    buffer_ref[:, :SLOTS, :] = buffer.reshape(EXPERTS, SLOTS, D)
    if saving:
        moe_ref[...] = moe_in
        grad = grad_ref[...].astype(F32)
        buffer_ref[:, SLOTS:, :] = spread_grad(tables, gates, grad).reshape(EXPERTS, SLOTS, D)


def spread_grad(tables, gates, grad):
    return sum(
        mm(table.astype(BF), (gate * grad).astype(BF)) for table, gate in zip(tables, gates)
    ).astype(BF)


def send_grad(gates_ref, grad_ref, slots_t_ref, buffer_ref):
    grad = grad_ref[...].astype(F32)
    gates = [gates_ref[:, k : k + 1] for k in range(TOP)]
    tables = [slot_rows(slots_t_ref, k) for k in range(TOP)]
    buffer_ref[...] = spread_grad(tables, gates, grad).reshape(EXPERTS, SLOTS, D)


def expert_forward(rows_ref, first_ref, second_ref, made_ref, total_ref):
    step = pl.program_id(0)
    rows = rows_ref[...].reshape(-1, D)
    _, hidden, _ = gelu_parts(mm(rows, first_ref[...]))
    part = mm(hidden.astype(BF), second_ref[...])

    @pl.when(step == 0)
    def _():
        total_ref[...] = part

    @pl.when(step > 0)
    def _():
        total_ref[...] += part

    @pl.when(step == BLOCKS - 1)
    def _():
        made_ref[...] = total_ref[...].astype(BF).reshape(made_ref.shape)


def expert_both(rows_ref, first_ref, second_ref, made_ref, hidden_ref, slope_ref, total_ref, back_ref):
    step = pl.program_id(0)
    rows = rows_ref[:, :SLOTS, :].reshape(-1, D)
    grads = rows_ref[:, SLOTS:, :].reshape(-1, D)
    share, hidden, square = gelu_parts(mm(rows, first_ref[...]))
    hidden_ref[...] = hidden.astype(BF)
    slope = gelu_slope(share, hidden, square)
    slope_ref[...] = slope.astype(BF)
    part = mm(hidden.astype(BF), second_ref[...])
    pre_grad = (mm_nt(grads, second_ref[...]) * slope).astype(BF)
    back = mm_nt(pre_grad, first_ref[...])

    @pl.when(step == 0)
    def _():
        total_ref[...] = part
        back_ref[...] = back

    @pl.when(step > 0)
    def _():
        total_ref[...] += part
        back_ref[...] += back

    @pl.when(step == BLOCKS - 1)
    def _():
        made_ref[:, :SLOTS, :] = total_ref[...].astype(BF).reshape(-1, SLOTS, D)
        made_ref[:, SLOTS:, :] = back_ref[...].astype(BF).reshape(-1, SLOTS, D)


def expert_back(grads_ref, first_ref, second_ref, slope_ref, made_ref, pre_ref, back_ref):
    step = pl.program_id(0)
    grads = grads_ref[...].reshape(-1, D)
    pre_grad = (mm_nt(grads, second_ref[...]) * slope_ref[...].astype(F32)).astype(BF)
    pre_ref[...] = pre_grad
    back = mm_nt(pre_grad, first_ref[...])

    @pl.when(step == 0)
    def _():
        back_ref[...] = back

    @pl.when(step > 0)
    def _():
        back_ref[...] += back

    @pl.when(step == BLOCKS - 1)
    def _():
        made_ref[...] = back_ref[...].astype(BF).reshape(made_ref.shape)


def combine(slots_ref, gates_ref, middle_ref, returned_ref, out_ref):
    returned = returned_ref[...].reshape(-1, D)
    out = middle_ref[...]
    for k in range(TOP):
        out = out + gates_ref[:, k : k + 1] * mm(slot_columns(slots_ref, k).astype(BF), returned)
    out_ref[...] = out.astype(BF)


def attention_back(
    core, grad, picked, back_rows, x_ref, mine_ref, theirs_ref, slots_ref, gates_ref, projected_ref,
    probs_ref, middle_ref, branch_ref, branch_grad_ref, projected_grad_ref, rel_ref=None,
):
    gates = [gates_ref[:, k : k + 1] for k in range(TOP)]
    gate_grad = [jnp.sum(rows * grad, axis=-1, keepdims=True) for rows in picked]
    shared = gates[0] * gate_grad[0] + gates[1] * gate_grad[1]
    lane = iota((ROWS, LANES), 1)
    logit_grad = sum(
        jnp.where(lane == slots_ref[:, k : k + 1] // SLOTS, gates[k] * (gate_grad[k] - shared), 0.0)
        for k in range(TOP)
    )
    extras = mine_ref[:, QH + OH :]
    logit_high, logit_low = halves(logit_grad)
    tables = (slot_columns(slots_ref, 0) | slot_columns(slots_ref, 1)).astype(BF)
    moe_grad = mm(tables, back_rows) + mm_nt(logit_high, extras) + mm_nt(logit_low, extras)
    gains = gain_rows(mine_ref)
    middle_grad, gain_two = norm_back(middle_ref[...], gains[1:2], moe_grad)
    middle_grad = middle_grad + grad
    branch_ref[...] = middle_grad.astype(BF)
    own, other = places(core, OH)
    branch_grad_ref[...] = (
        mm_nt(branch_ref[:, own], mine_ref[:, QH : QH + OH])
        + mm_nt(branch_ref[:, other], theirs_ref[:, QH : QH + OH])
    ).astype(BF)
    low_lanes = iota((1, LANES), 1) < HD
    backwards = (iota((ROWS, ROWS), 0) + iota((ROWS, ROWS), 1) == ROWS - 1).astype(BF)
    for pair in range(H // 2):
        at = pair * LANES
        query = projected_ref[:, at : at + LANES]
        key = projected_ref[:, D + at : D + at + LANES]
        value = projected_ref[:, 2 * D + at : 2 * D + at + LANES]
        coming = branch_grad_ref[:, at : at + LANES]
        zero = jnp.zeros_like(query)
        query_grad = key_grad = value_grad = jnp.zeros((ROWS, LANES), F32)
        for side in range(2):
            head = 2 * pair + side
            chosen = low_lanes if side == 0 else jnp.logical_not(low_lanes)
            probs = probs_ref[head]
            own_coming = jnp.where(chosen, coming, zero)
            value_grad = value_grad + mm_tn(probs.astype(BF), own_coming)
            prob_grad = mm_nt(own_coming, value)
            score_grad = probs * (prob_grad - jnp.sum(probs * prob_grad, axis=-1, keepdims=True))
            score_grad = score_grad.astype(BF)
            query_grad = query_grad + mm(score_grad, jnp.where(chosen, key, zero))
            key_grad = key_grad + mm_tn(score_grad, jnp.where(chosen, query, zero))
            if rel_ref is not None:
                turned = pltpu.roll(mm(backwards, score_grad), 1, 1, stride=1, stride_axis=0)
                row = REL_AT + head % REL_OWN
                rel_ref[head // REL_OWN, row : row + 1, :] = jnp.sum(turned, axis=0, keepdims=True)
        projected_grad_ref[:, at : at + LANES] = (query_grad * SCALE).astype(BF)
        projected_grad_ref[:, D + at : D + at + LANES] = (key_grad * SCALE).astype(BF)
        projected_grad_ref[:, 2 * D + at : 2 * D + at + LANES] = value_grad.astype(BF)
    own, other = places(core, QH)
    normed_grad = mm_nt(projected_grad_ref[:, own], mine_ref[:, :QH]) + mm_nt(
        projected_grad_ref[:, other], theirs_ref[:, :QH]
    )
    x_grad, gain_one = norm_back(x_ref[...].astype(F32), gains[0:1], normed_grad)
    return x_grad + middle_grad, gain_one, gain_two, (logit_high, logit_low)


def finish_middle(
    core_ref, x_ref, grad_ref, mine_ref, theirs_ref, slots_ref, gates_ref, projected_ref, probs_ref,
    middle_ref, returned_ref, out_ref, input_ref, picked_ref, branch_ref, branch_grad_ref, projected_grad_ref,
):
    returned = returned_ref[:, :SLOTS, :].reshape(-1, D)
    back_rows = returned_ref[:, SLOTS:, :].reshape(-1, D)
    out = middle_ref[...]
    picked = []
    for k in range(TOP):
        rows = mm(slot_columns(slots_ref, k).astype(BF), returned)
        out = out + gates_ref[:, k : k + 1] * rows
        picked_ref[k] = rows
        picked.append(rows)
    out_ref[...] = out.astype(BF)
    input_grad, _, _, _ = attention_back(
        core_ref[0], grad_ref[...].astype(F32), picked, back_rows, x_ref, mine_ref, theirs_ref, slots_ref,
        gates_ref, projected_ref, probs_ref, middle_ref, branch_ref, branch_grad_ref, projected_grad_ref,
    )
    input_ref[...] = input_grad.astype(BF)


def finish_last(
    core_ref, x_ref, grad_ref, mine_ref, theirs_ref, target_ref, slots_ref, gates_ref, projected_ref, probs_ref,
    middle_ref, moe_ref, picked_ref, returned_ref, input_ref, projected_grad_ref, branch_ref, extras_ref,
    branch_grad_ref, rel_ref,
):
    rel_ref[...] = jnp.zeros_like(rel_ref)
    back_rows = returned_ref[...].reshape(-1, D)
    input_grad, gain_one, gain_two, logits = attention_back(
        core_ref[0], grad_ref[...].astype(F32), [picked_ref[0], picked_ref[1]], back_rows, x_ref, mine_ref,
        theirs_ref, slots_ref, gates_ref, projected_ref, probs_ref, middle_ref, branch_ref, branch_grad_ref,
        projected_grad_ref, rel_ref,
    )
    input_ref[...] = input_grad
    moe_in = moe_ref[...]
    lane = iota((ROWS, LANES), 1)
    extras = mm_tn(moe_in, logits[0]) + mm_tn(moe_in, logits[1])
    for at, terms in ((GAIN_AT, gain_one), (GAIN_AT + 1, gain_two)):
        column = (lane == at).astype(BF)
        for piece in halves(terms):
            extras = extras + mm_tn(piece, column)
    for part in range(2):
        table = bucket_rows(target_ref, part)
        for piece in halves(rel_ref[part]):
            extras = extras + mm_nt(table, piece)
    extras_ref[...] = extras


def weight_totals(
    core_ref, normed_ref, normed_other_ref, attended_ref, attended_other_ref, projected_ref, branch_ref,
    other_ref, extras_ref, extras_other_ref, total_ref,
):
    own, _ = places(core_ref[0], QH)
    total_ref[:, :QH] = (
        mm_tn(normed_ref[...], projected_ref[:, own]) + mm_tn(normed_other_ref[...], other_ref[:, :QH])
    ).astype(BF)
    own, _ = places(core_ref[0], OH)
    total_ref[:, QH : QH + OH] = (
        mm_tn(attended_ref[...], branch_ref[:, own]) + mm_tn(attended_other_ref[...], other_ref[:, QH:])
    ).astype(BF)
    total_ref[:, QH + OH :] = (extras_ref[...] + extras_other_ref[...].astype(F32)).astype(BF)


def shaped(*pairs):
    return [jax.ShapeDtypeStruct(shape, dtype) for shape, dtype in pairs]


def run(body, inputs, outputs, scratch=(), scalars=1, flops=0):
    size = sum(value.size * value.dtype.itemsize for value in inputs)
    size += sum(value.size * value.dtype.itemsize for value in outputs)
    return pl.pallas_call(
        body,
        out_shape=outputs,
        in_specs=[SMEM] * scalars + [VMEM] * (len(inputs) - scalars),
        out_specs=[VMEM] * len(outputs),
        scratch_shapes=list(scratch),
        compiler_params=pltpu.CompilerParams(vmem_limit_bytes=LIMIT),
        cost_estimate=pl.CostEstimate(flops=flops, bytes_accessed=size, transcendentals=0),
    )(*inputs)


def run_expert(body, rows, first, second, slope, outputs, blocked, scratch, flops):
    whole = lambda value: pl.BlockSpec(value.shape, lambda step: (0,) * len(value.shape))
    wide = lambda value: pl.BlockSpec((value.shape[0], BLOCK), lambda step: (0, step))
    tall = pl.BlockSpec((BLOCK, D), lambda step: (step, 0))
    inputs, specs = [rows, first, second], [whole(rows), wide(first), tall]
    if slope is not None:
        inputs.append(slope)
        specs.append(wide(slope))
    size = sum(value.size * value.dtype.itemsize for value in inputs)
    size += sum(value.size * value.dtype.itemsize for value in outputs)
    return pl.pallas_call(
        body,
        grid=(BLOCKS,),
        out_shape=outputs,
        in_specs=specs,
        out_specs=[wide(value) if split else whole(value) for value, split in zip(outputs, blocked)],
        scratch_shapes=scratch,
        compiler_params=pltpu.CompilerParams(vmem_limit_bytes=LIMIT),
        cost_estimate=pl.CostEstimate(flops=flops, bytes_accessed=size, transcendentals=0),
    )(*inputs)


def pack_columns(core, qkv, out, router, gain_one, gain_two, rel):
    rel_rows = jnp.pad(rel[None, :], ((0, OWN - 1), (0, 0)))
    extras = jnp.concatenate([router, gain_one[:, None], gain_two[:, None], rel_rows], axis=1)
    extras = jnp.pad(extras, ((0, 0), (0, LANES - extras.shape[1])))
    cut = lambda side: jnp.concatenate(
        [qkv[:, side * QH : (side + 1) * QH], out[:, side * OH : (side + 1) * OH], extras], axis=1
    )
    sides = cut(0), cut(1)
    return jnp.where(core == 0, sides[0], sides[1]), jnp.where(core == 0, sides[1], sides[0])


def gather_dense(core, chips, shards):
    kept, given = pack_columns(core, *shards)
    other = core_swap(given)
    pair = jnp.concatenate(
        [jnp.where(core == 0, kept, other), jnp.where(core == 0, other, kept)], axis=0
    )
    spread = jnp.broadcast_to(pair[None], (chips,) + pair.shape)
    mine = chip_exchange(spread).reshape(chips * 2 * OWN, WIDE)
    return mine, core_swap(mine)


def scatter_dense(core, chips, total):
    arrived = chip_exchange(total.reshape(chips, 2 * OWN, WIDE))
    summed = jnp.sum(arrived.astype(F32), axis=0)
    kept = jnp.where(core == 0, summed[:OWN], summed[OWN:])
    given = jnp.where(core == 0, summed[OWN:], summed[:OWN])
    other = core_swap(given[:, : QH + OH])
    low = jnp.where(core == 0, kept[:, : QH + OH], other)
    high = jnp.where(core == 0, other, kept[:, : QH + OH])
    qkv = jnp.concatenate([low[:, :QH], high[:, :QH]], axis=1)
    out = jnp.concatenate([low[:, QH:], high[:, QH:]], axis=1)
    return qkv, out, kept[:, QH + OH :]


def from_experts(mine, theirs):
    total = (mine.astype(F32) + core_swap(theirs).astype(F32)).astype(BF)
    return chip_exchange(total)


def visible_mask(lengths):
    positions = jnp.arange(ROWS, dtype=jnp.int32)
    first = lengths[:, 0, 0]
    segment = jnp.where(
        positions < TOK,
        (positions >= first[0]).astype(jnp.int32),
        2 + (positions >= TOK + first[1]).astype(jnp.int32),
    )
    seen = (segment[:, None] == segment[None, :]) & (positions[:, None] >= positions[None, :])
    return jnp.where(seen, 0.0, -1e30).astype(F32)


def slot_table(routes):
    flat = routes.reshape(MB, TOK * TOP)
    order = jnp.arange(TOK * TOP, dtype=jnp.int32)
    same = (flat[:, :, None] == flat[:, None, :]) & (order[None, :, None] > order[None, None, :])
    rank = jnp.sum(same.astype(jnp.int32), axis=-1, dtype=jnp.int32)
    micro = jnp.arange(MB, dtype=jnp.int32)[:, None]
    return (flat * SLOTS + micro * CAP + rank).reshape(ROWS, TOP)


def per_device(
    tokens,
    cotangent,
    lengths,
    routes,
    buckets,
    qkv_weight,
    out_weight,
    router_weight,
    norm1_gain,
    norm2_gain,
    rel_bias,
    expert_in,
    expert_out,
):
    chips = lax.axis_size("chip")
    core = lax.axis_index("core")
    section = lax.axis_index("section")
    last = lax.axis_size("section") - 1
    first, second = expert_in[0, 0], expert_out[0, 0]
    mine, theirs = gather_dense(
        core,
        chips,
        (qkv_weight[0], out_weight[0], router_weight[0], norm1_gain[0], norm2_gain[0], rel_bias[0]),
    )
    where = core.astype(jnp.int32).reshape(1)
    mask = visible_mask(lengths)
    slots = slot_table(routes[0])
    slots_t = slots.T
    turned = jnp.concatenate([buckets[:1], jnp.zeros((TOK,), jnp.int32), buckets[:0:-1]])
    target = (turned * (2 * OWN)).reshape(1, LANES)

    row = (ROWS, D)
    flat = (chips * SLOTS, D)
    dense_flops = 2 * ROWS * D * (4 * D + LANES) + 4 * H * ROWS * ROWS * LANES + 2 * ROWS * D * EXPERTS * SLOTS
    expert_flops = 4 * chips * SLOTS * D * FFH

    begin = tokens.reshape(row)
    shared = (mine, theirs, mask, target, slots, slots_t)
    middle, gates, buffer = run(
        functools.partial(front, False),
        (where, begin) + shared,
        shaped((row, F32), ((ROWS, LANES), F32), ((EXPERTS, SLOTS, D), BF)),
        [pltpu.VMEM((ROWS, 3 * D), BF), pltpu.VMEM(row, BF)],
        flops=dense_flops,
    )
    arrived = chip_exchange(buffer)
    arrived = (arrived, core_swap(arrived))
    made = [
        run_expert(
            expert_forward, rows, first, second, None, shaped((rows.shape, BF)), (False,),
            [pltpu.VMEM(flat, F32)], expert_flops,
        )[0]
        for rows in arrived
    ]
    returned = from_experts(*made)
    (result,) = run(
        combine, (slots, gates, middle, returned), shaped((row, BF)), scalars=0, flops=4 * ROWS * D * EXPERTS * SLOTS
    )
    passed = lax.ppermute(result, "section", [(0, 1)])
    layer_in = jnp.where(section == 0, begin, passed)

    ending = cotangent.reshape(row)
    normed, projected, probs, attended, middle, moe_in, gates, buffer = run(
        functools.partial(front, True),
        (where, layer_in) + shared + (ending,),
        shaped(
            (row, BF),
            ((ROWS, 3 * D), BF),
            ((H, ROWS, ROWS), F32),
            (row, BF),
            (row, F32),
            (row, BF),
            ((ROWS, LANES), F32),
            ((EXPERTS, 2 * SLOTS, D), BF),
        ),
        flops=dense_flops,
    )
    normed_other, attended_other = core_swap(normed), core_swap(attended)
    arrived = chip_exchange(buffer)
    arrived = (arrived, core_swap(arrived))
    wide = (chips * SLOTS, FFH)
    made, hidden, slope = zip(
        *[
            run_expert(
                expert_both, rows, first, second, None, shaped((rows.shape, BF), (wide, BF), (wide, BF)),
                (False, True, True), [pltpu.VMEM(flat, F32)] * 2, 2 * expert_flops,
            )
            for rows in arrived
        ]
    )
    returned = from_experts(*made)
    result, input_grad, picked = run(
        finish_middle,
        (where, layer_in, ending, mine, theirs, slots, gates, projected, probs, middle, returned),
        shaped((row, BF), (row, BF), ((TOP,) + row, F32)),
        [pltpu.VMEM(row, BF), pltpu.VMEM(row, BF), pltpu.VMEM((ROWS, 3 * D), BF)],
        flops=2 * dense_flops,
    )
    passed = lax.ppermute(input_grad, "section", [(1, 0)])
    grad_out = jnp.where(section == last, ending, passed)

    (buffer,) = run(
        send_grad,
        (gates, grad_out, slots_t),
        shaped(((EXPERTS, SLOTS, D), BF)),
        scalars=0,
        flops=4 * ROWS * D * EXPERTS * SLOTS,
    )
    grads = chip_exchange(buffer)
    grads = (grads, core_swap(grads))
    made, pre_grad = zip(
        *[
            run_expert(
                expert_back, rows, first, second, slopes, shaped((rows.shape, BF), (wide, BF)),
                (False, True), [pltpu.VMEM(flat, F32)], expert_flops,
            )
            for rows, slopes in zip(grads, slope)
        ]
    )
    returned = from_experts(*made)
    second_total = sum(mm_tn(value, rows.reshape(flat)) for value, rows in zip(hidden, grads))
    first_total = sum(mm_tn(rows[:, :SLOTS].reshape(flat), value) for rows, value in zip(arrived, pre_grad))
    input_grad, projected_grad, branch, extras = run(
        finish_last,
        (where, layer_in, grad_out, mine, theirs, target, slots, gates, projected, probs, middle, moe_in, picked, returned),
        shaped((row, F32), ((ROWS, 3 * D), BF), (row, BF), ((D, LANES), F32)),
        [pltpu.VMEM(row, BF), pltpu.VMEM((2, LANES, LANES), F32)],
        flops=2 * dense_flops,
    )
    given = jnp.concatenate(
        [
            lax.dynamic_slice(projected_grad, (0, (1 - core) * QH), (ROWS, QH)),
            lax.dynamic_slice(branch, (0, (1 - core) * OH), (ROWS, OH)),
        ],
        axis=1,
    )
    (total,) = run(
        weight_totals,
        (
            where, normed, normed_other, attended, attended_other, projected_grad, branch,
            core_swap(given), extras, core_swap(extras.astype(BF)),
        ),
        shaped(((D, WIDE), BF)),
        flops=4 * ROWS * D * WIDE,
    )
    qkv_grad, out_grad, small = scatter_dense(core, chips, total)
    return (
        result.reshape(1, MB, TOK, D),
        input_grad.reshape(1, MB, TOK, D),
        qkv_grad[None],
        out_grad[None],
        small[None, :, :EXPERTS],
        small[None, :, GAIN_AT],
        small[None, :, GAIN_AT + 1],
        small[None, 0, REL_AT : REL_AT + REL_OWN],
        first_total[None, None],
        second_total[None, None],
    )


def solution(mesh):
    sections, members = mesh.devices.shape
    fine = Mesh(mesh.devices.reshape(sections, members // 2, 2), ("section", "chip", "core"))
    dp = ("chip", "core")
    return jax.shard_map(
        per_device,
        mesh=fine,
        in_specs=(
            P(None, dp, None),
            P(None, dp, None),
            P(None, dp, None),
            P("section", None, dp, None),
            P(),
            P("section", dp, None),
            P("section", dp, None),
            P("section", dp, None),
            P("section", dp),
            P("section", dp),
            P("section", dp),
            P("section", dp, None, None),
            P("section", dp, None, None),
        ),
        out_specs=(
            P("section", None, dp, None),
            P("section", None, dp, None),
            P("section", dp, None),
            P("section", dp, None),
            P("section", dp, None),
            P("section", dp),
            P("section", dp),
            P("section", dp),
            P("section", dp, None, None),
            P("section", dp, None, None),
        ),
        check_vma=False,
    )
```

```python
import functools

import jax
import jax.numpy as jnp
from jax import lax
from jax.experimental import pallas as pl
from jax.experimental.pallas import tpu as pltpu
from jax.sharding import Mesh, PartitionSpec as P

D = 768
H = 12
HD = 64
TOK = 64
MB = 2
NB = 32
TOP = 2
CAP = 8
ROWS = MB * TOK
LANES = 128
EXPERTS = 32
SLOTS = MB * CAP
FFH = 1536
QH = 3 * D // 2
OH = D // 2
WIDE = QH + OH + LANES
GAIN_AT = EXPERTS
REL_AT = EXPERTS + 2
REL_OWN = 6
OWN = 12
BLOCKS = 6
BLOCK = FFH // BLOCKS

EPSILON = 1e-06
SCALE = HD ** (-0.5)
BF = jnp.bfloat16
F32 = jnp.float32
VMEM = pl.BlockSpec(memory_space=pltpu.VMEM)
SMEM = pl.BlockSpec(memory_space=pltpu.SMEM)
HBM = pl.BlockSpec(memory_space=pltpu.HBM)
STATE = 6 * D
LIMIT = 24 * 1024 * 1024


def mm(a, b):
    return jnp.dot(a, b, preferred_element_type=F32)


def mm_nt(a, b):
    return lax.dot_general(a, b, (((1,), (1,)), ((), ())), preferred_element_type=F32)


def mm_tn(a, b):
    return lax.dot_general(a, b, (((0,), (0,)), ((), ())), preferred_element_type=F32)


def begin_copy(source, target, semaphore):
    copy = pltpu.make_async_copy(source, target, semaphore)
    copy.start()
    return copy


def halves(value):
    high = value.astype(BF)
    return high, (value - high.astype(F32)).astype(BF)


def core_swap(value):
    return lax.ppermute(value, "core", [(0, 1), (1, 0)])


def chip_exchange(value):
    return lax.all_to_all(value, "chip", split_axis=0, concat_axis=0, tiled=True)


def iota(shape, axis):
    return lax.broadcasted_iota(jnp.int32, shape, axis)


def places(core, width):
    mine = pl.multiple_of(core * width, LANES)
    theirs = pl.multiple_of((1 - core) * width, LANES)
    return pl.ds(mine, width), pl.ds(theirs, width)


def gain_rows(mine_ref):
    chosen = (iota((16, LANES), 1) == iota((16, LANES), 0) + GAIN_AT).astype(BF)
    return mm_nt(chosen, mine_ref[:, QH + OH :])


def norm_factor(values):
    return lax.rsqrt(jnp.mean(values * values, axis=-1, keepdims=True) + EPSILON)


def norm_back(values, gain, grad_in):
    factor = norm_factor(values)
    normed = values * factor
    weighted = grad_in * gain
    value_grad = factor * (weighted - normed * jnp.mean(weighted * normed, axis=-1, keepdims=True))
    return value_grad, grad_in * normed


def gelu_parts(pre):
    outer = 0.7978845608028654
    inner = outer * 0.044715
    square = pre * pre
    share = 0.5 + 0.5 * jnp.tanh(pre * (outer + inner * square))
    hidden = pre * share
    return share, hidden, square


def gelu_slope(share, hidden, square):
    outer = 0.7978845608028654
    inner = outer * 0.044715
    return share + hidden * (1.0 - share) * (2.0 * outer + 6.0 * inner * square)


def two_heads(values):
    low = iota((1, LANES), 1) < HD
    zero = jnp.zeros_like(values)
    return jnp.concatenate([jnp.where(low, values, zero), jnp.where(low, zero, values)], axis=0)


def slot_rows(slots_t_ref, k):
    return iota((EXPERTS * SLOTS, ROWS), 0) == slots_t_ref[k : k + 1, :]


def slot_columns(slots_ref, k):
    return iota((ROWS, EXPERTS * SLOTS), 1) == slots_ref[:, k : k + 1]


def bucket_rows(target_ref, part):
    return (iota((D, LANES), 0) == target_ref[...] + OWN * part).astype(BF)


def as_column(row_ref):
    size = row_ref.shape[1]
    eye = iota((size, size), 0) == iota((size, size), 1)
    return jnp.sum(jnp.where(eye, row_ref[...].astype(F32), 0.0), axis=1, keepdims=True)


def prepare(
    core_ref, lengths_ref, qkv_ref, out_ref, router_ref, one_ref, two_ref, rel_ref, routes_in, buckets_ref,
    kept_ref, given_ref, mask_ref, slots_ref, slots_t_ref, target_ref,
):
    core = core_ref[0]
    lane = iota((OWN, LANES), 1)
    extras = mm(router_ref[...], (iota((EXPERTS, LANES), 0) == iota((EXPERTS, LANES), 1)).astype(BF))
    extras = extras + jnp.where(lane == GAIN_AT, as_column(one_ref), 0.0)
    extras = extras + jnp.where(lane == GAIN_AT + 1, as_column(two_ref), 0.0)
    moved = iota((REL_OWN, LANES), 0) + REL_AT == iota((REL_OWN, LANES), 1)
    rel = jnp.sum(jnp.where(moved, as_column(rel_ref), 0.0), axis=0, keepdims=True)
    extras = extras + jnp.where(iota((OWN, LANES), 0) == 0, rel, 0.0)
    for target, at in zip((kept_ref, given_ref), (0, 1)):
        target[:, :QH] = qkv_ref[:, places(core, QH)[at]]
        target[:, QH : QH + OH] = out_ref[:, places(core, OH)[at]]
        target[:, QH + OH :] = extras.astype(BF)

    def segment(axis):
        place = iota((ROWS, ROWS), axis)
        early = (place >= lengths_ref[0, :, 0:1]).astype(jnp.int32)
        late = 2 + (place >= TOK + lengths_ref[1, :, 0:1]).astype(jnp.int32)
        return jnp.where(place < TOK, early, late)

    row, column = iota((ROWS, ROWS), 0), iota((ROWS, ROWS), 1)
    seen = (segment(0) == segment(1)) & (row <= column)
    mask_ref[...] = jnp.where(seen, 0.0, -1e30)
    together = (row < TOK) == (column < TOK)
    rows = [jnp.concatenate([routes_in[m, k : k + 1, :] for m in range(MB)], axis=1) for k in range(TOP)]
    columns = [jnp.sum(jnp.where(row == column, value, 0), axis=1, keepdims=True) for value in rows]
    for k in range(TOP):
        own, own_t = columns[k], rows[k]
        rank = jnp.zeros((ROWS, ROWS), jnp.int32)
        rank_t = jnp.zeros((ROWS, ROWS), jnp.int32)
        for other in range(TOP):
            same = together & (own == rows[other]) & (column < row)
            rank = rank + same.astype(jnp.int32)
            same_t = together & (columns[other] == own_t) & (row < column)
            rank_t = rank_t + same_t.astype(jnp.int32)
        micro = (iota((ROWS, 1), 0) >= TOK).astype(jnp.int32)
        micro_t = (iota((1, ROWS), 1) >= TOK).astype(jnp.int32)
        slots_ref[:, k : k + 1] = own * SLOTS + micro * CAP + jnp.sum(rank, axis=1, keepdims=True)
        slots_t_ref[k : k + 1, :] = own_t * SLOTS + micro_t * CAP + jnp.sum(rank_t, axis=0, keepdims=True)
    target_ref[...] = jnp.concatenate([buckets_ref[...] * (2 * OWN), jnp.zeros((1, LANES - TOK), jnp.int32)], axis=1)


def front(saving, core_ref, x_ref, mine_ref, theirs_ref, mask_ref, target_ref, slots_ref, slots_t_ref, *refs):
    if saving:
        grad_ref, factor_ref, state_ref, kept_ref, gates_ref, buffer_ref = refs[:6]
        projected_ref, attended_ref, scores_ref, probs_ref, middle_ref, moe_ref, theirs_space, mask_space, semaphores = refs[6:]
    else:
        middle_ref, gates_ref, buffer_ref, projected_ref, attended_ref, scores_ref = refs
        probs_ref = scores_ref
    core = core_ref[0]
    if saving:
        coming_theirs = begin_copy(theirs_ref, theirs_space, semaphores.at[0])
        coming_mask = begin_copy(mask_ref, mask_space, semaphores.at[4 + H])
        theirs_ref, mask_ref = theirs_space, mask_space
    x = x_ref[...].astype(F32)
    gains = gain_rows(mine_ref)
    normed = (x * norm_factor(x) * gains[0:1]).astype(BF)
    if saving:
        factor_ref[:, :D] = normed
    own, other = places(core, QH)
    projected_ref[:, own] = mm(normed, mine_ref[:, :QH]).astype(BF)
    if saving:
        coming_theirs.wait()
    projected_ref[:, other] = mm(normed, theirs_ref[:, :QH]).astype(BF)
    copies = []
    if saving:
        copies.append(begin_copy(projected_ref, state_ref.at[:, : 3 * D], semaphores.at[3 + H]))
    extras = mine_ref[:, QH + OH :]
    rel = [mm_tn(extras, bucket_rows(target_ref, part)) for part in range(2)]
    if saving:
        coming_mask.wait()
    mask = mask_ref[...]
    for pair in range(H // 2):
        at = pair * LANES
        query = projected_ref[:, at : at + LANES]
        scores = mm_nt(two_heads(projected_ref[:, D + at : D + at + LANES]), query) * SCALE
        for side in range(2):
            head = 2 * pair + side
            row = REL_AT + head % REL_OWN
            spread = jnp.broadcast_to(rel[head // REL_OWN][row : row + 1, :], (ROWS, LANES))
            bias = pltpu.roll(spread, 0, 1, stride=1, stride_axis=0)
            scores_ref[head] = scores[side * ROWS : (side + 1) * ROWS] + bias + mask
    for head in range(H):
        scores = scores_ref[head]
        raised = jnp.exp(scores - jnp.max(scores, axis=0, keepdims=True))
        probs = raised * (1.0 / jnp.sum(raised, axis=0, keepdims=True))
        probs_ref[head] = probs.astype(probs_ref.dtype)
    if saving:
        for head in range(H):
            place = state_ref.at[:, 3 * D + head * ROWS : 3 * D + (head + 1) * ROWS]
            copies.append(begin_copy(probs_ref.at[head], place, semaphores.at[3 + head]))
    for pair in range(H // 2):
        at = pair * LANES
        value = two_heads(projected_ref[:, 2 * D + at : 2 * D + at + LANES])
        probs = probs_ref[2 * pair : 2 * pair + 2].reshape(2 * ROWS, ROWS).astype(BF)
        attended_ref[:, at : at + LANES] = mm_tn(probs, value).astype(BF)
    attended = attended_ref[...]
    if saving:
        factor_ref[:, D:] = attended
    own, other = places(core, OH)
    middle_ref[:, own] = mm(attended, mine_ref[:, QH : QH + OH])
    middle_ref[:, other] = mm(attended, theirs_ref[:, QH : QH + OH])
    middle = x + middle_ref[...]
    middle_ref[...] = middle
    if saving:
        copies.append(begin_copy(middle_ref, kept_ref, semaphores.at[1]))
    moe_in = (middle * norm_factor(middle) * gains[1:2]).astype(BF)
    logits = mm(moe_in, extras)
    lane = iota((ROWS, LANES), 1)
    picked = [
        jnp.sum(jnp.where(lane == slots_ref[:, k : k + 1] // SLOTS, logits, 0.0), axis=-1, keepdims=True)
        for k in range(TOP)
    ]
    peak = jnp.maximum(picked[0], picked[1])
    raised = [jnp.exp(value - peak) for value in picked]
    gates = [value / (raised[0] + raised[1]) for value in raised]
    gates_ref[...] = jnp.where(lane == 0, gates[0], jnp.where(lane == 1, gates[1], 0.0))
    tables = [slot_rows(slots_t_ref, k) for k in range(TOP)]
    buffer = mm((tables[0] | tables[1]).astype(BF), moe_in).astype(BF)
    buffer_ref[:, :SLOTS, :] = buffer.reshape(EXPERTS, SLOTS, D)
    if saving:
        moe_ref[...] = moe_in
        copies.append(begin_copy(moe_ref, state_ref.at[:, 5 * D : 6 * D], semaphores.at[2]))
        grad = grad_ref[...].astype(F32)
        buffer_ref[:, SLOTS:, :] = spread_grad(tables, gates, grad).reshape(EXPERTS, SLOTS, D)
    for copy in copies:
        copy.wait()


def spread_grad(tables, gates, grad):
    return sum(
        mm(table.astype(BF), (gate * grad).astype(BF)) for table, gate in zip(tables, gates)
    ).astype(BF)


def send_grad(gates_ref, grad_ref, slots_t_ref, buffer_ref):
    grad = grad_ref[...].astype(F32)
    gates = [gates_ref[:, k : k + 1] for k in range(TOP)]
    tables = [slot_rows(slots_t_ref, k) for k in range(TOP)]
    buffer_ref[...] = spread_grad(tables, gates, grad).reshape(EXPERTS, SLOTS, D)


def expert_forward(rows_ref, first_ref, second_ref, made_ref, hidden_ref):
    rows = rows_ref[...].reshape(-1, D)
    for block in range(BLOCKS):
        part = slice(block * BLOCK, (block + 1) * BLOCK)
        _, hidden, _ = gelu_parts(mm(rows, first_ref[:, part]))
        hidden_ref[:, part] = hidden.astype(BF)
    made_ref[...] = mm(hidden_ref[...], second_ref[...]).astype(BF).reshape(made_ref.shape)


def expert_both(
    rows_ref, first_ref, second_ref, made_ref, hidden_out, slope_out, hidden_ref, slope_ref, pre_ref, semaphores
):
    rows = rows_ref[:, :SLOTS, :].reshape(-1, D)
    grads = rows_ref[:, SLOTS:, :].reshape(-1, D)
    copies = []
    for block in range(BLOCKS):
        part = slice(block * BLOCK, (block + 1) * BLOCK)
        share, hidden, square = gelu_parts(mm(rows, first_ref[:, part]))
        hidden_ref[:, part] = hidden.astype(BF)
        slope = gelu_slope(share, hidden, square)
        slope_ref[:, part] = slope.astype(BF)
        pre_ref[:, part] = (mm_nt(grads, second_ref[part, :]) * slope).astype(BF)
    copies.append(begin_copy(hidden_ref, hidden_out, semaphores.at[0]))
    copies.append(begin_copy(slope_ref, slope_out, semaphores.at[1]))
    made_ref[:, :SLOTS, :] = mm(hidden_ref[...], second_ref[...]).astype(BF).reshape(-1, SLOTS, D)
    made_ref[:, SLOTS:, :] = mm_nt(pre_ref[...], first_ref[...]).astype(BF).reshape(-1, SLOTS, D)
    for copy in copies:
        copy.wait()


def expert_back(
    own_ref, other_ref, first_ref, second_in, own_slope_in, other_slope_in,
    own_made_ref, other_made_ref, own_pre_out, other_pre_out, second_ref, slope_ref, pre_ref, semaphores,
):
    parts = [slice(block * BLOCK, (block + 1) * BLOCK) for block in range(BLOCKS)]
    chunk = own_ref.shape[0] // 2
    pieces = [(side, half) for side in range(2) for half in range(2)]
    numbers = iter(range(BLOCKS + 2 * len(pieces)))
    sources = ((own_ref, own_made_ref, own_slope_in, own_pre_out), (other_ref, other_made_ref, other_slope_in, other_pre_out))
    slopes = []
    for at, (side, half) in enumerate(pieces):
        rows = slice(half * chunk * SLOTS, (half + 1) * chunk * SLOTS)
        slopes.append(begin_copy(sources[side][2].at[rows, :], slope_ref.at[side, rows, :], semaphores.at[next(numbers)]))
        if at == 0:
            weights = [
                begin_copy(second_in.at[part, :], second_ref.at[part, :], semaphores.at[next(numbers)]) for part in parts
            ]
    leaving = []
    for at, (side, half) in enumerate(pieces):
        grads_ref, made_ref, _, pre_out = sources[side]
        rows = slice(half * chunk * SLOTS, (half + 1) * chunk * SLOTS)
        sent = slice(half * chunk, (half + 1) * chunk)
        grads = grads_ref[sent].reshape(-1, D)
        for block, part in enumerate(parts):
            if at == 0:
                weights[block].wait()
            hidden_grad = mm_nt(grads, second_ref[part, :])
            if block == 0:
                slopes[at].wait()
            pre_ref[side, rows, part] = (hidden_grad * slope_ref[side, rows, part].astype(F32)).astype(BF)
        leaving.append(begin_copy(pre_ref.at[side, rows, :], pre_out.at[rows, :], semaphores.at[next(numbers)]))
        made_ref[sent] = mm_nt(pre_ref[side, rows, :], first_ref[...]).astype(BF).reshape(chunk, SLOTS, D)
    for copy in leaving:
        copy.wait()


def combine(slots_ref, gates_ref, middle_ref, returned_ref, out_ref):
    returned = returned_ref[...].reshape(-1, D)
    out = middle_ref[...]
    for k in range(TOP):
        out = out + gates_ref[:, k : k + 1] * mm(slot_columns(slots_ref, k).astype(BF), returned)
    out_ref[...] = out.astype(BF)


def attention_back(
    core, grad, picked, back_rows, x_ref, mine_ref, theirs_ref, slots_ref, gates_ref, projected_ref,
    probs_ref, middle_ref, coming_state, coming_middle, coming_theirs, branch_ref, branch_grad_ref, projected_grad_ref, score_grad_ref, rel_ref=None,
):
    gates = [gates_ref[:, k : k + 1] for k in range(TOP)]
    gate_grad = [jnp.sum(rows * grad, axis=-1, keepdims=True) for rows in picked]
    shared = gates[0] * gate_grad[0] + gates[1] * gate_grad[1]
    lane = iota((ROWS, LANES), 1)
    logit_grad = sum(
        jnp.where(lane == slots_ref[:, k : k + 1] // SLOTS, gates[k] * (gate_grad[k] - shared), 0.0)
        for k in range(TOP)
    )
    extras = mine_ref[:, QH + OH :]
    logit_high, logit_low = halves(logit_grad)
    tables = (slot_columns(slots_ref, 0) | slot_columns(slots_ref, 1)).astype(BF)
    moe_grad = mm(tables, back_rows) + mm_nt(logit_high, extras) + mm_nt(logit_low, extras)
    gains = gain_rows(mine_ref)
    coming_middle.wait()
    middle_grad, gain_two = norm_back(middle_ref[...], gains[1:2], moe_grad)
    middle_grad = middle_grad + grad
    branch_ref[...] = middle_grad.astype(BF)
    own, other = places(core, OH)
    coming_theirs.wait()
    branch_grad_ref[...] = (
        mm_nt(branch_ref[:, own], mine_ref[:, QH : QH + OH])
        + mm_nt(branch_ref[:, other], theirs_ref[:, QH : QH + OH])
    ).astype(BF)
    coming_state.wait()
    for pair in range(H // 2):
        at = pair * LANES
        value = two_heads(projected_ref[:, 2 * D + at : 2 * D + at + LANES])
        coming = branch_grad_ref[:, at : at + LANES]
        prob_grad = mm_nt(value, coming)
        for side in range(2):
            head = 2 * pair + side
            probs = probs_ref[:, head * ROWS : (head + 1) * ROWS].astype(F32)
            own_grad = prob_grad[side * ROWS : (side + 1) * ROWS]
            score_grad = probs * (own_grad - jnp.sum(probs * own_grad, axis=0, keepdims=True))
            score_grad_ref[head] = score_grad.astype(BF)
    for pair in range(H // 2):
        at = pair * LANES
        query = two_heads(projected_ref[:, at : at + LANES])
        key = two_heads(projected_ref[:, D + at : D + at + LANES])
        coming = two_heads(branch_grad_ref[:, at : at + LANES])
        probs = probs_ref[:, 2 * pair * ROWS : 2 * (pair + 1) * ROWS]
        tall = score_grad_ref[2 * pair : 2 * pair + 2].reshape(2 * ROWS, ROWS)
        wide = jnp.concatenate([tall[:ROWS], tall[ROWS:]], axis=1)
        projected_grad_ref[:, at : at + LANES] = (mm_tn(tall, key) * SCALE).astype(BF)
        projected_grad_ref[:, D + at : D + at + LANES] = (mm(wide, query) * SCALE).astype(BF)
        projected_grad_ref[:, 2 * D + at : 2 * D + at + LANES] = mm(probs, coming).astype(BF)
    if rel_ref is not None:
        backwards = (iota((ROWS, ROWS), 0) + iota((ROWS, ROWS), 1) == ROWS - 1).astype(BF)
        for head in range(H):
            turned = pltpu.roll(mm(backwards, score_grad_ref[head]), 1, 1, stride=1, stride_axis=0)
            row = REL_AT + head % REL_OWN
            rel_ref[head // REL_OWN, row : row + 1, :] = jnp.sum(turned, axis=0, keepdims=True)
    own, other = places(core, QH)
    normed_grad = mm_nt(projected_grad_ref[:, own], mine_ref[:, :QH]) + mm_nt(
        projected_grad_ref[:, other], theirs_ref[:, :QH]
    )
    x_grad, gain_one = norm_back(x_ref[...].astype(F32), gains[0:1], normed_grad)
    return x_grad + middle_grad, gain_one, gain_two, (logit_high, logit_low)


def finish_middle(
    core_ref, x_ref, grad_ref, mine_ref, theirs_in, slots_ref, gates_ref, state_in, middle_in, returned_ref,
    out_ref, input_ref, picked_out, state_ref, middle_ref, picked_ref, branch_ref, branch_grad_ref,
    projected_grad_ref, score_grad_ref, theirs_ref, semaphores,
):
    wanted = 5 * D
    coming_middle = begin_copy(middle_in, middle_ref, semaphores.at[0])
    coming_theirs = begin_copy(theirs_in, theirs_ref, semaphores.at[3])
    coming_state = begin_copy(state_in.at[:, :wanted], state_ref, semaphores.at[1])
    returned = returned_ref[:, :SLOTS, :].reshape(-1, D)
    back_rows = returned_ref[:, SLOTS:, :].reshape(-1, D)
    picked = [mm(slot_columns(slots_ref, k).astype(BF), returned) for k in range(TOP)]
    for k in range(TOP):
        picked_ref[:, k * D : (k + 1) * D] = picked[k].astype(BF)
    leaving = begin_copy(picked_ref, picked_out, semaphores.at[2])
    input_grad, _, _, _ = attention_back(
        core_ref[0], grad_ref[...].astype(F32), picked, back_rows, x_ref, mine_ref, theirs_ref, slots_ref,
        gates_ref, state_ref.at[:, : 3 * D], state_ref.at[:, 3 * D :], middle_ref, coming_state, coming_middle,
        coming_theirs, branch_ref, branch_grad_ref, projected_grad_ref, score_grad_ref,
    )
    input_ref[...] = input_grad.astype(BF)
    out = middle_ref[...]
    for k in range(TOP):
        out = out + gates_ref[:, k : k + 1] * picked[k]
    out_ref[...] = out.astype(BF)
    leaving.wait()


def finish_last(
    core_ref, x_ref, grad_in, mine_ref, theirs_in, target_ref, slots_in, gates_in, state_in, middle_in,
    picked_in, returned_ref, input_ref, projected_grad_ref, branch_ref, extras_ref, state_ref, middle_ref,
    picked_ref, branch_grad_ref, score_grad_ref, rel_ref, theirs_ref,
    grad_ref, slots_ref, gates_ref, semaphores,
):
    small = ((grad_in, grad_ref), (slots_in, slots_ref), (gates_in, gates_ref))
    coming_small = [begin_copy(*pair, semaphores.at[4 + at]) for at, pair in enumerate(small)]
    coming_picked = begin_copy(picked_in, picked_ref, semaphores.at[2])
    coming_middle = begin_copy(middle_in, middle_ref, semaphores.at[0])
    coming_theirs = begin_copy(theirs_in, theirs_ref, semaphores.at[3])
    coming_state = begin_copy(state_in, state_ref, semaphores.at[1])
    rel_ref[...] = jnp.zeros_like(rel_ref)
    back_rows = returned_ref[...].reshape(-1, D)
    for copy in coming_small:
        copy.wait()
    coming_picked.wait()
    picked = [picked_ref[:, k * D : (k + 1) * D].astype(F32) for k in range(TOP)]
    input_grad, gain_one, gain_two, logits = attention_back(
        core_ref[0], grad_ref[...].astype(F32), picked, back_rows, x_ref, mine_ref, theirs_ref, slots_ref,
        gates_ref, state_ref.at[:, : 3 * D], state_ref.at[:, 3 * D : 5 * D], middle_ref, coming_state, coming_middle,
        coming_theirs, branch_ref, branch_grad_ref, projected_grad_ref, score_grad_ref, rel_ref,
    )
    input_ref[...] = input_grad
    moe_in = state_ref[:, 5 * D : 6 * D]
    lane = iota((ROWS, LANES), 1)
    extras = mm_tn(moe_in, logits[0]) + mm_tn(moe_in, logits[1])
    for at, terms in ((GAIN_AT, gain_one), (GAIN_AT + 1, gain_two)):
        column = (lane == at).astype(BF)
        for piece in halves(terms):
            extras = extras + mm_tn(piece, column)
    for part in range(2):
        table = bucket_rows(target_ref, part)
        for piece in halves(rel_ref[part]):
            extras = extras + mm_nt(table, piece)
    extras_ref[...] = extras


def weight_totals(
    core_ref, factor_ref, factor_other_ref, projected_ref, branch_ref,
    other_ref, extras_ref, extras_other_ref, total_ref,
):
    own, _ = places(core_ref[0], QH)
    total_ref[:, :QH] = (
        mm_tn(factor_ref[:, :D], projected_ref[:, own]) + mm_tn(factor_other_ref[:, :D], other_ref[:, :QH])
    ).astype(BF)
    own, _ = places(core_ref[0], OH)
    total_ref[:, QH : QH + OH] = (
        mm_tn(factor_ref[:, D:], branch_ref[:, own]) + mm_tn(factor_other_ref[:, D:], other_ref[:, QH:])
    ).astype(BF)
    total_ref[:, QH + OH :] = (extras_ref[...] + extras_other_ref[...].astype(F32)).astype(BF)


def add_arrived(core_ref, arrived_ref, kept_ref, given_ref):
    total = arrived_ref[0].astype(F32)
    for chip in range(1, arrived_ref.shape[0]):
        total = total + arrived_ref[chip].astype(F32)
    first = core_ref[0] == 0
    kept_ref[...] = jnp.where(first, total[:OWN], total[OWN:])
    given_ref[...] = jnp.where(first, total[OWN:, : QH + OH], total[:OWN, : QH + OH])


def lay_out(
    core_ref, kept_ref, other_ref, qkv_out, out_out, router_out, one_ref, two_ref, rel_ref, qkv_ref, out_ref, router_ref,
    semaphores,
):
    core = core_ref[0]
    own, other = places(core, QH)
    own_out, other_out = places(core, OH)
    extras = kept_ref[:, QH + OH :]
    for row in range(OWN):
        at = slice(row, row + 1)
        qkv_ref[row, :, own] = kept_ref[at, :QH]
        qkv_ref[row, :, other] = other_ref[at, :QH]
        out_ref[row, :, own_out] = kept_ref[at, QH : QH + OH]
        out_ref[row, :, other_out] = other_ref[at, QH:]
        router_ref[row] = extras[at, :EXPERTS]
    copies = [
        begin_copy(source, target, semaphores.at[at])
        for at, (source, target) in enumerate(((qkv_ref, qkv_out), (out_ref, out_out), (router_ref, router_out)))
    ]
    eye = iota((OWN, OWN), 0) == iota((OWN, OWN), 1)
    for k, target in enumerate((one_ref, two_ref)):
        column = extras[:, GAIN_AT + k : GAIN_AT + k + 1]
        target[...] = jnp.sum(jnp.where(eye, column, 0.0), axis=0, keepdims=True)
    rel_ref[...] = extras[:1, REL_AT : REL_AT + REL_OWN]
    for copy in copies:
        copy.wait()


def shaped(*pairs):
    return [jax.ShapeDtypeStruct(shape, dtype) for shape, dtype in pairs]


def fetching(body, wanted, count, *refs):
    inputs, rest = list(refs[:count]), refs[count:]
    spaces, semaphores, rest = rest[-1 - len(wanted) : -1], rest[-1], rest[: -1 - len(wanted)]
    copies = [
        begin_copy(inputs[at], space, semaphores.at[order]) for order, (at, space) in enumerate(zip(wanted, spaces))
    ]
    for at, space in zip(wanted, spaces):
        inputs[at] = space
    for copy in copies:
        copy.wait()
    body(*inputs, *rest)


def run(body, inputs, outputs, scratch=(), scalars=0, flops=0, far_in=(), far_out=(), fetched=()):
    size = sum(value.size * value.dtype.itemsize for value in inputs)
    size += sum(value.size * value.dtype.itemsize for value in outputs)
    scratch, far_in = list(scratch), tuple(far_in) + tuple(fetched)
    if fetched:
        body = functools.partial(fetching, body, fetched, len(inputs))
        scratch += [pltpu.VMEM(inputs[at].shape, inputs[at].dtype) for at in fetched]
        scratch += [pltpu.SemaphoreType.DMA((len(fetched),))]
    inputs = [
        pltpu.with_memory_space_constraint(value, pltpu.HBM) if at in far_in else value
        for at, value in enumerate(inputs)
    ]
    return pl.pallas_call(
        body,
        out_shape=[
            pltpu.HBM(value.shape, value.dtype) if at in far_out else value for at, value in enumerate(outputs)
        ],
        in_specs=[SMEM if at < scalars else HBM if at in far_in else VMEM for at in range(len(inputs))],
        out_specs=[HBM if at in far_out else VMEM for at in range(len(outputs))],
        scratch_shapes=scratch,
        compiler_params=pltpu.CompilerParams(vmem_limit_bytes=LIMIT),
        cost_estimate=pl.CostEstimate(flops=flops, bytes_accessed=size, transcendentals=0),
    )(*inputs)


def gather_dense(core, chips, kept, given):
    other = core_swap(given)
    pair = jnp.concatenate(
        [jnp.where(core == 0, kept, other), jnp.where(core == 0, other, kept)], axis=0
    )
    spread = jnp.broadcast_to(pair[None], (chips,) + pair.shape)
    mine = chip_exchange(spread).reshape(chips * 2 * OWN, WIDE)
    return mine, core_swap(mine)


def from_experts(mine, theirs):
    total = (mine.astype(F32) + core_swap(theirs).astype(F32)).astype(BF)
    return chip_exchange(total)


def per_device(
    tokens,
    cotangent,
    lengths,
    routes,
    buckets,
    qkv_weight,
    out_weight,
    router_weight,
    norm1_gain,
    norm2_gain,
    rel_bias,
    expert_in,
    expert_out,
):
    chips = lax.axis_size("chip")
    core = lax.axis_index("core")
    section = lax.axis_index("section")
    last = lax.axis_size("section") - 1
    first, second = expert_in[0, 0], expert_out[0, 0]
    where = core.astype(jnp.int32).reshape(1)
    kept, given, mask, slots, slots_t, target = run(
        prepare,
        (
            where, lengths, qkv_weight[0], out_weight[0], router_weight[0], norm1_gain, norm2_gain,
            rel_bias, routes[0].transpose(0, 2, 1), buckets.reshape(1, TOK),
        ),
        shaped(
            ((OWN, WIDE), BF),
            ((OWN, WIDE), BF),
            ((ROWS, ROWS), F32),
            ((ROWS, TOP), jnp.int32),
            ((TOP, ROWS), jnp.int32),
            ((1, LANES), jnp.int32),
        ),
        scalars=1,
        fetched=tuple(range(1, 10)),
    )
    mine, theirs = gather_dense(core, chips, kept, given)

    row = (ROWS, D)
    flat = (chips * SLOTS, D)
    wide = (chips * SLOTS, FFH)
    dense_flops = 2 * ROWS * D * (4 * D + LANES) + 4 * H * ROWS * ROWS * LANES + 2 * ROWS * D * EXPERTS * SLOTS
    expert_flops = 4 * chips * SLOTS * D * FFH

    whole = pltpu.VMEM((D, WIDE), BF)
    squares = pltpu.VMEM((H, ROWS, ROWS), F32)
    small_squares = pltpu.VMEM((H, ROWS, ROWS), BF)
    begin = tokens.reshape(row)
    shared = (mine, theirs, mask, target, slots, slots_t)
    middle, gates, buffer = run(
        functools.partial(front, False),
        (where, begin) + shared,
        shaped((row, F32), ((ROWS, LANES), F32), ((EXPERTS, SLOTS, D), BF)),
        [pltpu.VMEM((ROWS, 3 * D), BF), pltpu.VMEM(row, BF), squares],
        scalars=1,
        flops=dense_flops,
    )
    arrived = chip_exchange(buffer)
    arrived = (arrived, core_swap(arrived))
    made = [
        run(
            expert_forward, (rows, first, second), shaped((rows.shape, BF)), [pltpu.VMEM(wide, BF)], flops=expert_flops
        )[0]
        for rows in arrived
    ]
    returned = from_experts(*made)
    (result,) = run(
        combine, (slots, gates, middle, returned), shaped((row, BF)), flops=4 * ROWS * D * EXPERTS * SLOTS
    )
    passed = lax.ppermute(result, "section", [(0, 1), (1, 0)])
    layer_in = jnp.where(section == 0, begin, passed)

    ending = cotangent.reshape(row)
    factors, state, middle, gates, buffer = run(
        functools.partial(front, True),
        (where, layer_in) + shared + (ending,),
        shaped(
            ((ROWS, 2 * D), BF),
            ((ROWS, STATE), BF),
            (row, F32),
            ((ROWS, LANES), F32),
            ((EXPERTS, 2 * SLOTS, D), BF),
        ),
        [
            pltpu.VMEM((ROWS, 3 * D), BF), pltpu.VMEM(row, BF), squares, small_squares, pltpu.VMEM(row, F32),
            pltpu.VMEM(row, BF), whole, pltpu.VMEM((ROWS, ROWS), F32), pltpu.SemaphoreType.DMA((5 + H,)),
        ],
        scalars=1,
        flops=dense_flops,
        far_in=(3, 4),
        far_out=(1, 2),
    )
    factors_other = core_swap(factors)
    arrived = chip_exchange(buffer)
    arrived = (arrived, core_swap(arrived))
    made, hidden, slope = zip(
        *[
            run(
                expert_both,
                (rows, first, second),
                shaped((rows.shape, BF), (wide, BF), (wide, BF)),
                [pltpu.VMEM(wide, BF)] * 3 + [pltpu.SemaphoreType.DMA((2,))],
                flops=2 * expert_flops,
                far_out=(1, 2),
            )
            for rows in arrived
        ]
    )
    returned = from_experts(*made)
    result, input_grad, picked = run(
        finish_middle,
        (where, layer_in, ending, mine, theirs, slots, gates, state, middle, returned),
        shaped((row, BF), (row, BF), ((ROWS, TOP * D), BF)),
        [
            pltpu.VMEM((ROWS, 5 * D), BF), pltpu.VMEM(row, F32), pltpu.VMEM((ROWS, TOP * D), BF), pltpu.VMEM(row, BF),
            pltpu.VMEM(row, BF), pltpu.VMEM((ROWS, 3 * D), BF), small_squares, whole,
            pltpu.SemaphoreType.DMA((4,)),
        ],
        scalars=1,
        flops=2 * dense_flops,
        far_in=(4, 7, 8),
        far_out=(2,),
    )
    passed = lax.ppermute(input_grad, "section", [(0, 1), (1, 0)])
    grad_out = jnp.where(section == last, ending, passed)

    (buffer,) = run(
        send_grad,
        (gates, grad_out, slots_t),
        shaped(((EXPERTS, SLOTS, D), BF)),
        flops=4 * ROWS * D * EXPERTS * SLOTS,
    )
    grads = chip_exchange(buffer)
    grads = (grads, core_swap(grads))
    made_own, made_other, *pre_grad = run(
        expert_back,
        (*grads, first, second, *slope),
        shaped((grads[0].shape, BF), (grads[0].shape, BF), (wide, BF), (wide, BF)),
        [
            pltpu.VMEM((FFH, D), BF), pltpu.VMEM((2,) + wide, BF), pltpu.VMEM((2,) + wide, BF),
            pltpu.SemaphoreType.DMA((BLOCKS + 8,)),
        ],
        flops=2 * expert_flops,
        far_in=(3, 4, 5),
        far_out=(2, 3),
    )
    returned = from_experts(made_own, made_other)
    input_grad, projected_grad, branch, extras = run(
        finish_last,
        (where, layer_in, grad_out, mine, theirs, target, slots, gates, state, middle, picked, returned),
        shaped((row, F32), ((ROWS, 3 * D), BF), (row, BF), ((D, LANES), F32)),
        [
            pltpu.VMEM((ROWS, STATE), BF), pltpu.VMEM(row, F32), pltpu.VMEM((ROWS, TOP * D), BF), pltpu.VMEM(row, BF),
            small_squares, pltpu.VMEM((2, LANES, LANES), F32), whole,
            pltpu.VMEM(row, BF), pltpu.VMEM((ROWS, TOP), jnp.int32), pltpu.VMEM((ROWS, LANES), F32),
            pltpu.SemaphoreType.DMA((7,)),
        ],
        scalars=1,
        flops=2 * dense_flops,
        far_in=(2, 4, 6, 7, 8, 9, 10),
    )
    given = jnp.concatenate(
        [
            lax.dynamic_slice(projected_grad, (0, (1 - core) * QH), (ROWS, QH)),
            lax.dynamic_slice(branch, (0, (1 - core) * OH), (ROWS, OH)),
        ],
        axis=1,
    )
    (total,) = run(
        weight_totals,
        (
            where, factors, factors_other, projected_grad, branch,
            core_swap(given), extras, core_swap(extras.astype(BF)),
        ),
        shaped(((D, WIDE), BF)),
        scalars=1,
        flops=4 * ROWS * D * WIDE,
    )
    total, hidden, grads, arrived, pre_grad = lax.optimization_barrier(
        (total, hidden, grads, arrived, tuple(pre_grad))
    )
    summands = chip_exchange(total.reshape(chips, 2 * OWN, WIDE))
    second_total = sum(mm_tn(value, rows.reshape(flat)) for value, rows in zip(hidden, grads))
    first_total = sum(mm_tn(rows[:, :SLOTS].reshape(flat), value) for rows, value in zip(arrived, pre_grad))
    summands, first_total, second_total = lax.optimization_barrier((summands, first_total, second_total))
    kept, given = run(
        add_arrived, (where, summands), shaped(((OWN, WIDE), F32), ((OWN, QH + OH), F32)), scalars=1
    )
    dense_grads = run(
        lay_out,
        (where, kept, core_swap(given)),
        shaped(
            ((OWN, 1, 3 * D), F32),
            ((OWN, 1, D), F32),
            ((OWN, 1, EXPERTS), F32),
            ((1, OWN), F32),
            ((1, OWN), F32),
            ((1, REL_OWN), F32),
        ),
        [
            pltpu.VMEM((OWN, 1, 3 * D), F32), pltpu.VMEM((OWN, 1, D), F32), pltpu.VMEM((OWN, 1, EXPERTS), F32),
            pltpu.SemaphoreType.DMA((3,)),
        ],
        scalars=1,
        far_out=(0, 1, 2),
    )
    return (
        result.reshape(1, MB, TOK, D),
        input_grad.reshape(1, MB, TOK, D),
        dense_grads[0].transpose(1, 0, 2),
        dense_grads[1].transpose(1, 0, 2),
        dense_grads[2].transpose(1, 0, 2),
        dense_grads[3],
        dense_grads[4],
        dense_grads[5],
        first_total[None, None],
        second_total[None, None],
    )


def solution(mesh):
    sections, members = mesh.devices.shape
    fine = Mesh(mesh.devices.reshape(sections, members // 2, 2), ("section", "chip", "core"))
    dp = ("chip", "core")
    return jax.shard_map(
        per_device,
        mesh=fine,
        in_specs=(
            P(None, dp, None),
            P(None, dp, None),
            P(None, dp, None),
            P("section", None, dp, None),
            P(),
            P("section", dp, None),
            P("section", dp, None),
            P("section", dp, None),
            P("section", dp),
            P("section", dp),
            P("section", dp),
            P("section", dp, None, None),
            P("section", dp, None, None),
        ),
        out_specs=(
            P("section", None, dp, None),
            P("section", None, dp, None),
            P("section", dp, None),
            P("section", dp, None),
            P("section", dp, None),
            P("section", dp),
            P("section", dp),
            P("section", dp),
            P("section", dp, None, None),
            P("section", dp, None, None),
        ),
        check_vma=False,
    )
```

```python
import functools

import jax
import jax.numpy as jnp
from jax import lax
from jax.experimental import pallas as pl
from jax.experimental.pallas import tpu as pltpu
from jax.sharding import Mesh, PartitionSpec as P

D = 768
H = 12
HD = 64
TOK = 64
MB = 2
NB = 32
TOP = 2
CAP = 8
ROWS = MB * TOK
LANES = 128
EXPERTS = 32
SLOTS = MB * CAP
FFH = 1536
QH = 3 * D // 2
OH = D // 2
WIDE = QH + OH + LANES
GAIN_AT = EXPERTS
REL_AT = EXPERTS + 2
REL_OWN = 6
OWN = 12
BLOCKS = 6
BLOCK = FFH // BLOCKS

EPSILON = 1e-06
SCALE = HD ** (-0.5)
BF = jnp.bfloat16
F32 = jnp.float32
VMEM = pl.BlockSpec(memory_space=pltpu.VMEM)
SMEM = pl.BlockSpec(memory_space=pltpu.SMEM)
HBM = pl.BlockSpec(memory_space=pltpu.HBM)
STATE = 6 * D
LIMIT = 24 * 1024 * 1024


def mm(a, b):
    return jnp.dot(a, b, preferred_element_type=F32)


def mm_nt(a, b):
    return lax.dot_general(a, b, (((1,), (1,)), ((), ())), preferred_element_type=F32)


def mm_tn(a, b):
    return lax.dot_general(a, b, (((0,), (0,)), ((), ())), preferred_element_type=F32)


def begin_copy(source, target, semaphore):
    copy = pltpu.make_async_copy(source, target, semaphore)
    copy.start()
    return copy


def halves(value):
    high = value.astype(BF)
    return high, (value - high.astype(F32)).astype(BF)


def core_swap(value):
    return lax.ppermute(value, "core", [(0, 1), (1, 0)])


def chip_exchange(value):
    return lax.all_to_all(value, "chip", split_axis=0, concat_axis=0, tiled=True)


def iota(shape, axis):
    return lax.broadcasted_iota(jnp.int32, shape, axis)


def places(core, width):
    mine = pl.multiple_of(core * width, LANES)
    theirs = pl.multiple_of((1 - core) * width, LANES)
    return pl.ds(mine, width), pl.ds(theirs, width)


def gain_rows(mine_ref):
    chosen = (iota((16, LANES), 1) == iota((16, LANES), 0) + GAIN_AT).astype(BF)
    return mm_nt(chosen, mine_ref[:, QH + OH :])


def norm_factor(values):
    return lax.rsqrt(jnp.mean(values * values, axis=-1, keepdims=True) + EPSILON)


def norm_back(values, gain, grad_in):
    factor = norm_factor(values)
    normed = values * factor
    weighted = grad_in * gain
    value_grad = factor * (weighted - normed * jnp.mean(weighted * normed, axis=-1, keepdims=True))
    return value_grad, grad_in * normed


def gelu_parts(pre):
    outer = 0.7978845608028654
    inner = outer * 0.044715
    square = pre * pre
    share = 0.5 + 0.5 * jnp.tanh(pre * (outer + inner * square))
    hidden = pre * share
    return share, hidden, square


def gelu_slope(share, hidden, square):
    outer = 0.7978845608028654
    inner = outer * 0.044715
    return share + hidden * (1.0 - share) * (2.0 * outer + 6.0 * inner * square)


def two_heads(values):
    low = iota((1, LANES), 1) < HD
    zero = jnp.zeros_like(values)
    return jnp.concatenate([jnp.where(low, values, zero), jnp.where(low, zero, values)], axis=0)


def slot_rows(slots_t_ref, k):
    return iota((EXPERTS * SLOTS, ROWS), 0) == slots_t_ref[k : k + 1, :]


def slot_columns(slots_ref, k):
    return iota((ROWS, EXPERTS * SLOTS), 1) == slots_ref[:, k : k + 1]


def bucket_rows(target_ref, part):
    return (iota((D, LANES), 0) == target_ref[...] + OWN * part).astype(BF)


def as_column(row_ref):
    size = row_ref.shape[1]
    eye = iota((size, size), 0) == iota((size, size), 1)
    return jnp.sum(jnp.where(eye, row_ref[...].astype(F32), 0.0), axis=1, keepdims=True)


def prepare(
    core_ref, lengths_ref, qkv_ref, out_ref, router_ref, one_ref, two_ref, rel_ref, routes_in, buckets_ref,
    kept_ref, given_ref, mask_ref, slots_ref, slots_t_ref, target_ref,
):
    core = core_ref[0]
    lane = iota((OWN, LANES), 1)
    extras = mm(router_ref[...], (iota((EXPERTS, LANES), 0) == iota((EXPERTS, LANES), 1)).astype(BF))
    extras = extras + jnp.where(lane == GAIN_AT, as_column(one_ref), 0.0)
    extras = extras + jnp.where(lane == GAIN_AT + 1, as_column(two_ref), 0.0)
    moved = iota((REL_OWN, LANES), 0) + REL_AT == iota((REL_OWN, LANES), 1)
    rel = jnp.sum(jnp.where(moved, as_column(rel_ref), 0.0), axis=0, keepdims=True)
    extras = extras + jnp.where(iota((OWN, LANES), 0) == 0, rel, 0.0)
    for target, at in zip((kept_ref, given_ref), (0, 1)):
        target[:, :QH] = qkv_ref[:, places(core, QH)[at]]
        target[:, QH : QH + OH] = out_ref[:, places(core, OH)[at]]
        target[:, QH + OH :] = extras.astype(BF)

    def segment(axis):
        place = iota((ROWS, ROWS), axis)
        early = (place >= lengths_ref[0, :, 0:1]).astype(jnp.int32)
        late = 2 + (place >= TOK + lengths_ref[1, :, 0:1]).astype(jnp.int32)
        return jnp.where(place < TOK, early, late)

    row, column = iota((ROWS, ROWS), 0), iota((ROWS, ROWS), 1)
    seen = (segment(0) == segment(1)) & (row <= column)
    mask_ref[...] = jnp.where(seen, 0.0, -1e30)
    together = (row < TOK) == (column < TOK)
    rows = [jnp.concatenate([routes_in[m, k : k + 1, :] for m in range(MB)], axis=1) for k in range(TOP)]
    columns = [jnp.sum(jnp.where(row == column, value, 0), axis=1, keepdims=True) for value in rows]
    for k in range(TOP):
        own, own_t = columns[k], rows[k]
        rank = jnp.zeros((ROWS, ROWS), jnp.int32)
        rank_t = jnp.zeros((ROWS, ROWS), jnp.int32)
        for other in range(TOP):
            same = together & (own == rows[other]) & (column < row)
            rank = rank + same.astype(jnp.int32)
            same_t = together & (columns[other] == own_t) & (row < column)
            rank_t = rank_t + same_t.astype(jnp.int32)
        micro = (iota((ROWS, 1), 0) >= TOK).astype(jnp.int32)
        micro_t = (iota((1, ROWS), 1) >= TOK).astype(jnp.int32)
        slots_ref[:, k : k + 1] = own * SLOTS + micro * CAP + jnp.sum(rank, axis=1, keepdims=True)
        slots_t_ref[k : k + 1, :] = own_t * SLOTS + micro_t * CAP + jnp.sum(rank_t, axis=0, keepdims=True)
    target_ref[...] = jnp.concatenate([buckets_ref[...] * (2 * OWN), jnp.zeros((1, LANES - TOK), jnp.int32)], axis=1)


def front(saving, core_ref, x_ref, mine_ref, theirs_ref, mask_ref, target_ref, slots_ref, slots_t_ref, *refs):
    if saving:
        grad_ref, factor_ref, state_ref, kept_ref, gates_ref, buffer_ref = refs[:6]
        projected_ref, attended_ref, scores_ref, probs_ref, middle_ref, moe_ref, theirs_space, mask_space, semaphores = refs[6:]
    else:
        middle_ref, gates_ref, buffer_ref, projected_ref, attended_ref, scores_ref = refs
        probs_ref = scores_ref
    core = core_ref[0]
    if saving:
        coming_theirs = begin_copy(theirs_ref, theirs_space, semaphores.at[0])
        coming_mask = begin_copy(mask_ref, mask_space, semaphores.at[4 + H])
        theirs_ref, mask_ref = theirs_space, mask_space
    x = x_ref[...].astype(F32)
    gains = gain_rows(mine_ref)
    normed = (x * norm_factor(x) * gains[0:1]).astype(BF)
    if saving:
        factor_ref[:, :D] = normed
    extras = mine_ref[:, QH + OH :]
    rel = [mm_tn(extras, bucket_rows(target_ref, part)) for part in range(2)]
    if saving:
        coming_mask.wait()
    mask = mask_ref[...]
    for head in range(H):
        row = REL_AT + head % REL_OWN
        spread = jnp.broadcast_to(rel[head // REL_OWN][row : row + 1, :], (ROWS, LANES))
        scores_ref[head] = pltpu.roll(spread, 0, 1, stride=1, stride_axis=0) + mask
    own, other = places(core, QH)
    projected_ref[:, own] = mm(normed, mine_ref[:, :QH]).astype(BF)
    if saving:
        coming_theirs.wait()
    projected_ref[:, other] = mm(normed, theirs_ref[:, :QH]).astype(BF)
    copies = []
    if saving:
        copies.append(begin_copy(projected_ref, state_ref.at[:, : 3 * D], semaphores.at[3 + H]))
    for pair in range(H // 2):
        at = pair * LANES
        query = projected_ref[:, at : at + LANES]
        scores = mm_nt(two_heads(projected_ref[:, D + at : D + at + LANES]), query) * SCALE
        for side in range(2):
            scores_ref[2 * pair + side] += scores[side * ROWS : (side + 1) * ROWS]
    for head in range(H):
        scores = scores_ref[head]
        raised = jnp.exp(scores - jnp.max(scores, axis=0, keepdims=True))
        probs = raised * (1.0 / jnp.sum(raised, axis=0, keepdims=True))
        probs_ref[head] = probs.astype(probs_ref.dtype)
    if saving:
        for head in range(H):
            place = state_ref.at[:, 3 * D + head * ROWS : 3 * D + (head + 1) * ROWS]
            copies.append(begin_copy(probs_ref.at[head], place, semaphores.at[3 + head]))
    for pair in range(H // 2):
        at = pair * LANES
        value = two_heads(projected_ref[:, 2 * D + at : 2 * D + at + LANES])
        probs = probs_ref[2 * pair : 2 * pair + 2].reshape(2 * ROWS, ROWS).astype(BF)
        attended_ref[:, at : at + LANES] = mm_tn(probs, value).astype(BF)
    attended = attended_ref[...]
    if saving:
        factor_ref[:, D:] = attended
    own, other = places(core, OH)
    middle_ref[:, own] = mm(attended, mine_ref[:, QH : QH + OH])
    middle_ref[:, other] = mm(attended, theirs_ref[:, QH : QH + OH])
    middle = x + middle_ref[...]
    middle_ref[...] = middle
    if saving:
        copies.append(begin_copy(middle_ref, kept_ref, semaphores.at[1]))
    moe_in = (middle * norm_factor(middle) * gains[1:2]).astype(BF)
    logits = mm(moe_in, extras)
    lane = iota((ROWS, LANES), 1)
    picked = [
        jnp.sum(jnp.where(lane == slots_ref[:, k : k + 1] // SLOTS, logits, 0.0), axis=-1, keepdims=True)
        for k in range(TOP)
    ]
    peak = jnp.maximum(picked[0], picked[1])
    raised = [jnp.exp(value - peak) for value in picked]
    gates = [value / (raised[0] + raised[1]) for value in raised]
    gates_ref[...] = jnp.where(lane == 0, gates[0], jnp.where(lane == 1, gates[1], 0.0))
    tables = [slot_rows(slots_t_ref, k) for k in range(TOP)]
    buffer = mm((tables[0] | tables[1]).astype(BF), moe_in).astype(BF)
    buffer_ref[:, :SLOTS, :] = buffer.reshape(EXPERTS, SLOTS, D)
    if saving:
        moe_ref[...] = moe_in
        copies.append(begin_copy(moe_ref, state_ref.at[:, 5 * D : 6 * D], semaphores.at[2]))
        grad = grad_ref[...].astype(F32)
        buffer_ref[:, SLOTS:, :] = spread_grad(tables, gates, grad).reshape(EXPERTS, SLOTS, D)
    for copy in copies:
        copy.wait()


def spread_grad(tables, gates, grad):
    return sum(
        mm(table.astype(BF), (gate * grad).astype(BF)) for table, gate in zip(tables, gates)
    ).astype(BF)


def send_grad(gates_ref, grad_ref, slots_t_ref, buffer_ref):
    grad = grad_ref[...].astype(F32)
    gates = [gates_ref[:, k : k + 1] for k in range(TOP)]
    tables = [slot_rows(slots_t_ref, k) for k in range(TOP)]
    buffer_ref[...] = spread_grad(tables, gates, grad).reshape(EXPERTS, SLOTS, D)


def expert_forward(at, rows_ref, first_ref, second_ref, made_ref, hidden_ref):
    rows = rows_ref[at].reshape(-1, D)
    for block in range(BLOCKS):
        part = slice(block * BLOCK, (block + 1) * BLOCK)
        _, hidden, _ = gelu_parts(mm(rows, first_ref[:, part]))
        hidden_ref[:, part] = hidden.astype(BF)
    made_ref[...] = mm(hidden_ref[...], second_ref[...]).astype(BF).reshape(made_ref.shape)


def expert_both(
    at, rows_ref, first_ref, second_ref, made_ref, hidden_out, slope_out, hidden_ref, slope_ref, pre_ref, semaphores
):
    rows = rows_ref[at, :SLOTS, :].reshape(-1, D)
    grads = rows_ref[at, SLOTS:, :].reshape(-1, D)
    for block in range(BLOCKS):
        part = slice(block * BLOCK, (block + 1) * BLOCK)
        share, hidden, square = gelu_parts(mm(rows, first_ref[:, part]))
        hidden_ref[:, part] = hidden.astype(BF)
        slope = gelu_slope(share, hidden, square)
        slope_ref[:, part] = slope.astype(BF)
        pre_ref[:, part] = (mm_nt(grads, second_ref[part, :]) * slope).astype(BF)
    copies = [
        begin_copy(hidden_ref, hidden_out, semaphores.at[0]),
        begin_copy(slope_ref, slope_out, semaphores.at[1]),
    ]
    made_ref[:, :SLOTS, :] = mm(hidden_ref[...], second_ref[...]).astype(BF).reshape(-1, SLOTS, D)
    made_ref[:, SLOTS:, :] = mm_nt(pre_ref[...], first_ref[...]).astype(BF).reshape(-1, SLOTS, D)
    for copy in copies:
        copy.wait()


def expert_back(at, grads_ref, first_ref, second_ref, slope_ref, made_ref, pre_out, pre_ref, semaphores):
    grads = grads_ref[at].reshape(-1, D)
    for block in range(BLOCKS):
        part = slice(block * BLOCK, (block + 1) * BLOCK)
        slope = slope_ref[:, part].astype(F32)
        pre_ref[:, part] = (mm_nt(grads, second_ref[part, :]) * slope).astype(BF)
    leaving = begin_copy(pre_ref, pre_out, semaphores.at[0])
    made_ref[...] = mm_nt(pre_ref[...], first_ref[...]).astype(BF).reshape(made_ref.shape)
    leaving.wait()


def combine(slots_ref, gates_ref, middle_ref, returned_ref, out_ref):
    returned = returned_ref[...].reshape(-1, D)
    out = middle_ref[...]
    for k in range(TOP):
        out = out + gates_ref[:, k : k + 1] * mm(slot_columns(slots_ref, k).astype(BF), returned)
    out_ref[...] = out.astype(BF)


def attention_back(
    core, grad, picked, back_rows, x_ref, mine_ref, theirs_ref, slots_ref, gates_ref, projected_ref,
    probs_ref, middle_ref, branch_ref, branch_grad_ref, projected_grad_ref, score_grad_ref, rel_ref=None,
):
    gates = [gates_ref[:, k : k + 1] for k in range(TOP)]
    gate_grad = [jnp.sum(rows * grad, axis=-1, keepdims=True) for rows in picked]
    shared = gates[0] * gate_grad[0] + gates[1] * gate_grad[1]
    lane = iota((ROWS, LANES), 1)
    logit_grad = sum(
        jnp.where(lane == slots_ref[:, k : k + 1] // SLOTS, gates[k] * (gate_grad[k] - shared), 0.0)
        for k in range(TOP)
    )
    extras = mine_ref[:, QH + OH :]
    logit_high, logit_low = halves(logit_grad)
    tables = (slot_columns(slots_ref, 0) | slot_columns(slots_ref, 1)).astype(BF)
    moe_grad = mm(tables, back_rows) + mm_nt(logit_high, extras) + mm_nt(logit_low, extras)
    gains = gain_rows(mine_ref)
    middle_grad, gain_two = norm_back(middle_ref[...], gains[1:2], moe_grad)
    middle_grad = middle_grad + grad
    branch_ref[...] = middle_grad.astype(BF)
    own, other = places(core, OH)
    branch_grad_ref[...] = (
        mm_nt(branch_ref[:, own], mine_ref[:, QH : QH + OH])
        + mm_nt(branch_ref[:, other], theirs_ref[:, QH : QH + OH])
    ).astype(BF)
    for pair in range(H // 2):
        at = pair * LANES
        value = two_heads(projected_ref[:, 2 * D + at : 2 * D + at + LANES])
        coming = branch_grad_ref[:, at : at + LANES]
        prob_grad = mm_nt(value, coming)
        for side in range(2):
            head = 2 * pair + side
            probs = probs_ref[:, head * ROWS : (head + 1) * ROWS].astype(F32)
            own_grad = prob_grad[side * ROWS : (side + 1) * ROWS]
            score_grad = probs * (own_grad - jnp.sum(probs * own_grad, axis=0, keepdims=True))
            score_grad_ref[head] = score_grad.astype(BF)
    for pair in range(H // 2):
        at = pair * LANES
        query = two_heads(projected_ref[:, at : at + LANES])
        key = two_heads(projected_ref[:, D + at : D + at + LANES])
        coming = two_heads(branch_grad_ref[:, at : at + LANES])
        probs = probs_ref[:, 2 * pair * ROWS : 2 * (pair + 1) * ROWS]
        tall = score_grad_ref[2 * pair : 2 * pair + 2].reshape(2 * ROWS, ROWS)
        wide = jnp.concatenate([tall[:ROWS], tall[ROWS:]], axis=1)
        projected_grad_ref[:, at : at + LANES] = (mm_tn(tall, key) * SCALE).astype(BF)
        projected_grad_ref[:, D + at : D + at + LANES] = (mm(wide, query) * SCALE).astype(BF)
        projected_grad_ref[:, 2 * D + at : 2 * D + at + LANES] = mm(probs, coming).astype(BF)
    if rel_ref is not None:
        backwards = (iota((ROWS, ROWS), 0) + iota((ROWS, ROWS), 1) == ROWS - 1).astype(BF)
        for head in range(H):
            turned = pltpu.roll(mm(backwards, score_grad_ref[head]), 1, 1, stride=1, stride_axis=0)
            row = REL_AT + head % REL_OWN
            rel_ref[head // REL_OWN, row : row + 1, :] = jnp.sum(turned, axis=0, keepdims=True)
    own, other = places(core, QH)
    normed_grad = mm_nt(projected_grad_ref[:, own], mine_ref[:, :QH]) + mm_nt(
        projected_grad_ref[:, other], theirs_ref[:, :QH]
    )
    x_grad, gain_one = norm_back(x_ref[...].astype(F32), gains[0:1], normed_grad)
    return x_grad + middle_grad, gain_one, gain_two, (logit_high, logit_low)


def finish_middle(
    core_ref, x_ref, grad_ref, mine_ref, theirs_ref, slots_ref, gates_ref, state_ref, middle_ref, returned_ref,
    out_ref, input_ref, picked_out, picked_ref, branch_ref, branch_grad_ref, projected_grad_ref, score_grad_ref,
    semaphores,
):
    returned = returned_ref[:, :SLOTS, :].reshape(-1, D)
    back_rows = returned_ref[:, SLOTS:, :].reshape(-1, D)
    picked = [mm(slot_columns(slots_ref, k).astype(BF), returned) for k in range(TOP)]
    for k in range(TOP):
        picked_ref[:, k * D : (k + 1) * D] = picked[k].astype(BF)
    leaving = begin_copy(picked_ref, picked_out, semaphores.at[0])
    input_grad, _, _, _ = attention_back(
        core_ref[0], grad_ref[...].astype(F32), picked, back_rows, x_ref, mine_ref, theirs_ref, slots_ref,
        gates_ref, state_ref.at[:, : 3 * D], state_ref.at[:, 3 * D : 5 * D], middle_ref, branch_ref, branch_grad_ref, projected_grad_ref, score_grad_ref,
    )
    input_ref[...] = input_grad.astype(BF)
    out = middle_ref[...]
    for k in range(TOP):
        out = out + gates_ref[:, k : k + 1] * picked[k]
    out_ref[...] = out.astype(BF)
    leaving.wait()


def finish_last(
    core_ref, x_ref, grad_ref, mine_ref, theirs_ref, target_ref, slots_ref, gates_ref, state_ref, middle_ref,
    picked_ref, returned_ref, input_ref, projected_grad_ref, branch_ref, extras_ref, given_ref, branch_grad_ref,
    score_grad_ref, rel_ref,
):
    rel_ref[...] = jnp.zeros_like(rel_ref)
    back_rows = returned_ref[...].reshape(-1, D)
    picked = [picked_ref[:, k * D : (k + 1) * D].astype(F32) for k in range(TOP)]
    input_grad, gain_one, gain_two, logits = attention_back(
        core_ref[0], grad_ref[...].astype(F32), picked, back_rows, x_ref, mine_ref, theirs_ref, slots_ref,
        gates_ref, state_ref.at[:, : 3 * D], state_ref.at[:, 3 * D : 5 * D], middle_ref, branch_ref, branch_grad_ref, projected_grad_ref, score_grad_ref, rel_ref,
    )
    input_ref[...] = input_grad
    moe_in = state_ref[:, 5 * D : 6 * D]
    lane = iota((ROWS, LANES), 1)
    extras = mm_tn(moe_in, logits[0]) + mm_tn(moe_in, logits[1])
    for at, terms in ((GAIN_AT, gain_one), (GAIN_AT + 1, gain_two)):
        column = (lane == at).astype(BF)
        for piece in halves(terms):
            extras = extras + mm_tn(piece, column)
    for part in range(2):
        table = bucket_rows(target_ref, part)
        for piece in halves(rel_ref[part]):
            extras = extras + mm_nt(table, piece)
    extras_ref[...] = extras
    given_ref[:, :QH] = projected_grad_ref[:, places(core_ref[0], QH)[1]]
    given_ref[:, QH:] = branch_ref[:, places(core_ref[0], OH)[1]]


def weight_totals(
    core_ref, factor_ref, factor_other_ref, projected_ref, branch_ref,
    other_ref, extras_ref, extras_other_ref, total_out, total_ref, semaphores,
):
    own, _ = places(core_ref[0], QH)
    own_out, _ = places(core_ref[0], OH)
    copies = []
    for piece in range(D // BLOCK):
        at = slice(piece * BLOCK, (piece + 1) * BLOCK)
        total_ref[at, :QH] = (
            mm_tn(factor_ref[:, at], projected_ref[:, own]) + mm_tn(factor_other_ref[:, at], other_ref[:, :QH])
        ).astype(BF)
        later = slice(D + piece * BLOCK, D + (piece + 1) * BLOCK)
        total_ref[at, QH : QH + OH] = (
            mm_tn(factor_ref[:, later], branch_ref[:, own_out]) + mm_tn(factor_other_ref[:, later], other_ref[:, QH:])
        ).astype(BF)
        total_ref[at, QH + OH :] = (extras_ref[at, :] + extras_other_ref[at, :].astype(F32)).astype(BF)
        copies.append(begin_copy(total_ref.at[at, :], total_out.at[at, :], semaphores.at[piece]))
    for copy in copies:
        copy.wait()


def add_arrived(core_ref, arrived_ref, kept_ref, given_ref):
    total = arrived_ref[0].astype(F32)
    for chip in range(1, arrived_ref.shape[0]):
        total = total + arrived_ref[chip].astype(F32)
    first = core_ref[0] == 0
    kept_ref[...] = jnp.where(first, total[:OWN], total[OWN:])
    given_ref[...] = jnp.where(first, total[OWN:, : QH + OH], total[:OWN, : QH + OH])


def lay_out(
    core_ref, kept_ref, other_ref, qkv_out, out_out, router_out, one_ref, two_ref, rel_ref, qkv_ref, out_ref, router_ref,
    semaphores,
):
    core = core_ref[0]
    own, other = places(core, QH)
    own_out, other_out = places(core, OH)
    extras = kept_ref[:, QH + OH :]
    for row in range(OWN):
        at = slice(row, row + 1)
        qkv_ref[row, :, own] = kept_ref[at, :QH]
        qkv_ref[row, :, other] = other_ref[at, :QH]
        out_ref[row, :, own_out] = kept_ref[at, QH : QH + OH]
        out_ref[row, :, other_out] = other_ref[at, QH:]
        router_ref[row] = extras[at, :EXPERTS]
    copies = [
        begin_copy(source, target, semaphores.at[at])
        for at, (source, target) in enumerate(((qkv_ref, qkv_out), (out_ref, out_out), (router_ref, router_out)))
    ]
    eye = iota((OWN, OWN), 0) == iota((OWN, OWN), 1)
    for k, target in enumerate((one_ref, two_ref)):
        column = extras[:, GAIN_AT + k : GAIN_AT + k + 1]
        target[...] = jnp.sum(jnp.where(eye, column, 0.0), axis=0, keepdims=True)
    rel_ref[...] = extras[:1, REL_AT : REL_AT + REL_OWN]
    for copy in copies:
        copy.wait()


def shaped(*pairs):
    return [jax.ShapeDtypeStruct(shape, dtype) for shape, dtype in pairs]


def fetching(body, wanted, count, *refs):
    inputs, rest = list(refs[:count]), refs[count:]
    spaces, semaphores, rest = rest[-1 - len(wanted) : -1], rest[-1], rest[: -1 - len(wanted)]
    copies = [
        begin_copy(inputs[at], space, semaphores.at[order]) for order, (at, space) in enumerate(zip(wanted, spaces))
    ]
    for at, space in zip(wanted, spaces):
        inputs[at] = space
    for copy in copies:
        copy.wait()
    body(*inputs, *rest)


def run(body, inputs, outputs, scratch=(), scalars=0, flops=0, far_in=(), far_out=(), fetched=()):
    size = sum(value.size * value.dtype.itemsize for value in inputs)
    size += sum(value.size * value.dtype.itemsize for value in outputs)
    scratch, far_in = list(scratch), tuple(far_in) + tuple(fetched)
    if fetched:
        body = functools.partial(fetching, body, fetched, len(inputs))
        scratch += [pltpu.VMEM(inputs[at].shape, inputs[at].dtype) for at in fetched]
        scratch += [pltpu.SemaphoreType.DMA((len(fetched),))]
    inputs = [
        pltpu.with_memory_space_constraint(value, pltpu.HBM) if at in far_in else value
        for at, value in enumerate(inputs)
    ]
    return pl.pallas_call(
        body,
        out_shape=[
            pltpu.HBM(value.shape, value.dtype) if at in far_out else value for at, value in enumerate(outputs)
        ],
        in_specs=[SMEM if at < scalars else HBM if at in far_in else VMEM for at in range(len(inputs))],
        out_specs=[HBM if at in far_out else VMEM for at in range(len(outputs))],
        scratch_shapes=scratch,
        compiler_params=pltpu.CompilerParams(vmem_limit_bytes=LIMIT),
        cost_estimate=pl.CostEstimate(flops=flops, bytes_accessed=size, transcendentals=0),
    )(*inputs)


def gather_dense(core, chips, kept, given):
    other = core_swap(given)
    pair = jnp.concatenate(
        [jnp.where(core == 0, kept, other), jnp.where(core == 0, other, kept)], axis=0
    )
    spread = jnp.broadcast_to(pair[None], (chips,) + pair.shape)
    mine = chip_exchange(spread).reshape(chips * 2 * OWN, WIDE)
    return mine, core_swap(mine)


def at_experts(arrived, run_part, tied=()):
    half = arrived.shape[0] // 2
    swapped = core_swap(arrived)
    early = run_part(slice(0, half), arrived, 0)
    swapped, first_made = lax.optimization_barrier((swapped, early[0]))
    other = run_part(slice(0, 2 * half), swapped, 1)
    arrived, other_made, tied = lax.optimization_barrier((arrived, other[0], tied))
    late = run_part(slice(half, 2 * half), arrived, 2)
    own = jnp.concatenate([first_made, late[0]], axis=0).astype(F32)
    returned = chip_exchange((own + core_swap(other_made).astype(F32)).astype(BF))
    return returned, (arrived, swapped), list(zip(early, other, late))[1:], tied


def join(pieces):
    return jnp.concatenate([pieces[0], pieces[2]], axis=0), pieces[1]


def per_device(
    tokens,
    cotangent,
    lengths,
    routes,
    buckets,
    qkv_weight,
    out_weight,
    router_weight,
    norm1_gain,
    norm2_gain,
    rel_bias,
    expert_in,
    expert_out,
):
    chips = lax.axis_size("chip")
    core = lax.axis_index("core")
    section = lax.axis_index("section")
    last = lax.axis_size("section") - 1
    first, second = expert_in[0, 0], expert_out[0, 0]
    where = core.astype(jnp.int32).reshape(1)
    kept, given, mask, slots, slots_t, target = run(
        prepare,
        (
            where, lengths, qkv_weight[0], out_weight[0], router_weight[0], norm1_gain, norm2_gain,
            rel_bias, routes[0].transpose(0, 2, 1), buckets.reshape(1, TOK),
        ),
        shaped(
            ((OWN, WIDE), BF),
            ((OWN, WIDE), BF),
            ((ROWS, ROWS), F32),
            ((ROWS, TOP), jnp.int32),
            ((TOP, ROWS), jnp.int32),
            ((1, LANES), jnp.int32),
        ),
        scalars=1,
        fetched=tuple(range(1, 10)),
    )
    mine, theirs = gather_dense(core, chips, kept, given)

    row = (ROWS, D)
    flat = (chips * SLOTS, D)
    wide = (chips * SLOTS, FFH)
    dense_flops = 2 * ROWS * D * (4 * D + LANES) + 4 * H * ROWS * ROWS * LANES + 2 * ROWS * D * EXPERTS * SLOTS
    expert_flops = 4 * chips * SLOTS * D * FFH

    whole = pltpu.VMEM((D, WIDE), BF)
    squares = pltpu.VMEM((H, ROWS, ROWS), F32)
    small_squares = pltpu.VMEM((H, ROWS, ROWS), BF)
    begin = tokens.reshape(row)
    shared = (mine, theirs, mask, target, slots, slots_t)
    middle, gates, buffer = run(
        functools.partial(front, False),
        (where, begin) + shared,
        shaped((row, F32), ((ROWS, LANES), F32), ((EXPERTS, SLOTS, D), BF)),
        [pltpu.VMEM((ROWS, 3 * D), BF), pltpu.VMEM(row, BF), squares],
        scalars=1,
        flops=dense_flops,
    )
    def forward_part(at, rows, _):
        count = at.stop - at.start
        return run(
            functools.partial(expert_forward, at),
            (rows, first, second),
            shaped(((count, SLOTS, D), BF)),
            [pltpu.VMEM((count * SLOTS, FFH), BF)],
            flops=expert_flops * count // chips,
        )

    returned, _, _, _ = at_experts(chip_exchange(buffer), forward_part)
    (result,) = run(
        combine, (slots, gates, middle, returned), shaped((row, BF)), flops=4 * ROWS * D * EXPERTS * SLOTS
    )
    passed = lax.ppermute(result, "section", [(0, 1), (1, 0)])
    layer_in = jnp.where(section == 0, begin, passed)

    ending = cotangent.reshape(row)
    factors, state, middle, gates, buffer = run(
        functools.partial(front, True),
        (where, layer_in) + shared + (ending,),
        shaped(
            ((ROWS, 2 * D), BF),
            ((ROWS, STATE), BF),
            (row, F32),
            ((ROWS, LANES), F32),
            ((EXPERTS, 2 * SLOTS, D), BF),
        ),
        [
            pltpu.VMEM((ROWS, 3 * D), BF), pltpu.VMEM(row, BF), squares, small_squares, pltpu.VMEM(row, F32),
            pltpu.VMEM(row, BF), whole, pltpu.VMEM((ROWS, ROWS), F32), pltpu.SemaphoreType.DMA((5 + H,)),
        ],
        scalars=1,
        flops=dense_flops,
        far_in=(3, 4),
        far_out=(1, 2),
    )
    factors_other = core_swap(factors)
    def both_part(at, rows, _):
        count = at.stop - at.start
        piece = (count * SLOTS, FFH)
        return run(
            functools.partial(expert_both, at),
            (rows, first, second),
            shaped(((count, 2 * SLOTS, D), BF), (piece, BF), (piece, BF)),
            [pltpu.VMEM(piece, BF)] * 3 + [pltpu.SemaphoreType.DMA((2,))],
            flops=2 * expert_flops * count // chips,
            far_out=(1, 2),
        )

    returned, arrived, (hidden, slope), (factors_other,) = at_experts(
        chip_exchange(buffer), both_part, (factors_other,)
    )
    result, input_grad, picked = run(
        finish_middle,
        (where, layer_in, ending, mine, theirs, slots, gates, state, middle, returned),
        shaped((row, BF), (row, BF), ((ROWS, TOP * D), BF)),
        [
            pltpu.VMEM((ROWS, TOP * D), BF), pltpu.VMEM(row, BF), pltpu.VMEM(row, BF), pltpu.VMEM((ROWS, 3 * D), BF),
            small_squares, pltpu.SemaphoreType.DMA((1,)),
        ],
        scalars=1,
        flops=2 * dense_flops,
        far_out=(2,),
    )
    passed = lax.ppermute(input_grad, "section", [(0, 1), (1, 0)])
    grad_out = jnp.where(section == last, ending, passed)

    (buffer,) = run(
        send_grad,
        (gates, grad_out, slots_t),
        shaped(((EXPERTS, SLOTS, D), BF)),
        flops=16 * dense_flops,
    )
    def back_part(at, rows, number):
        count = at.stop - at.start
        piece = (count * SLOTS, FFH)
        return run(
            functools.partial(expert_back, at),
            (rows, first, second, slope[number]),
            shaped(((count, SLOTS, D), BF), (piece, BF)),
            [pltpu.VMEM(piece, BF), pltpu.SemaphoreType.DMA((1,))],
            flops=expert_flops * count // chips,
            far_out=(1,),
        )

    returned, grads, (pre_grad,), _ = at_experts(chip_exchange(buffer), back_part)
    input_grad, projected_grad, branch, extras, given = run(
        finish_last,
        (where, layer_in, grad_out, mine, theirs, target, slots, gates, state, middle, picked, returned),
        shaped((row, F32), ((ROWS, 3 * D), BF), (row, BF), ((D, LANES), F32), ((ROWS, 2 * D), BF)),
        [
            pltpu.VMEM(row, BF), small_squares, pltpu.VMEM((2, LANES, LANES), F32),
        ],
        scalars=1,
        flops=2 * dense_flops,
    )
    (total,) = run(
        weight_totals,
        (
            where, factors, factors_other, projected_grad, branch,
            core_swap(given), extras, core_swap(extras.astype(BF)),
        ),
        shaped(((D, WIDE), BF)),
        [whole, pltpu.SemaphoreType.DMA((D // BLOCK,))],
        scalars=1,
        far_out=(0,),
        fetched=(1, 2),
        flops=4 * ROWS * D * WIDE,
    )
    total, hidden, grads, arrived, pre_grad = lax.optimization_barrier(
        (total, hidden, grads, arrived, pre_grad)
    )
    summands = chip_exchange(total.reshape(chips, 2 * OWN, WIDE))
    second_total = sum(mm_tn(value, rows.reshape(flat)) for value, rows in zip(join(hidden), grads))
    first_total = sum(mm_tn(rows[:, :SLOTS].reshape(flat), value) for rows, value in zip(arrived, join(pre_grad)))
    summands, first_total, second_total = lax.optimization_barrier((summands, first_total, second_total))
    kept, given = run(
        add_arrived, (where, summands), shaped(((OWN, WIDE), F32), ((OWN, QH + OH), F32)), scalars=1
    )
    dense_grads = run(
        lay_out,
        (where, kept, core_swap(given)),
        shaped(
            ((OWN, 1, 3 * D), F32),
            ((OWN, 1, D), F32),
            ((OWN, 1, EXPERTS), F32),
            ((1, OWN), F32),
            ((1, OWN), F32),
            ((1, REL_OWN), F32),
        ),
        [
            pltpu.VMEM((OWN, 1, 3 * D), F32), pltpu.VMEM((OWN, 1, D), F32), pltpu.VMEM((OWN, 1, EXPERTS), F32),
            pltpu.SemaphoreType.DMA((3,)),
        ],
        scalars=1,
        far_out=(0, 1, 2),
    )
    return (
        result.reshape(1, MB, TOK, D),
        input_grad.reshape(1, MB, TOK, D),
        dense_grads[0].transpose(1, 0, 2),
        dense_grads[1].transpose(1, 0, 2),
        dense_grads[2].transpose(1, 0, 2),
        dense_grads[3],
        dense_grads[4],
        dense_grads[5],
        first_total[None, None],
        second_total[None, None],
    )


def solution(mesh):
    sections, members = mesh.devices.shape
    fine = Mesh(mesh.devices.reshape(sections, members // 2, 2), ("section", "chip", "core"))
    dp = ("chip", "core")
    return jax.shard_map(
        per_device,
        mesh=fine,
        in_specs=(
            P(None, dp, None),
            P(None, dp, None),
            P(None, dp, None),
            P("section", None, dp, None),
            P(),
            P("section", dp, None),
            P("section", dp, None),
            P("section", dp, None),
            P("section", dp),
            P("section", dp),
            P("section", dp),
            P("section", dp, None, None),
            P("section", dp, None, None),
        ),
        out_specs=(
            P("section", None, dp, None),
            P("section", None, dp, None),
            P("section", dp, None),
            P("section", dp, None),
            P("section", dp, None),
            P("section", dp),
            P("section", dp),
            P("section", dp),
            P("section", dp, None, None),
            P("section", dp, None, None),
        ),
        check_vma=False,
    )
```

```python
import functools

import jax
import jax.numpy as jnp
from jax import lax
from jax.experimental import pallas as pl
from jax.experimental.pallas import tpu as pltpu
from jax.sharding import Mesh, PartitionSpec as P

D = 768
H = 12
HD = 64
TOK = 64
MB = 2
NB = 32
TOP = 2
CAP = 8
ROWS = MB * TOK
LANES = 128
EXPERTS = 32
SLOTS = MB * CAP
FFH = 1536
QH = 3 * D // 2
OH = D // 2
WIDE = QH + OH + LANES
GAIN_AT = EXPERTS
REL_AT = EXPERTS + 2
REL_OWN = 6
OWN = 12
BLOCKS = 6
BLOCK = FFH // BLOCKS

EPSILON = 1e-06
SCALE = HD ** (-0.5)
BF = jnp.bfloat16
F32 = jnp.float32
VMEM = pl.BlockSpec(memory_space=pltpu.VMEM)
SMEM = pl.BlockSpec(memory_space=pltpu.SMEM)
HBM = pl.BlockSpec(memory_space=pltpu.HBM)
STATE = 6 * D
LIMIT = 24 * 1024 * 1024


def mm(a, b):
    return jnp.dot(a, b, preferred_element_type=F32)


def mm_nt(a, b):
    return lax.dot_general(a, b, (((1,), (1,)), ((), ())), preferred_element_type=F32)


def mm_tn(a, b):
    return lax.dot_general(a, b, (((0,), (0,)), ((), ())), preferred_element_type=F32)


def begin_copy(source, target, semaphore):
    copy = pltpu.make_async_copy(source, target, semaphore)
    copy.start()
    return copy


def halves(value):
    high = value.astype(BF)
    return high, (value - high.astype(F32)).astype(BF)


def core_swap(value):
    return lax.ppermute(value, "core", [(0, 1), (1, 0)])


def chip_exchange(value):
    return lax.all_to_all(value, "chip", split_axis=0, concat_axis=0, tiled=True)


def iota(shape, axis):
    return lax.broadcasted_iota(jnp.int32, shape, axis)


def places(core, width):
    mine = pl.multiple_of(core * width, LANES)
    theirs = pl.multiple_of((1 - core) * width, LANES)
    return pl.ds(mine, width), pl.ds(theirs, width)


def gain_rows(mine_ref):
    chosen = (iota((16, LANES), 1) == iota((16, LANES), 0) + GAIN_AT).astype(BF)
    return mm_nt(chosen, mine_ref[:, QH + OH :])


def norm_factor(values):
    return lax.rsqrt(jnp.mean(values * values, axis=-1, keepdims=True) + EPSILON)


def norm_back(values, gain, grad_in):
    factor = norm_factor(values)
    normed = values * factor
    weighted = grad_in * gain
    value_grad = factor * (weighted - normed * jnp.mean(weighted * normed, axis=-1, keepdims=True))
    return value_grad, grad_in * normed


def gelu_parts(pre):
    outer = 0.7978845608028654
    inner = outer * 0.044715
    square = pre * pre
    share = 0.5 + 0.5 * jnp.tanh(pre * (outer + inner * square))
    hidden = pre * share
    return share, hidden, square


def gelu_slope(share, hidden, square):
    outer = 0.7978845608028654
    inner = outer * 0.044715
    return share + hidden * (1.0 - share) * (2.0 * outer + 6.0 * inner * square)


def two_heads(values):
    low = iota((1, LANES), 1) < HD
    zero = jnp.zeros_like(values)
    return jnp.concatenate([jnp.where(low, values, zero), jnp.where(low, zero, values)], axis=0)


def slot_rows(slots_t_ref, k):
    return iota((EXPERTS * SLOTS, ROWS), 0) == slots_t_ref[k : k + 1, :]


def slot_columns(slots_ref, k):
    return iota((ROWS, EXPERTS * SLOTS), 1) == slots_ref[:, k : k + 1]


def bucket_rows(target_ref, part):
    return (iota((D, LANES), 0) == target_ref[...] + OWN * part).astype(BF)


def as_column(row_ref):
    size = row_ref.shape[1]
    eye = iota((size, size), 0) == iota((size, size), 1)
    return jnp.sum(jnp.where(eye, row_ref[...].astype(F32), 0.0), axis=1, keepdims=True)


def prepare(
    core_ref, lengths_ref, qkv_ref, out_ref, router_ref, one_ref, two_ref, rel_ref, routes_in, buckets_ref,
    kept_ref, given_ref, mask_ref, slots_ref, slots_t_ref, target_ref,
):
    core = core_ref[0]
    lane = iota((OWN, LANES), 1)
    extras = mm(router_ref[...], (iota((EXPERTS, LANES), 0) == iota((EXPERTS, LANES), 1)).astype(BF))
    extras = extras + jnp.where(lane == GAIN_AT, as_column(one_ref), 0.0)
    extras = extras + jnp.where(lane == GAIN_AT + 1, as_column(two_ref), 0.0)
    moved = iota((REL_OWN, LANES), 0) + REL_AT == iota((REL_OWN, LANES), 1)
    rel = jnp.sum(jnp.where(moved, as_column(rel_ref), 0.0), axis=0, keepdims=True)
    extras = extras + jnp.where(iota((OWN, LANES), 0) == 0, rel, 0.0)
    for target, at in zip((kept_ref, given_ref), (0, 1)):
        target[:, :QH] = qkv_ref[:, places(core, QH)[at]]
        target[:, QH : QH + OH] = out_ref[:, places(core, OH)[at]]
        target[:, QH + OH :] = extras.astype(BF)

    def segment(axis):
        place = iota((ROWS, ROWS), axis)
        early = (place >= lengths_ref[0, :, 0:1]).astype(jnp.int32)
        late = 2 + (place >= TOK + lengths_ref[1, :, 0:1]).astype(jnp.int32)
        return jnp.where(place < TOK, early, late)

    row, column = iota((ROWS, ROWS), 0), iota((ROWS, ROWS), 1)
    seen = (segment(0) == segment(1)) & (row <= column)
    mask_ref[...] = jnp.where(seen, 0.0, -1e30)
    together = (row < TOK) == (column < TOK)
    rows = [jnp.concatenate([routes_in[m, k : k + 1, :] for m in range(MB)], axis=1) for k in range(TOP)]
    columns = [jnp.sum(jnp.where(row == column, value, 0), axis=1, keepdims=True) for value in rows]
    for k in range(TOP):
        own, own_t = columns[k], rows[k]
        rank = jnp.zeros((ROWS, ROWS), jnp.int32)
        rank_t = jnp.zeros((ROWS, ROWS), jnp.int32)
        for other in range(TOP):
            same = together & (own == rows[other]) & (column < row)
            rank = rank + same.astype(jnp.int32)
            same_t = together & (columns[other] == own_t) & (row < column)
            rank_t = rank_t + same_t.astype(jnp.int32)
        micro = (iota((ROWS, 1), 0) >= TOK).astype(jnp.int32)
        micro_t = (iota((1, ROWS), 1) >= TOK).astype(jnp.int32)
        slots_ref[:, k : k + 1] = own * SLOTS + micro * CAP + jnp.sum(rank, axis=1, keepdims=True)
        slots_t_ref[k : k + 1, :] = own_t * SLOTS + micro_t * CAP + jnp.sum(rank_t, axis=0, keepdims=True)
    target_ref[...] = jnp.concatenate([buckets_ref[...] * (2 * OWN), jnp.zeros((1, LANES - TOK), jnp.int32)], axis=1)


def front(saving, core_ref, x_ref, mine_ref, theirs_ref, mask_ref, target_ref, slots_ref, slots_t_ref, *refs):
    if saving:
        grad_ref, factor_ref, state_ref, kept_ref, gates_ref, buffer_ref = refs[:6]
        projected_ref, attended_ref, scores_ref, probs_ref, middle_ref, moe_ref, theirs_space, mask_space, semaphores = refs[6:]
    else:
        middle_ref, gates_ref, buffer_ref, projected_ref, attended_ref, scores_ref = refs
        probs_ref = scores_ref
    core = core_ref[0]
    if saving:
        coming_theirs = begin_copy(theirs_ref, theirs_space, semaphores.at[0])
        coming_mask = begin_copy(mask_ref, mask_space, semaphores.at[4 + H])
        theirs_ref, mask_ref = theirs_space, mask_space
    x = x_ref[...].astype(F32)
    gains = gain_rows(mine_ref)
    normed = (x * norm_factor(x) * gains[0:1]).astype(BF)
    if saving:
        factor_ref[:, :D] = normed
    extras = mine_ref[:, QH + OH :]
    rel = [mm_tn(extras, bucket_rows(target_ref, part)) for part in range(2)]
    if saving:
        coming_mask.wait()
    mask = mask_ref[...]
    for head in range(H):
        row = REL_AT + head % REL_OWN
        spread = jnp.broadcast_to(rel[head // REL_OWN][row : row + 1, :], (ROWS, LANES))
        scores_ref[head] = pltpu.roll(spread, 0, 1, stride=1, stride_axis=0) + mask
    own, other = places(core, QH)
    projected_ref[:, own] = mm(normed, mine_ref[:, :QH]).astype(BF)
    if saving:
        coming_theirs.wait()
    projected_ref[:, other] = mm(normed, theirs_ref[:, :QH]).astype(BF)
    copies = []
    if saving:
        copies.append(begin_copy(projected_ref, state_ref.at[:, : 3 * D], semaphores.at[3 + H]))
    for pair in range(H // 2):
        at = pair * LANES
        query = projected_ref[:, at : at + LANES]
        scores = mm_nt(two_heads(projected_ref[:, D + at : D + at + LANES]), query) * SCALE
        for side in range(2):
            scores_ref[2 * pair + side] += scores[side * ROWS : (side + 1) * ROWS]
    for head in range(H):
        scores = scores_ref[head]
        raised = jnp.exp(scores - jnp.max(scores, axis=0, keepdims=True))
        probs = raised * (1.0 / jnp.sum(raised, axis=0, keepdims=True))
        probs_ref[head] = probs.astype(probs_ref.dtype)
    if saving:
        for head in range(H):
            place = state_ref.at[:, 3 * D + head * ROWS : 3 * D + (head + 1) * ROWS]
            copies.append(begin_copy(probs_ref.at[head], place, semaphores.at[3 + head]))
    for pair in range(H // 2):
        at = pair * LANES
        value = two_heads(projected_ref[:, 2 * D + at : 2 * D + at + LANES])
        probs = probs_ref[2 * pair : 2 * pair + 2].reshape(2 * ROWS, ROWS).astype(BF)
        attended_ref[:, at : at + LANES] = mm_tn(probs, value).astype(BF)
    attended = attended_ref[...]
    if saving:
        factor_ref[:, D:] = attended
    own, other = places(core, OH)
    middle_ref[:, own] = mm(attended, mine_ref[:, QH : QH + OH])
    middle_ref[:, other] = mm(attended, theirs_ref[:, QH : QH + OH])
    middle = x + middle_ref[...]
    middle_ref[...] = middle
    if saving:
        copies.append(begin_copy(middle_ref, kept_ref, semaphores.at[1]))
    moe_in = (middle * norm_factor(middle) * gains[1:2]).astype(BF)
    logits = mm(moe_in, extras)
    lane = iota((ROWS, LANES), 1)
    picked = [
        jnp.sum(jnp.where(lane == slots_ref[:, k : k + 1] // SLOTS, logits, 0.0), axis=-1, keepdims=True)
        for k in range(TOP)
    ]
    peak = jnp.maximum(picked[0], picked[1])
    raised = [jnp.exp(value - peak) for value in picked]
    gates = [value / (raised[0] + raised[1]) for value in raised]
    gates_ref[...] = jnp.where(lane == 0, gates[0], jnp.where(lane == 1, gates[1], 0.0))
    tables = [slot_rows(slots_t_ref, k) for k in range(TOP)]
    buffer = mm((tables[0] | tables[1]).astype(BF), moe_in).astype(BF)
    buffer_ref[:, :SLOTS, :] = buffer.reshape(EXPERTS, SLOTS, D)
    if saving:
        moe_ref[...] = moe_in
        copies.append(begin_copy(moe_ref, state_ref.at[:, 5 * D : 6 * D], semaphores.at[2]))
        grad = grad_ref[...].astype(F32)
        buffer_ref[:, SLOTS:, :] = spread_grad(tables, gates, grad).reshape(EXPERTS, SLOTS, D)
    for copy in copies:
        copy.wait()


def spread_grad(tables, gates, grad):
    return sum(
        mm(table.astype(BF), (gate * grad).astype(BF)) for table, gate in zip(tables, gates)
    ).astype(BF)


def send_grad(gates_ref, grad_ref, slots_t_ref, buffer_ref):
    grad = grad_ref[...].astype(F32)
    gates = [gates_ref[:, k : k + 1] for k in range(TOP)]
    tables = [slot_rows(slots_t_ref, k) for k in range(TOP)]
    buffer_ref[...] = spread_grad(tables, gates, grad).reshape(EXPERTS, SLOTS, D)


def expert_forward(at, rows_ref, first_ref, second_ref, made_ref, hidden_ref):
    rows = rows_ref[at].reshape(-1, D)
    for block in range(BLOCKS):
        part = slice(block * BLOCK, (block + 1) * BLOCK)
        _, hidden, _ = gelu_parts(mm(rows, first_ref[:, part]))
        hidden_ref[:, part] = hidden.astype(BF)
    made_ref[...] = mm(hidden_ref[...], second_ref[...]).astype(BF).reshape(made_ref.shape)


def expert_both(
    at, rows_ref, first_ref, second_ref, back_ref, made_out, hidden_out, slope_out, made_ref, hidden_ref, slope_ref,
    pre_ref, semaphores,
):
    rows = rows_ref[at, :SLOTS, :].reshape(-1, D)
    grads = rows_ref[at, SLOTS:, :].reshape(-1, D)
    for block in range(BLOCKS):
        part = slice(block * BLOCK, (block + 1) * BLOCK)
        share, hidden, square = gelu_parts(mm(rows, first_ref[:, part]))
        hidden_ref[:, part] = hidden.astype(BF)
        slope = gelu_slope(share, hidden, square)
        slope_ref[:, part] = slope.astype(BF)
        pre_ref[:, part] = (mm_nt(grads, second_ref[part, :]) * slope).astype(BF)
    copies = [
        begin_copy(hidden_ref, hidden_out, semaphores.at[0]),
        begin_copy(slope_ref, slope_out, semaphores.at[1]),
    ]
    made_ref[...] = mm(hidden_ref[...], second_ref[...]).astype(BF)
    copies.append(begin_copy(made_ref, made_out, semaphores.at[2]))
    back_ref[:, :, :D] = mm_nt(pre_ref[...], first_ref[...]).astype(BF).reshape(-1, SLOTS, D)
    unit = jnp.sum(made_ref[...].astype(F32) * grads.astype(F32), axis=-1, keepdims=True)
    lane = iota((grads.shape[0], LANES), 1)
    back_ref[:, :, D:] = jnp.where(lane == 0, unit, 0.0).astype(BF).reshape(-1, SLOTS, LANES)
    for copy in copies:
        copy.wait()


def expert_back(at, grads_ref, first_ref, second_ref, slope_ref, made_ref, pre_out, pre_ref, semaphores):
    grads = grads_ref[at].reshape(-1, D)
    for block in range(BLOCKS):
        part = slice(block * BLOCK, (block + 1) * BLOCK)
        slope = slope_ref[:, part].astype(F32)
        pre_ref[:, part] = (mm_nt(grads, second_ref[part, :]) * slope).astype(BF)
    leaving = begin_copy(pre_ref, pre_out, semaphores.at[0])
    made_ref[...] = mm_nt(pre_ref[...], first_ref[...]).astype(BF).reshape(made_ref.shape)
    leaving.wait()


def combine(slots_ref, gates_ref, middle_ref, returned_ref, out_ref, picked_ref=None):
    returned = returned_ref[...].reshape(-1, D)
    out = middle_ref[...]
    for k in range(TOP):
        rows = mm(slot_columns(slots_ref, k).astype(BF), returned)
        out = out + gates_ref[:, k : k + 1] * rows
        if picked_ref is not None:
            picked_ref[:, k * D : (k + 1) * D] = rows.astype(BF)
    out_ref[...] = out.astype(BF)


def last_output(last_ref, slots_ref, gates_ref, middle_ref, returned_ref, picked_ref, out_ref):
    returned = returned_ref[...].reshape(-1, D)
    out = middle_ref[...]
    for k in range(TOP):
        rows = mm(slot_columns(slots_ref, k).astype(BF), returned)
        known = picked_ref[:, k * D : (k + 1) * D].astype(F32)
        out = out + gates_ref[:, k : k + 1] * jnp.where(last_ref[0] == 1, rows, known)
    out_ref[...] = out.astype(BF)


def attention_back(
    core, grad, units, back_rows, x_ref, mine_ref, theirs_ref, slots_ref, gates_ref, projected_ref,
    probs_ref, middle_ref, branch_ref, branch_grad_ref, projected_grad_ref, score_grad_ref, rel_ref=None,
):
    gates = [gates_ref[:, k : k + 1] for k in range(TOP)]
    shared = units[0] + units[1]
    lane = iota((ROWS, LANES), 1)
    logit_grad = sum(
        jnp.where(lane == slots_ref[:, k : k + 1] // SLOTS, units[k] - gates[k] * shared, 0.0)
        for k in range(TOP)
    )
    extras = mine_ref[:, QH + OH :]
    logit_high, logit_low = halves(logit_grad)
    tables = (slot_columns(slots_ref, 0) | slot_columns(slots_ref, 1)).astype(BF)
    moe_grad = mm(tables, back_rows) + mm_nt(logit_high, extras) + mm_nt(logit_low, extras)
    gains = gain_rows(mine_ref)
    middle_grad, gain_two = norm_back(middle_ref[...], gains[1:2], moe_grad)
    middle_grad = middle_grad + grad
    branch_ref[...] = middle_grad.astype(BF)
    own, other = places(core, OH)
    branch_grad_ref[...] = (
        mm_nt(branch_ref[:, own], mine_ref[:, QH : QH + OH])
        + mm_nt(branch_ref[:, other], theirs_ref[:, QH : QH + OH])
    ).astype(BF)
    for pair in range(H // 2):
        at = pair * LANES
        value = two_heads(projected_ref[:, 2 * D + at : 2 * D + at + LANES])
        coming = branch_grad_ref[:, at : at + LANES]
        prob_grad = mm_nt(value, coming)
        for side in range(2):
            head = 2 * pair + side
            probs = probs_ref[:, head * ROWS : (head + 1) * ROWS].astype(F32)
            own_grad = prob_grad[side * ROWS : (side + 1) * ROWS]
            score_grad = probs * (own_grad - jnp.sum(probs * own_grad, axis=0, keepdims=True))
            score_grad_ref[head] = score_grad.astype(BF)
    for pair in range(H // 2):
        at = pair * LANES
        query = two_heads(projected_ref[:, at : at + LANES])
        key = two_heads(projected_ref[:, D + at : D + at + LANES])
        coming = two_heads(branch_grad_ref[:, at : at + LANES])
        probs = probs_ref[:, 2 * pair * ROWS : 2 * (pair + 1) * ROWS]
        tall = score_grad_ref[2 * pair : 2 * pair + 2].reshape(2 * ROWS, ROWS)
        wide = jnp.concatenate([tall[:ROWS], tall[ROWS:]], axis=1)
        projected_grad_ref[:, at : at + LANES] = (mm_tn(tall, key) * SCALE).astype(BF)
        projected_grad_ref[:, D + at : D + at + LANES] = (mm(wide, query) * SCALE).astype(BF)
        projected_grad_ref[:, 2 * D + at : 2 * D + at + LANES] = mm(probs, coming).astype(BF)
    if rel_ref is not None:
        backwards = (iota((ROWS, ROWS), 0) + iota((ROWS, ROWS), 1) == ROWS - 1).astype(BF)
        for head in range(H):
            turned = pltpu.roll(mm(backwards, score_grad_ref[head]), 1, 1, stride=1, stride_axis=0)
            row = REL_AT + head % REL_OWN
            rel_ref[head // REL_OWN, row : row + 1, :] = jnp.sum(turned, axis=0, keepdims=True)
    own, other = places(core, QH)
    normed_grad = mm_nt(projected_grad_ref[:, own], mine_ref[:, :QH]) + mm_nt(
        projected_grad_ref[:, other], theirs_ref[:, :QH]
    )
    x_grad, gain_one = norm_back(x_ref[...].astype(F32), gains[0:1], normed_grad)
    return x_grad + middle_grad, gain_one, gain_two, (logit_high, logit_low)


def sent_units(slots_ref, returned_ref):
    sums = returned_ref[:, :, D:].reshape(-1, LANES)
    return [mm(slot_columns(slots_ref, k).astype(BF), sums)[:, :1] for k in range(TOP)]


def finish_middle(
    core_ref, x_ref, grad_ref, mine_ref, theirs_ref, slots_ref, gates_ref, state_ref, middle_ref, returned_ref,
    input_ref, branch_ref, branch_grad_ref, projected_grad_ref, score_grad_ref,
):
    back_rows = returned_ref[:, :, :D].reshape(-1, D)
    units = sent_units(slots_ref, returned_ref)
    input_grad, _, _, _ = attention_back(
        core_ref[0], grad_ref[...].astype(F32), units, back_rows, x_ref, mine_ref, theirs_ref, slots_ref,
        gates_ref, state_ref.at[:, : 3 * D], state_ref.at[:, 3 * D : 5 * D], middle_ref, branch_ref,
        branch_grad_ref, projected_grad_ref, score_grad_ref,
    )
    input_ref[...] = input_grad.astype(BF)


def finish_last(
    core_ref, last_ref, x_ref, grad_ref, mine_ref, theirs_ref, target_ref, slots_ref, gates_ref, state_ref, middle_ref,
    picked_ref, known_ref, returned_ref, input_ref, projected_grad_ref, branch_ref, extras_ref, given_ref, branch_grad_ref,
    score_grad_ref, rel_ref,
):
    rel_ref[...] = jnp.zeros_like(rel_ref)
    last = last_ref[0] == 1
    back_rows = jnp.where(last, known_ref[:, :, :D].reshape(-1, D), returned_ref[...].reshape(-1, D))
    grad = grad_ref[...].astype(F32)
    known_units = sent_units(slots_ref, known_ref)
    units = []
    for k in range(TOP):
        products = picked_ref[:, k * D : (k + 1) * D].astype(F32) * grad
        unit = gates_ref[:, k : k + 1] * jnp.sum(products, axis=-1, keepdims=True)
        units.append(jnp.where(last, known_units[k], unit))
    input_grad, gain_one, gain_two, logits = attention_back(
        core_ref[0], grad, units, back_rows, x_ref, mine_ref, theirs_ref, slots_ref,
        gates_ref, state_ref.at[:, : 3 * D], state_ref.at[:, 3 * D : 5 * D], middle_ref, branch_ref, branch_grad_ref, projected_grad_ref, score_grad_ref, rel_ref,
    )
    input_ref[...] = input_grad
    moe_in = state_ref[:, 5 * D : 6 * D]
    lane = iota((ROWS, LANES), 1)
    extras = mm_tn(moe_in, logits[0]) + mm_tn(moe_in, logits[1])
    for at, terms in ((GAIN_AT, gain_one), (GAIN_AT + 1, gain_two)):
        column = (lane == at).astype(BF)
        for piece in halves(terms):
            extras = extras + mm_tn(piece, column)
    for part in range(2):
        table = bucket_rows(target_ref, part)
        for piece in halves(rel_ref[part]):
            extras = extras + mm_nt(table, piece)
    extras_ref[...] = extras
    given_ref[:, :QH] = projected_grad_ref[:, places(core_ref[0], QH)[1]]
    given_ref[:, QH:] = branch_ref[:, places(core_ref[0], OH)[1]]


def weight_totals(
    core_ref, factor_ref, factor_other_ref, projected_ref, branch_ref,
    other_ref, extras_ref, extras_other_ref, total_out, total_ref, semaphores,
):
    own, _ = places(core_ref[0], QH)
    own_out, _ = places(core_ref[0], OH)
    copies = []
    for piece in range(D // BLOCK):
        at = slice(piece * BLOCK, (piece + 1) * BLOCK)
        total_ref[at, :QH] = (
            mm_tn(factor_ref[:, at], projected_ref[:, own]) + mm_tn(factor_other_ref[:, at], other_ref[:, :QH])
        ).astype(BF)
        later = slice(D + piece * BLOCK, D + (piece + 1) * BLOCK)
        total_ref[at, QH : QH + OH] = (
            mm_tn(factor_ref[:, later], branch_ref[:, own_out]) + mm_tn(factor_other_ref[:, later], other_ref[:, QH:])
        ).astype(BF)
        total_ref[at, QH + OH :] = (extras_ref[at, :] + extras_other_ref[at, :].astype(F32)).astype(BF)
        copies.append(begin_copy(total_ref.at[at, :], total_out.at[at, :], semaphores.at[piece]))
    for copy in copies:
        copy.wait()


def add_arrived(core_ref, arrived_ref, kept_ref, given_ref):
    total = arrived_ref[0].astype(F32)
    for chip in range(1, arrived_ref.shape[0]):
        total = total + arrived_ref[chip].astype(F32)
    first = core_ref[0] == 0
    kept_ref[...] = jnp.where(first, total[:OWN], total[OWN:])
    given_ref[...] = jnp.where(first, total[OWN:, : QH + OH], total[:OWN, : QH + OH])


def lay_out(
    core_ref, kept_ref, other_ref, qkv_out, out_out, router_out, one_ref, two_ref, rel_ref, qkv_ref, out_ref, router_ref,
    semaphores,
):
    core = core_ref[0]
    own, other = places(core, QH)
    own_out, other_out = places(core, OH)
    extras = kept_ref[:, QH + OH :]
    for row in range(OWN):
        at = slice(row, row + 1)
        qkv_ref[row, :, own] = kept_ref[at, :QH]
        qkv_ref[row, :, other] = other_ref[at, :QH]
        out_ref[row, :, own_out] = kept_ref[at, QH : QH + OH]
        out_ref[row, :, other_out] = other_ref[at, QH:]
        router_ref[row] = extras[at, :EXPERTS]
    copies = [
        begin_copy(source, target, semaphores.at[at])
        for at, (source, target) in enumerate(((qkv_ref, qkv_out), (out_ref, out_out), (router_ref, router_out)))
    ]
    eye = iota((OWN, OWN), 0) == iota((OWN, OWN), 1)
    for k, target in enumerate((one_ref, two_ref)):
        column = extras[:, GAIN_AT + k : GAIN_AT + k + 1]
        target[...] = jnp.sum(jnp.where(eye, column, 0.0), axis=0, keepdims=True)
    rel_ref[...] = extras[:1, REL_AT : REL_AT + REL_OWN]
    for copy in copies:
        copy.wait()


def shaped(*pairs):
    return [jax.ShapeDtypeStruct(shape, dtype) for shape, dtype in pairs]


def fetching(body, wanted, count, *refs):
    inputs, rest = list(refs[:count]), refs[count:]
    spaces, semaphores, rest = rest[-1 - len(wanted) : -1], rest[-1], rest[: -1 - len(wanted)]
    copies = [
        begin_copy(inputs[at], space, semaphores.at[order]) for order, (at, space) in enumerate(zip(wanted, spaces))
    ]
    for at, space in zip(wanted, spaces):
        inputs[at] = space
    for copy in copies:
        copy.wait()
    body(*inputs, *rest)


def run(body, inputs, outputs, scratch=(), scalars=0, flops=0, far_in=(), far_out=(), fetched=()):
    size = sum(value.size * value.dtype.itemsize for value in inputs)
    size += sum(value.size * value.dtype.itemsize for value in outputs)
    scratch, far_in = list(scratch), tuple(far_in) + tuple(fetched)
    if fetched:
        body = functools.partial(fetching, body, fetched, len(inputs))
        scratch += [pltpu.VMEM(inputs[at].shape, inputs[at].dtype) for at in fetched]
        scratch += [pltpu.SemaphoreType.DMA((len(fetched),))]
    inputs = [
        pltpu.with_memory_space_constraint(value, pltpu.HBM) if at in far_in else value
        for at, value in enumerate(inputs)
    ]
    return pl.pallas_call(
        body,
        out_shape=[
            pltpu.HBM(value.shape, value.dtype) if at in far_out else value for at, value in enumerate(outputs)
        ],
        in_specs=[SMEM if at < scalars else HBM if at in far_in else VMEM for at in range(len(inputs))],
        out_specs=[HBM if at in far_out else VMEM for at in range(len(outputs))],
        scratch_shapes=scratch,
        compiler_params=pltpu.CompilerParams(vmem_limit_bytes=LIMIT),
        cost_estimate=pl.CostEstimate(flops=flops, bytes_accessed=size, transcendentals=0),
    )(*inputs)


def gather_dense(core, chips, kept, given):
    other = core_swap(given)
    pair = jnp.concatenate(
        [jnp.where(core == 0, kept, other), jnp.where(core == 0, other, kept)], axis=0
    )
    spread = jnp.broadcast_to(pair[None], (chips,) + pair.shape)
    mine = chip_exchange(spread).reshape(chips * 2 * OWN, WIDE)
    return mine, core_swap(mine)


def at_experts(arrived, run_part, tied=(), instead=lambda total: total):
    half = arrived.shape[0] // 2
    swapped = core_swap(arrived)
    early = run_part(slice(0, half), arrived, 0)
    swapped, first_made = lax.optimization_barrier((swapped, early[0]))
    other = run_part(slice(0, 2 * half), swapped, 1)
    arrived, other_made, tied = lax.optimization_barrier((arrived, other[0], tied))
    late = run_part(slice(half, 2 * half), arrived, 2)
    own = jnp.concatenate([first_made, late[0]], axis=0).astype(F32)
    returned = chip_exchange(instead((own + core_swap(other_made).astype(F32)).astype(BF)))
    return returned, (arrived, swapped), list(zip(early, other, late))[1:], tied


def join(pieces):
    return jnp.concatenate([pieces[0], pieces[2]], axis=0), pieces[1]


def per_device(
    tokens,
    cotangent,
    lengths,
    routes,
    buckets,
    qkv_weight,
    out_weight,
    router_weight,
    norm1_gain,
    norm2_gain,
    rel_bias,
    expert_in,
    expert_out,
):
    chips = lax.axis_size("chip")
    core = lax.axis_index("core")
    section = lax.axis_index("section")
    last = lax.axis_size("section") - 1
    first, second = expert_in[0, 0], expert_out[0, 0]
    where = core.astype(jnp.int32).reshape(1)
    is_last = (section == last).astype(jnp.int32).reshape(1)
    kept, given, mask, slots, slots_t, target = run(
        prepare,
        (
            where, lengths, qkv_weight[0], out_weight[0], router_weight[0], norm1_gain, norm2_gain,
            rel_bias, routes[0].transpose(0, 2, 1), buckets.reshape(1, TOK),
        ),
        shaped(
            ((OWN, WIDE), BF),
            ((OWN, WIDE), BF),
            ((ROWS, ROWS), F32),
            ((ROWS, TOP), jnp.int32),
            ((TOP, ROWS), jnp.int32),
            ((1, LANES), jnp.int32),
        ),
        scalars=1,
        fetched=tuple(range(1, 10)),
    )
    mine, theirs = gather_dense(core, chips, kept, given)

    row = (ROWS, D)
    flat = (chips * SLOTS, D)
    wide = (chips * SLOTS, FFH)
    dense_flops = 2 * ROWS * D * (4 * D + LANES) + 4 * H * ROWS * ROWS * LANES + 2 * ROWS * D * EXPERTS * SLOTS
    expert_flops = 4 * chips * SLOTS * D * FFH

    whole = pltpu.VMEM((D, WIDE), BF)
    squares = pltpu.VMEM((H, ROWS, ROWS), F32)
    small_squares = pltpu.VMEM((H, ROWS, ROWS), BF)
    begin = tokens.reshape(row)
    shared = (mine, theirs, mask, target, slots, slots_t)
    middle, gates, buffer = run(
        functools.partial(front, False),
        (where, begin) + shared,
        shaped((row, F32), ((ROWS, LANES), F32), ((EXPERTS, SLOTS, D), BF)),
        [pltpu.VMEM((ROWS, 3 * D), BF), pltpu.VMEM(row, BF), squares],
        scalars=1,
        flops=dense_flops,
    )
    def forward_part(at, rows, _):
        count = at.stop - at.start
        return run(
            functools.partial(expert_forward, at),
            (rows, first, second),
            shaped(((count, SLOTS, D), BF)),
            [pltpu.VMEM((count * SLOTS, FFH), BF)],
            flops=expert_flops * count // chips,
        )

    returned, _, _, _ = at_experts(chip_exchange(buffer), forward_part)
    result, picked = run(
        combine, (slots, gates, middle, returned), shaped((row, BF), ((ROWS, TOP * D), BF)), flops=4 * ROWS * D * EXPERTS * SLOTS
    )
    passed = lax.ppermute(result, "section", [(0, 1), (1, 0)])
    layer_in = jnp.where(section == 0, begin, passed)

    ending = cotangent.reshape(row)
    factors, state, middle, gates, buffer = run(
        functools.partial(front, True),
        (where, layer_in) + shared + (ending,),
        shaped(
            ((ROWS, 2 * D), BF),
            ((ROWS, STATE), BF),
            (row, F32),
            ((ROWS, LANES), F32),
            ((EXPERTS, 2 * SLOTS, D), BF),
        ),
        [
            pltpu.VMEM((ROWS, 3 * D), BF), pltpu.VMEM(row, BF), squares, small_squares, pltpu.VMEM(row, F32),
            pltpu.VMEM(row, BF), whole, pltpu.VMEM((ROWS, ROWS), F32), pltpu.SemaphoreType.DMA((5 + H,)),
        ],
        scalars=1,
        flops=dense_flops,
        far_in=(3, 4),
        far_out=(1, 2),
    )
    factors_other = core_swap(factors)
    def both_part(at, rows, _):
        count = at.stop - at.start
        piece = (count * SLOTS, FFH)
        return run(
            functools.partial(expert_both, at),
            (rows, first, second),
            shaped(((count, SLOTS, D + LANES), BF), ((count * SLOTS, D), BF), (piece, BF), (piece, BF)),
            [pltpu.VMEM((count * SLOTS, D), BF)] + [pltpu.VMEM(piece, BF)] * 3 + [pltpu.SemaphoreType.DMA((3,))],
            flops=2 * expert_flops * count // chips,
            far_out=(1, 2, 3),
        )

    known, arrived, (made, hidden, slope), (factors_other,) = at_experts(
        chip_exchange(buffer), both_part, (factors_other,)
    )
    (input_grad,) = run(
        finish_middle,
        (where, layer_in, ending, mine, theirs, slots, gates, state, middle, known),
        shaped((row, BF)),
        [pltpu.VMEM(row, BF), pltpu.VMEM(row, BF), pltpu.VMEM((ROWS, 3 * D), BF), small_squares],
        scalars=1,
        flops=2 * dense_flops,
    )
    input_grad, made = lax.optimization_barrier((input_grad, made))
    passed = lax.ppermute(input_grad, "section", [(0, 1), (1, 0)])
    made_own, made_other = join(made)
    outputs = (made_own.astype(F32) + core_swap(made_other).astype(F32)).astype(BF).reshape(EXPERTS, SLOTS, D)
    grad_out = jnp.where(section == last, ending, passed)

    (buffer,) = run(
        send_grad,
        (gates, grad_out, slots_t),
        shaped(((EXPERTS, SLOTS, D), BF)),
        flops=16 * dense_flops,
    )
    def back_part(at, rows, number):
        count = at.stop - at.start
        piece = (count * SLOTS, FFH)
        return run(
            functools.partial(expert_back, at),
            (rows, first, second, slope[number]),
            shaped(((count, SLOTS, D), BF), (piece, BF)),
            [pltpu.VMEM(piece, BF), pltpu.SemaphoreType.DMA((1,))],
            flops=expert_flops * count // chips,
            far_out=(1,),
        )

    buffer, outputs, is_last = lax.optimization_barrier((buffer, outputs, is_last))
    returned, grads, (pre_grad,), _ = at_experts(
        chip_exchange(buffer), back_part, instead=lambda total: jnp.where(section == last, outputs, total)
    )
    input_grad, projected_grad, branch, extras, given = run(
        finish_last,
        (
            where, is_last, layer_in, grad_out, mine, theirs, target, slots, gates, state, middle, picked, known,
            returned,
        ),
        shaped((row, F32), ((ROWS, 3 * D), BF), (row, BF), ((D, LANES), F32), ((ROWS, 2 * D), BF)),
        [
            pltpu.VMEM(row, BF), small_squares, pltpu.VMEM((2, LANES, LANES), F32),
        ],
        scalars=2,
        flops=2 * dense_flops,
    )
    (total,) = run(
        weight_totals,
        (
            where, factors, factors_other, projected_grad, branch,
            core_swap(given), extras, core_swap(extras.astype(BF)),
        ),
        shaped(((D, WIDE), BF)),
        [whole, pltpu.SemaphoreType.DMA((D // BLOCK,))],
        scalars=1,
        far_out=(0,),
        fetched=(1, 2),
        flops=4 * ROWS * D * WIDE,
    )
    total, hidden, grads, arrived, pre_grad, gated = lax.optimization_barrier(
        (total, hidden, grads, arrived, pre_grad, returned)
    )
    summands = chip_exchange(total.reshape(chips, 2 * OWN, WIDE))
    second_total = sum(mm_tn(value, rows.reshape(flat)) for value, rows in zip(join(hidden), grads))
    first_total = sum(mm_tn(rows[:, :SLOTS].reshape(flat), value) for rows, value in zip(arrived, join(pre_grad)))
    (result,) = run(
        last_output,
        (is_last, slots, gates, middle, gated, picked),
        shaped((row, BF)),
        scalars=1,
        flops=4 * ROWS * D * EXPERTS * SLOTS,
        fetched=(1, 2, 3, 4, 5),
    )
    summands, first_total, second_total, result = lax.optimization_barrier(
        (summands, first_total, second_total, result)
    )
    kept, given = run(
        add_arrived, (where, summands), shaped(((OWN, WIDE), F32), ((OWN, QH + OH), F32)), scalars=1
    )
    dense_grads = run(
        lay_out,
        (where, kept, core_swap(given)),
        shaped(
            ((OWN, 1, 3 * D), F32),
            ((OWN, 1, D), F32),
            ((OWN, 1, EXPERTS), F32),
            ((1, OWN), F32),
            ((1, OWN), F32),
            ((1, REL_OWN), F32),
        ),
        [
            pltpu.VMEM((OWN, 1, 3 * D), F32), pltpu.VMEM((OWN, 1, D), F32), pltpu.VMEM((OWN, 1, EXPERTS), F32),
            pltpu.SemaphoreType.DMA((3,)),
        ],
        scalars=1,
        far_out=(0, 1, 2),
    )
    return (
        result.reshape(1, MB, TOK, D),
        input_grad.reshape(1, MB, TOK, D),
        dense_grads[0].transpose(1, 0, 2),
        dense_grads[1].transpose(1, 0, 2),
        dense_grads[2].transpose(1, 0, 2),
        dense_grads[3],
        dense_grads[4],
        dense_grads[5],
        first_total[None, None],
        second_total[None, None],
    )


def solution(mesh):
    sections, members = mesh.devices.shape
    fine = Mesh(mesh.devices.reshape(sections, members // 2, 2), ("section", "chip", "core"))
    dp = ("chip", "core")
    return jax.shard_map(
        per_device,
        mesh=fine,
        in_specs=(
            P(None, dp, None),
            P(None, dp, None),
            P(None, dp, None),
            P("section", None, dp, None),
            P(),
            P("section", dp, None),
            P("section", dp, None),
            P("section", dp, None),
            P("section", dp),
            P("section", dp),
            P("section", dp),
            P("section", dp, None, None),
            P("section", dp, None, None),
        ),
        out_specs=(
            P("section", None, dp, None),
            P("section", None, dp, None),
            P("section", dp, None),
            P("section", dp, None),
            P("section", dp, None),
            P("section", dp),
            P("section", dp),
            P("section", dp),
            P("section", dp, None, None),
            P("section", dp, None, None),
        ),
        check_vma=False,
    )
```

```python
import functools

import jax
import jax.numpy as jnp
from jax import lax
from jax.experimental import pallas as pl
from jax.experimental.pallas import tpu as pltpu
from jax.sharding import Mesh, PartitionSpec as P

D = 768
H = 12
HD = 64
TOK = 64
MB = 2
NB = 32
TOP = 2
CAP = 8
ROWS = MB * TOK
LANES = 128
EXPERTS = 32
SLOTS = MB * CAP
FFH = 1536
QH = 3 * D // 2
OH = D // 2
WIDE = QH + OH + LANES
GAIN_AT = EXPERTS
REL_AT = EXPERTS + 2
REL_OWN = 6
OWN = 12
BLOCKS = 6
BLOCK = FFH // BLOCKS

EPSILON = 1e-06
SCALE = HD ** (-0.5)
BF = jnp.bfloat16
F32 = jnp.float32
VMEM = pl.BlockSpec(memory_space=pltpu.VMEM)
SMEM = pl.BlockSpec(memory_space=pltpu.SMEM)
HBM = pl.BlockSpec(memory_space=pltpu.HBM)
STATE = 6 * D
LIMIT = 24 * 1024 * 1024


def mm(a, b):
    return jnp.dot(a, b, preferred_element_type=F32)


def mm_nt(a, b):
    return lax.dot_general(a, b, (((1,), (1,)), ((), ())), preferred_element_type=F32)


def mm_tn(a, b):
    return lax.dot_general(a, b, (((0,), (0,)), ((), ())), preferred_element_type=F32)


def begin_copy(source, target, semaphore):
    copy = pltpu.make_async_copy(source, target, semaphore)
    copy.start()
    return copy


def halves(value):
    high = value.astype(BF)
    return high, (value - high.astype(F32)).astype(BF)


def core_swap(value):
    return lax.ppermute(value, "core", [(0, 1), (1, 0)])


def chip_exchange(value):
    return lax.all_to_all(value, "chip", split_axis=0, concat_axis=0, tiled=True)


def iota(shape, axis):
    return lax.broadcasted_iota(jnp.int32, shape, axis)


def places(core, width):
    mine = pl.multiple_of(core * width, LANES)
    theirs = pl.multiple_of((1 - core) * width, LANES)
    return pl.ds(mine, width), pl.ds(theirs, width)


def gain_rows(mine_ref):
    chosen = (iota((16, LANES), 1) == iota((16, LANES), 0) + GAIN_AT).astype(BF)
    return mm_nt(chosen, mine_ref[:, QH + OH :])


def norm_factor(values):
    return lax.rsqrt(jnp.mean(values * values, axis=-1, keepdims=True) + EPSILON)


def norm_back(values, gain, grad_in):
    factor = norm_factor(values)
    normed = values * factor
    weighted = grad_in * gain
    value_grad = factor * (weighted - normed * jnp.mean(weighted * normed, axis=-1, keepdims=True))
    return value_grad, grad_in * normed


def gelu_parts(pre):
    outer = 0.7978845608028654
    inner = outer * 0.044715
    square = pre * pre
    share = 0.5 + 0.5 * jnp.tanh(pre * (outer + inner * square))
    hidden = pre * share
    return share, hidden, square


def gelu_slope(share, hidden, square):
    outer = 0.7978845608028654
    inner = outer * 0.044715
    return share + hidden * (1.0 - share) * (2.0 * outer + 6.0 * inner * square)


def two_heads(values):
    low = iota((1, LANES), 1) < HD
    zero = jnp.zeros_like(values)
    return jnp.concatenate([jnp.where(low, values, zero), jnp.where(low, zero, values)], axis=0)


def slot_rows(slots_t_ref, k):
    return iota((EXPERTS * SLOTS, ROWS), 0) == slots_t_ref[k : k + 1, :]


def slot_columns(slots_ref, k):
    return iota((ROWS, EXPERTS * SLOTS), 1) == slots_ref[:, k : k + 1]


def bucket_rows(target_ref, part):
    return (iota((D, LANES), 0) == target_ref[...] + OWN * part).astype(BF)


def as_column(row_ref):
    size = row_ref.shape[1]
    eye = iota((size, size), 0) == iota((size, size), 1)
    return jnp.sum(jnp.where(eye, row_ref[...].astype(F32), 0.0), axis=1, keepdims=True)


def prepare(
    core_ref, lengths_ref, qkv_ref, out_ref, router_ref, one_ref, two_ref, rel_ref, routes_in, buckets_ref,
    kept_ref, given_ref, mask_ref, slots_ref, slots_t_ref, target_ref,
):
    core = core_ref[0]
    lane = iota((OWN, LANES), 1)
    extras = mm(router_ref[...], (iota((EXPERTS, LANES), 0) == iota((EXPERTS, LANES), 1)).astype(BF))
    extras = extras + jnp.where(lane == GAIN_AT, as_column(one_ref), 0.0)
    extras = extras + jnp.where(lane == GAIN_AT + 1, as_column(two_ref), 0.0)
    moved = iota((REL_OWN, LANES), 0) + REL_AT == iota((REL_OWN, LANES), 1)
    rel = jnp.sum(jnp.where(moved, as_column(rel_ref), 0.0), axis=0, keepdims=True)
    extras = extras + jnp.where(iota((OWN, LANES), 0) == 0, rel, 0.0)
    for target, at in zip((kept_ref, given_ref), (0, 1)):
        target[:, :QH] = qkv_ref[:, places(core, QH)[at]]
        target[:, QH : QH + OH] = out_ref[:, places(core, OH)[at]]
        target[:, QH + OH :] = extras.astype(BF)

    def segment(axis):
        place = iota((ROWS, ROWS), axis)
        early = (place >= lengths_ref[0, :, 0:1]).astype(jnp.int32)
        late = 2 + (place >= TOK + lengths_ref[1, :, 0:1]).astype(jnp.int32)
        return jnp.where(place < TOK, early, late)

    row, column = iota((ROWS, ROWS), 0), iota((ROWS, ROWS), 1)
    seen = (segment(0) == segment(1)) & (row <= column)
    mask_ref[...] = jnp.where(seen, 0.0, -1e30)
    together = (row < TOK) == (column < TOK)
    rows = [jnp.concatenate([routes_in[m, k : k + 1, :] for m in range(MB)], axis=1) for k in range(TOP)]
    columns = [jnp.sum(jnp.where(row == column, value, 0), axis=1, keepdims=True) for value in rows]
    for k in range(TOP):
        own, own_t = columns[k], rows[k]
        rank = jnp.zeros((ROWS, ROWS), jnp.int32)
        rank_t = jnp.zeros((ROWS, ROWS), jnp.int32)
        for other in range(TOP):
            same = together & (own == rows[other]) & (column < row)
            rank = rank + same.astype(jnp.int32)
            same_t = together & (columns[other] == own_t) & (row < column)
            rank_t = rank_t + same_t.astype(jnp.int32)
        micro = (iota((ROWS, 1), 0) >= TOK).astype(jnp.int32)
        micro_t = (iota((1, ROWS), 1) >= TOK).astype(jnp.int32)
        slots_ref[:, k : k + 1] = own * SLOTS + micro * CAP + jnp.sum(rank, axis=1, keepdims=True)
        slots_t_ref[k : k + 1, :] = own_t * SLOTS + micro_t * CAP + jnp.sum(rank_t, axis=0, keepdims=True)
    target_ref[...] = jnp.concatenate([buckets_ref[...] * (2 * OWN), jnp.zeros((1, LANES - TOK), jnp.int32)], axis=1)


def front(saving, core_ref, x_ref, mine_ref, theirs_ref, mask_ref, target_ref, slots_ref, slots_t_ref, *refs):
    if saving:
        grad_ref, factor_ref, state_ref, kept_ref, gates_ref, buffer_ref = refs[:6]
        projected_ref, attended_ref, scores_ref, probs_ref, middle_ref, moe_ref, theirs_space, mask_space, semaphores = refs[6:]
    else:
        middle_ref, gates_ref, buffer_ref, projected_ref, attended_ref, scores_ref = refs
        probs_ref = scores_ref
    core = core_ref[0]
    if saving:
        coming_theirs = begin_copy(theirs_ref, theirs_space, semaphores.at[0])
        coming_mask = begin_copy(mask_ref, mask_space, semaphores.at[4 + H])
        theirs_ref, mask_ref = theirs_space, mask_space
    x = x_ref[...].astype(F32)
    gains = gain_rows(mine_ref)
    normed = (x * norm_factor(x) * gains[0:1]).astype(BF)
    if saving:
        factor_ref[:, :D] = normed
    extras = mine_ref[:, QH + OH :]
    rel = [mm_tn(extras, bucket_rows(target_ref, part)) for part in range(2)]
    if saving:
        coming_mask.wait()
    mask = mask_ref[...]
    for head in range(H):
        row = REL_AT + head % REL_OWN
        spread = jnp.broadcast_to(rel[head // REL_OWN][row : row + 1, :], (ROWS, LANES))
        scores_ref[head] = pltpu.roll(spread, 0, 1, stride=1, stride_axis=0) + mask
    own, other = places(core, QH)
    projected_ref[:, own] = mm(normed, mine_ref[:, :QH]).astype(BF)
    if saving:
        coming_theirs.wait()
    projected_ref[:, other] = mm(normed, theirs_ref[:, :QH]).astype(BF)
    copies = []
    if saving:
        copies.append(begin_copy(projected_ref, state_ref.at[:, : 3 * D], semaphores.at[3 + H]))
    for pair in range(H // 2):
        at = pair * LANES
        query = projected_ref[:, at : at + LANES]
        scores = mm_nt(two_heads(projected_ref[:, D + at : D + at + LANES]), query) * SCALE
        for side in range(2):
            scores_ref[2 * pair + side] += scores[side * ROWS : (side + 1) * ROWS]
    for head in range(H):
        scores = scores_ref[head]
        raised = jnp.exp(scores - jnp.max(scores, axis=0, keepdims=True))
        probs = raised * (1.0 / jnp.sum(raised, axis=0, keepdims=True))
        probs_ref[head] = probs.astype(probs_ref.dtype)
    if saving:
        for head in range(H):
            place = state_ref.at[:, 3 * D + head * ROWS : 3 * D + (head + 1) * ROWS]
            copies.append(begin_copy(probs_ref.at[head], place, semaphores.at[3 + head]))
    for pair in range(H // 2):
        at = pair * LANES
        value = two_heads(projected_ref[:, 2 * D + at : 2 * D + at + LANES])
        probs = probs_ref[2 * pair : 2 * pair + 2].reshape(2 * ROWS, ROWS).astype(BF)
        attended_ref[:, at : at + LANES] = mm_tn(probs, value).astype(BF)
    attended = attended_ref[...]
    if saving:
        factor_ref[:, D:] = attended
    own, other = places(core, OH)
    middle_ref[:, own] = mm(attended, mine_ref[:, QH : QH + OH])
    middle_ref[:, other] = mm(attended, theirs_ref[:, QH : QH + OH])
    middle = x + middle_ref[...]
    middle_ref[...] = middle
    if saving:
        copies.append(begin_copy(middle_ref, kept_ref, semaphores.at[1]))
    moe_in = (middle * norm_factor(middle) * gains[1:2]).astype(BF)
    logits = mm(moe_in, extras)
    lane = iota((ROWS, LANES), 1)
    picked = [
        jnp.sum(jnp.where(lane == slots_ref[:, k : k + 1] // SLOTS, logits, 0.0), axis=-1, keepdims=True)
        for k in range(TOP)
    ]
    peak = jnp.maximum(picked[0], picked[1])
    raised = [jnp.exp(value - peak) for value in picked]
    gates = [value / (raised[0] + raised[1]) for value in raised]
    gates_ref[...] = jnp.where(lane == 0, gates[0], jnp.where(lane == 1, gates[1], 0.0))
    tables = [slot_rows(slots_t_ref, k) for k in range(TOP)]
    buffer = mm((tables[0] | tables[1]).astype(BF), moe_in).astype(BF)
    buffer_ref[:, :SLOTS, :] = buffer.reshape(EXPERTS, SLOTS, D)
    if saving:
        moe_ref[...] = moe_in
        copies.append(begin_copy(moe_ref, state_ref.at[:, 5 * D : 6 * D], semaphores.at[2]))
        grad = grad_ref[...].astype(F32)
        buffer_ref[:, SLOTS:, :] = spread_grad(tables, gates, grad).reshape(EXPERTS, SLOTS, D)
    for copy in copies:
        copy.wait()


def spread_grad(tables, gates, grad):
    return sum(
        mm(table.astype(BF), (gate * grad).astype(BF)) for table, gate in zip(tables, gates)
    ).astype(BF)


def send_grad(gates_ref, grad_ref, slots_t_ref, buffer_ref):
    grad = grad_ref[...].astype(F32)
    gates = [gates_ref[:, k : k + 1] for k in range(TOP)]
    tables = [slot_rows(slots_t_ref, k) for k in range(TOP)]
    buffer_ref[...] = spread_grad(tables, gates, grad).reshape(EXPERTS, SLOTS, D)


def expert_forward(at, rows_ref, first_ref, second_ref, made_ref, hidden_ref):
    rows = rows_ref[at].reshape(-1, D)
    for block in range(BLOCKS):
        part = slice(block * BLOCK, (block + 1) * BLOCK)
        _, hidden, _ = gelu_parts(mm(rows, first_ref[:, part]))
        hidden_ref[:, part] = hidden.astype(BF)
    made_ref[...] = mm(hidden_ref[...], second_ref[...]).astype(BF).reshape(made_ref.shape)


def expert_both(
    at, rows_ref, first_ref, second_ref, back_ref, made_out, hidden_out, slope_out, made_ref, hidden_ref, slope_ref,
    pre_ref, semaphores,
):
    rows = rows_ref[at, :SLOTS, :].reshape(-1, D)
    grads = rows_ref[at, SLOTS:, :].reshape(-1, D)
    for block in range(BLOCKS):
        part = slice(block * BLOCK, (block + 1) * BLOCK)
        share, hidden, square = gelu_parts(mm(rows, first_ref[:, part]))
        hidden_ref[:, part] = hidden.astype(BF)
        slope = gelu_slope(share, hidden, square)
        slope_ref[:, part] = slope.astype(BF)
        pre_ref[:, part] = (mm_nt(grads, second_ref[part, :]) * slope).astype(BF)
    copies = [
        begin_copy(hidden_ref, hidden_out, semaphores.at[0]),
        begin_copy(slope_ref, slope_out, semaphores.at[1]),
    ]
    made_ref[...] = mm(hidden_ref[...], second_ref[...]).astype(BF)
    copies.append(begin_copy(made_ref, made_out, semaphores.at[2]))
    back_ref[:, :, :D] = mm_nt(pre_ref[...], first_ref[...]).astype(BF).reshape(-1, SLOTS, D)
    unit = jnp.sum(made_ref[...].astype(F32) * grads.astype(F32), axis=-1, keepdims=True)
    lane = iota((grads.shape[0], LANES), 1)
    back_ref[:, :, D:] = jnp.where(lane == 0, unit, 0.0).astype(BF).reshape(-1, SLOTS, LANES)
    for copy in copies:
        copy.wait()


def expert_back(at, grads_ref, first_ref, second_ref, slope_ref, made_ref, pre_out, pre_ref, semaphores):
    grads = grads_ref[at].reshape(-1, D)
    for block in range(BLOCKS):
        part = slice(block * BLOCK, (block + 1) * BLOCK)
        slope = slope_ref[:, part].astype(F32)
        pre_ref[:, part] = (mm_nt(grads, second_ref[part, :]) * slope).astype(BF)
    leaving = begin_copy(pre_ref, pre_out, semaphores.at[0])
    made_ref[...] = mm_nt(pre_ref[...], first_ref[...]).astype(BF).reshape(made_ref.shape)
    leaving.wait()


def combine(slots_ref, gates_ref, middle_ref, returned_ref, out_ref, picked_ref=None):
    returned = returned_ref[...].reshape(-1, D)
    out = middle_ref[...]
    for k in range(TOP):
        rows = mm(slot_columns(slots_ref, k).astype(BF), returned)
        out = out + gates_ref[:, k : k + 1] * rows
        if picked_ref is not None:
            picked_ref[:, k * D : (k + 1) * D] = rows.astype(BF)
    out_ref[...] = out.astype(BF)


def last_output(last_ref, slots_ref, gates_ref, middle_ref, returned_ref, picked_ref, out_ref):
    returned = returned_ref[...].reshape(-1, D)
    out = middle_ref[...]
    for k in range(TOP):
        rows = mm(slot_columns(slots_ref, k).astype(BF), returned)
        known = picked_ref[:, k * D : (k + 1) * D].astype(F32)
        out = out + gates_ref[:, k : k + 1] * jnp.where(last_ref[0] == 1, rows, known)
    out_ref[...] = out.astype(BF)


def attention_back(
    core, grad, units, back_rows, x_ref, mine_ref, theirs_ref, slots_ref, gates_ref, projected_ref,
    probs_ref, middle_ref, branch_ref, branch_grad_ref, projected_grad_ref, score_grad_ref, rel_ref=None,
):
    gates = [gates_ref[:, k : k + 1] for k in range(TOP)]
    shared = units[0] + units[1]
    lane = iota((ROWS, LANES), 1)
    logit_grad = sum(
        jnp.where(lane == slots_ref[:, k : k + 1] // SLOTS, units[k] - gates[k] * shared, 0.0)
        for k in range(TOP)
    )
    extras = mine_ref[:, QH + OH :]
    logit_high, logit_low = halves(logit_grad)
    tables = (slot_columns(slots_ref, 0) | slot_columns(slots_ref, 1)).astype(BF)
    moe_grad = mm(tables, back_rows) + mm_nt(logit_high, extras) + mm_nt(logit_low, extras)
    gains = gain_rows(mine_ref)
    middle_grad, gain_two = norm_back(middle_ref[...], gains[1:2], moe_grad)
    middle_grad = middle_grad + grad
    branch_ref[...] = middle_grad.astype(BF)
    own, other = places(core, OH)
    branch_grad_ref[...] = (
        mm_nt(branch_ref[:, own], mine_ref[:, QH : QH + OH])
        + mm_nt(branch_ref[:, other], theirs_ref[:, QH : QH + OH])
    ).astype(BF)
    for pair in range(H // 2):
        at = pair * LANES
        value = two_heads(projected_ref[:, 2 * D + at : 2 * D + at + LANES])
        coming = branch_grad_ref[:, at : at + LANES]
        prob_grad = mm_nt(value, coming)
        for side in range(2):
            head = 2 * pair + side
            probs = probs_ref[:, head * ROWS : (head + 1) * ROWS].astype(F32)
            own_grad = prob_grad[side * ROWS : (side + 1) * ROWS]
            score_grad = probs * (own_grad - jnp.sum(probs * own_grad, axis=0, keepdims=True))
            score_grad_ref[head] = score_grad.astype(BF)
    for pair in range(H // 2):
        at = pair * LANES
        query = two_heads(projected_ref[:, at : at + LANES])
        key = two_heads(projected_ref[:, D + at : D + at + LANES])
        coming = two_heads(branch_grad_ref[:, at : at + LANES])
        probs = probs_ref[:, 2 * pair * ROWS : 2 * (pair + 1) * ROWS]
        tall = score_grad_ref[2 * pair : 2 * pair + 2].reshape(2 * ROWS, ROWS)
        wide = jnp.concatenate([tall[:ROWS], tall[ROWS:]], axis=1)
        projected_grad_ref[:, at : at + LANES] = (mm_tn(tall, key) * SCALE).astype(BF)
        projected_grad_ref[:, D + at : D + at + LANES] = (mm(wide, query) * SCALE).astype(BF)
        projected_grad_ref[:, 2 * D + at : 2 * D + at + LANES] = mm(probs, coming).astype(BF)
    if rel_ref is not None:
        backwards = (iota((ROWS, ROWS), 0) + iota((ROWS, ROWS), 1) == ROWS - 1).astype(BF)
        for head in range(H):
            turned = pltpu.roll(mm(backwards, score_grad_ref[head]), 1, 1, stride=1, stride_axis=0)
            row = REL_AT + head % REL_OWN
            rel_ref[head // REL_OWN, row : row + 1, :] = jnp.sum(turned, axis=0, keepdims=True)
    own, other = places(core, QH)
    normed_grad = mm_nt(projected_grad_ref[:, own], mine_ref[:, :QH]) + mm_nt(
        projected_grad_ref[:, other], theirs_ref[:, :QH]
    )
    x_grad, gain_one = norm_back(x_ref[...].astype(F32), gains[0:1], normed_grad)
    return x_grad + middle_grad, gain_one, gain_two, (logit_high, logit_low)


def sent_units(slots_ref, returned_ref):
    sums = returned_ref[:, :, D:].reshape(-1, LANES)
    return [mm(slot_columns(slots_ref, k).astype(BF), sums)[:, :1] for k in range(TOP)]


def finish_middle(
    core_ref, x_ref, grad_ref, mine_ref, theirs_ref, slots_ref, gates_ref, state_ref, middle_ref, returned_ref,
    input_ref, branch_ref, branch_grad_ref, projected_grad_ref, score_grad_ref,
):
    back_rows = returned_ref[:, :, :D].reshape(-1, D)
    units = sent_units(slots_ref, returned_ref)
    input_grad, _, _, _ = attention_back(
        core_ref[0], grad_ref[...].astype(F32), units, back_rows, x_ref, mine_ref, theirs_ref, slots_ref,
        gates_ref, state_ref.at[:, : 3 * D], state_ref.at[:, 3 * D : 5 * D], middle_ref, branch_ref,
        branch_grad_ref, projected_grad_ref, score_grad_ref,
    )
    input_ref[...] = input_grad.astype(BF)


def finish_last(
    core_ref, last_ref, x_ref, grad_ref, mine_ref, theirs_ref, target_ref, slots_ref, gates_ref, state_ref, middle_ref,
    picked_ref, known_ref, returned_ref, input_ref, projected_grad_ref, branch_ref, extras_ref, given_ref, branch_grad_ref,
    score_grad_ref, rel_ref,
):
    rel_ref[...] = jnp.zeros_like(rel_ref)
    last = last_ref[0] == 1
    back_rows = jnp.where(last, known_ref[:, :, :D].reshape(-1, D), returned_ref[...].reshape(-1, D))
    grad = grad_ref[...].astype(F32)
    known_units = sent_units(slots_ref, known_ref)
    units = []
    for k in range(TOP):
        products = picked_ref[:, k * D : (k + 1) * D].astype(F32) * grad
        unit = gates_ref[:, k : k + 1] * jnp.sum(products, axis=-1, keepdims=True)
        units.append(jnp.where(last, known_units[k], unit))
    input_grad, gain_one, gain_two, logits = attention_back(
        core_ref[0], grad, units, back_rows, x_ref, mine_ref, theirs_ref, slots_ref,
        gates_ref, state_ref.at[:, : 3 * D], state_ref.at[:, 3 * D : 5 * D], middle_ref, branch_ref, branch_grad_ref, projected_grad_ref, score_grad_ref, rel_ref,
    )
    input_ref[...] = input_grad
    moe_in = state_ref[:, 5 * D : 6 * D]
    lane = iota((ROWS, LANES), 1)
    extras = mm_tn(moe_in, logits[0]) + mm_tn(moe_in, logits[1])
    for at, terms in ((GAIN_AT, gain_one), (GAIN_AT + 1, gain_two)):
        column = (lane == at).astype(BF)
        for piece in halves(terms):
            extras = extras + mm_tn(piece, column)
    for part in range(2):
        table = bucket_rows(target_ref, part)
        for piece in halves(rel_ref[part]):
            extras = extras + mm_nt(table, piece)
    extras_ref[...] = extras
    given_ref[:, :QH] = projected_grad_ref[:, places(core_ref[0], QH)[1]]
    given_ref[:, QH:] = branch_ref[:, places(core_ref[0], OH)[1]]


def weight_totals(
    core_ref, factor_ref, factor_other_ref, projected_ref, branch_ref,
    other_ref, extras_ref, extras_other_ref, total_out, total_ref, semaphores,
):
    own, _ = places(core_ref[0], QH)
    own_out, _ = places(core_ref[0], OH)
    copies = []
    for piece in range(D // BLOCK):
        at = slice(piece * BLOCK, (piece + 1) * BLOCK)
        total_ref[at, :QH] = (
            mm_tn(factor_ref[:, at], projected_ref[:, own]) + mm_tn(factor_other_ref[:, at], other_ref[:, :QH])
        ).astype(BF)
        later = slice(D + piece * BLOCK, D + (piece + 1) * BLOCK)
        total_ref[at, QH : QH + OH] = (
            mm_tn(factor_ref[:, later], branch_ref[:, own_out]) + mm_tn(factor_other_ref[:, later], other_ref[:, QH:])
        ).astype(BF)
        total_ref[at, QH + OH :] = (extras_ref[at, :] + extras_other_ref[at, :].astype(F32)).astype(BF)
        copies.append(begin_copy(total_ref.at[at, :], total_out.at[at, :], semaphores.at[piece]))
    for copy in copies:
        copy.wait()


def add_arrived(core_ref, arrived_ref, kept_ref, given_ref):
    total = arrived_ref[0].astype(F32)
    for chip in range(1, arrived_ref.shape[0]):
        total = total + arrived_ref[chip].astype(F32)
    first = core_ref[0] == 0
    kept_ref[...] = jnp.where(first, total[:OWN], total[OWN:])
    given_ref[...] = jnp.where(first, total[OWN:, : QH + OH], total[:OWN, : QH + OH])


def lay_out(
    core_ref, kept_ref, other_ref, qkv_out, out_out, router_out, one_ref, two_ref, rel_ref, qkv_ref, out_ref, router_ref,
    semaphores,
):
    core = core_ref[0]
    own, other = places(core, QH)
    own_out, other_out = places(core, OH)
    extras = kept_ref[:, QH + OH :]
    for row in range(OWN):
        at = slice(row, row + 1)
        qkv_ref[row, :, own] = kept_ref[at, :QH]
        qkv_ref[row, :, other] = other_ref[at, :QH]
        out_ref[row, :, own_out] = kept_ref[at, QH : QH + OH]
        out_ref[row, :, other_out] = other_ref[at, QH:]
        router_ref[row] = extras[at, :EXPERTS]
    copies = [
        begin_copy(source, target, semaphores.at[at])
        for at, (source, target) in enumerate(((qkv_ref, qkv_out), (out_ref, out_out), (router_ref, router_out)))
    ]
    eye = iota((OWN, OWN), 0) == iota((OWN, OWN), 1)
    for k, target in enumerate((one_ref, two_ref)):
        column = extras[:, GAIN_AT + k : GAIN_AT + k + 1]
        target[...] = jnp.sum(jnp.where(eye, column, 0.0), axis=0, keepdims=True)
    rel_ref[...] = extras[:1, REL_AT : REL_AT + REL_OWN]
    for copy in copies:
        copy.wait()


def shaped(*pairs):
    return [jax.ShapeDtypeStruct(shape, dtype) for shape, dtype in pairs]


def fetching(body, wanted, count, *refs):
    inputs, rest = list(refs[:count]), refs[count:]
    spaces, semaphores, rest = rest[-1 - len(wanted) : -1], rest[-1], rest[: -1 - len(wanted)]
    copies = [
        begin_copy(inputs[at], space, semaphores.at[order]) for order, (at, space) in enumerate(zip(wanted, spaces))
    ]
    for at, space in zip(wanted, spaces):
        inputs[at] = space
    for copy in copies:
        copy.wait()
    body(*inputs, *rest)


def run(body, inputs, outputs, scratch=(), scalars=0, flops=0, far_in=(), far_out=(), fetched=()):
    size = sum(value.size * value.dtype.itemsize for value in inputs)
    size += sum(value.size * value.dtype.itemsize for value in outputs)
    scratch, far_in = list(scratch), tuple(far_in) + tuple(fetched)
    if fetched:
        body = functools.partial(fetching, body, fetched, len(inputs))
        scratch += [pltpu.VMEM(inputs[at].shape, inputs[at].dtype) for at in fetched]
        scratch += [pltpu.SemaphoreType.DMA((len(fetched),))]
    inputs = [
        pltpu.with_memory_space_constraint(value, pltpu.HBM) if at in far_in else value
        for at, value in enumerate(inputs)
    ]
    return pl.pallas_call(
        body,
        out_shape=[
            pltpu.HBM(value.shape, value.dtype) if at in far_out else value for at, value in enumerate(outputs)
        ],
        in_specs=[SMEM if at < scalars else HBM if at in far_in else VMEM for at in range(len(inputs))],
        out_specs=[HBM if at in far_out else VMEM for at in range(len(outputs))],
        scratch_shapes=scratch,
        compiler_params=pltpu.CompilerParams(vmem_limit_bytes=LIMIT),
        cost_estimate=pl.CostEstimate(flops=flops, bytes_accessed=size, transcendentals=0),
    )(*inputs)


def gather_dense(core, chips, kept, given):
    other = core_swap(given)
    pair = jnp.concatenate(
        [jnp.where(core == 0, kept, other), jnp.where(core == 0, other, kept)], axis=0
    )
    spread = jnp.broadcast_to(pair[None], (chips,) + pair.shape)
    mine = chip_exchange(spread).reshape(chips * 2 * OWN, WIDE)
    return mine, core_swap(mine)


def at_experts(arrived, run_part, tied=(), instead=lambda total: total):
    half = arrived.shape[0] // 2
    swapped = core_swap(arrived)
    early = run_part(slice(0, half), arrived, 0)
    swapped, first_made = lax.optimization_barrier((swapped, early[0]))
    other = run_part(slice(0, 2 * half), swapped, 1)
    arrived, other_made, tied = lax.optimization_barrier((arrived, other[0], tied))
    late = run_part(slice(half, 2 * half), arrived, 2)
    own = jnp.concatenate([first_made, late[0]], axis=0).astype(F32)
    returned = chip_exchange(instead((own + core_swap(other_made).astype(F32)).astype(BF)))
    return returned, (arrived, swapped), list(zip(early, other, late))[1:], tied


def join(pieces):
    return jnp.concatenate([pieces[0], pieces[2]], axis=0), pieces[1]


def per_device(
    tokens,
    cotangent,
    lengths,
    routes,
    buckets,
    qkv_weight,
    out_weight,
    router_weight,
    norm1_gain,
    norm2_gain,
    rel_bias,
    expert_in,
    expert_out,
):
    chips = lax.axis_size("chip")
    core = lax.axis_index("core")
    section = lax.axis_index("section")
    last = lax.axis_size("section") - 1
    first, second = expert_in[0, 0], expert_out[0, 0]
    where = core.astype(jnp.int32).reshape(1)
    is_last = (section == last).astype(jnp.int32).reshape(1)
    kept, given, mask, slots, slots_t, target = run(
        prepare,
        (
            where, lengths, qkv_weight[0], out_weight[0], router_weight[0], norm1_gain, norm2_gain,
            rel_bias, routes[0].transpose(0, 2, 1), buckets.reshape(1, TOK),
        ),
        shaped(
            ((OWN, WIDE), BF),
            ((OWN, WIDE), BF),
            ((ROWS, ROWS), F32),
            ((ROWS, TOP), jnp.int32),
            ((TOP, ROWS), jnp.int32),
            ((1, LANES), jnp.int32),
        ),
        scalars=1,
        fetched=tuple(range(1, 10)),
    )
    mine, theirs = gather_dense(core, chips, kept, given)

    row = (ROWS, D)
    flat = (chips * SLOTS, D)
    wide = (chips * SLOTS, FFH)
    dense_flops = 2 * ROWS * D * (4 * D + LANES) + 4 * H * ROWS * ROWS * LANES + 2 * ROWS * D * EXPERTS * SLOTS
    expert_flops = 4 * chips * SLOTS * D * FFH

    whole = pltpu.VMEM((D, WIDE), BF)
    squares = pltpu.VMEM((H, ROWS, ROWS), F32)
    small_squares = pltpu.VMEM((H, ROWS, ROWS), BF)
    begin = tokens.reshape(row)
    shared = (mine, theirs, mask, target, slots, slots_t)
    middle, gates, buffer = run(
        functools.partial(front, False),
        (where, begin) + shared,
        shaped((row, F32), ((ROWS, LANES), F32), ((EXPERTS, SLOTS, D), BF)),
        [pltpu.VMEM((ROWS, 3 * D), BF), pltpu.VMEM(row, BF), squares],
        scalars=1,
        flops=dense_flops,
    )
    def forward_part(at, rows, _):
        count = at.stop - at.start
        return run(
            functools.partial(expert_forward, at),
            (rows, first, second),
            shaped(((count, SLOTS, D), BF)),
            [pltpu.VMEM((count * SLOTS, FFH), BF)],
            flops=expert_flops * count // chips,
        )

    returned, _, _, _ = at_experts(chip_exchange(buffer), forward_part)
    result, picked = run(
        combine, (slots, gates, middle, returned), shaped((row, BF), ((ROWS, TOP * D), BF)), flops=4 * ROWS * D * EXPERTS * SLOTS
    )
    passed = lax.ppermute(result, "section", [(0, 1), (1, 0)])
    layer_in = jnp.where(section == 0, begin, passed)

    ending = cotangent.reshape(row)
    factors, state, middle, gates, buffer = run(
        functools.partial(front, True),
        (where, layer_in) + shared + (ending,),
        shaped(
            ((ROWS, 2 * D), BF),
            ((ROWS, STATE), BF),
            (row, F32),
            ((ROWS, LANES), F32),
            ((EXPERTS, 2 * SLOTS, D), BF),
        ),
        [
            pltpu.VMEM((ROWS, 3 * D), BF), pltpu.VMEM(row, BF), squares, small_squares, pltpu.VMEM(row, F32),
            pltpu.VMEM(row, BF), whole, pltpu.VMEM((ROWS, ROWS), F32), pltpu.SemaphoreType.DMA((5 + H,)),
        ],
        scalars=1,
        flops=dense_flops,
        far_in=(3, 4),
        far_out=(1, 2),
    )
    factors_other = core_swap(factors)
    def both_part(at, rows, _):
        count = at.stop - at.start
        piece = (count * SLOTS, FFH)
        return run(
            functools.partial(expert_both, at),
            (rows, first, second),
            shaped(((count, SLOTS, D + LANES), BF), ((count * SLOTS, D), BF), (piece, BF), (piece, BF)),
            [pltpu.VMEM((count * SLOTS, D), BF)] + [pltpu.VMEM(piece, BF)] * 3 + [pltpu.SemaphoreType.DMA((3,))],
            flops=2 * expert_flops * count // chips,
            far_out=(1, 2, 3),
        )

    known, arrived, (made, hidden, slope), (factors_other,) = at_experts(
        chip_exchange(buffer), both_part, (factors_other,)
    )
    (input_grad,) = run(
        finish_middle,
        (where, layer_in, ending, mine, theirs, slots, gates, state, middle, known),
        shaped((row, BF)),
        [pltpu.VMEM(row, BF), pltpu.VMEM(row, BF), pltpu.VMEM((ROWS, 3 * D), BF), small_squares],
        scalars=1,
        flops=2 * dense_flops,
    )
    input_grad, made = lax.optimization_barrier((input_grad, made))
    passed = lax.ppermute(input_grad, "section", [(0, 1), (1, 0)])
    made_own, made_other = join(made)
    outputs = (made_own.astype(F32) + core_swap(made_other).astype(F32)).astype(BF).reshape(EXPERTS, SLOTS, D)
    grad_out = jnp.where(section == last, ending, passed)

    (buffer,) = run(
        send_grad,
        (gates, grad_out, slots_t),
        shaped(((EXPERTS, SLOTS, D), BF)),
        flops=16 * dense_flops,
    )
    def back_part(at, rows, number):
        count = at.stop - at.start
        piece = (count * SLOTS, FFH)
        return run(
            functools.partial(expert_back, at),
            (rows, first, second, slope[number]),
            shaped(((count, SLOTS, D), BF), (piece, BF)),
            [pltpu.VMEM(piece, BF), pltpu.SemaphoreType.DMA((1,))],
            flops=expert_flops * count // chips,
            far_out=(1,),
        )

    buffer, outputs, is_last = lax.optimization_barrier((buffer, outputs, is_last))
    returned, grads, (pre_grad,), _ = at_experts(
        chip_exchange(buffer), back_part, instead=lambda total: jnp.where(section == last, outputs, total)
    )
    input_grad, projected_grad, branch, extras, given = run(
        finish_last,
        (
            where, is_last, layer_in, grad_out, mine, theirs, target, slots, gates, state, middle, picked, known,
            returned,
        ),
        shaped((row, F32), ((ROWS, 3 * D), BF), (row, BF), ((D, LANES), F32), ((ROWS, 2 * D), BF)),
        [
            pltpu.VMEM(row, BF), small_squares, pltpu.VMEM((2, LANES, LANES), F32),
        ],
        scalars=2,
        fetched=(8, 12),
        flops=2 * dense_flops,
    )
    (total,) = run(
        weight_totals,
        (
            where, factors, factors_other, projected_grad, branch,
            core_swap(given), extras, core_swap(extras.astype(BF)),
        ),
        shaped(((D, WIDE), BF)),
        [whole, pltpu.SemaphoreType.DMA((D // BLOCK,))],
        scalars=1,
        far_out=(0,),
        fetched=(1, 2),
        flops=4 * ROWS * D * WIDE,
    )
    total, hidden, grads, arrived, pre_grad, gated = lax.optimization_barrier(
        (total, hidden, grads, arrived, pre_grad, returned)
    )
    summands = chip_exchange(total.reshape(chips, 2 * OWN, WIDE))
    second_total = sum(mm_tn(value, rows.reshape(flat)) for value, rows in zip(join(hidden), grads))
    first_total = sum(mm_tn(rows[:, :SLOTS].reshape(flat), value) for rows, value in zip(arrived, join(pre_grad)))
    (result,) = run(
        last_output,
        (is_last, slots, gates, middle, gated, picked),
        shaped((row, BF)),
        scalars=1,
        flops=4 * ROWS * D * EXPERTS * SLOTS,
        fetched=(1, 2, 3, 4, 5),
    )
    summands, first_total, second_total, result = lax.optimization_barrier(
        (summands, first_total, second_total, result)
    )
    kept, given = run(
        add_arrived, (where, summands), shaped(((OWN, WIDE), F32), ((OWN, QH + OH), F32)), scalars=1
    )
    dense_grads = run(
        lay_out,
        (where, kept, core_swap(given)),
        shaped(
            ((OWN, 1, 3 * D), F32),
            ((OWN, 1, D), F32),
            ((OWN, 1, EXPERTS), F32),
            ((1, OWN), F32),
            ((1, OWN), F32),
            ((1, REL_OWN), F32),
        ),
        [
            pltpu.VMEM((OWN, 1, 3 * D), F32), pltpu.VMEM((OWN, 1, D), F32), pltpu.VMEM((OWN, 1, EXPERTS), F32),
            pltpu.SemaphoreType.DMA((3,)),
        ],
        scalars=1,
        far_out=(0, 1, 2),
    )
    return (
        result.reshape(1, MB, TOK, D),
        input_grad.reshape(1, MB, TOK, D),
        dense_grads[0].transpose(1, 0, 2),
        dense_grads[1].transpose(1, 0, 2),
        dense_grads[2].transpose(1, 0, 2),
        dense_grads[3],
        dense_grads[4],
        dense_grads[5],
        first_total[None, None],
        second_total[None, None],
    )


def solution(mesh):
    sections, members = mesh.devices.shape
    fine = Mesh(mesh.devices.reshape(sections, members // 2, 2), ("section", "chip", "core"))
    dp = ("chip", "core")
    return jax.shard_map(
        per_device,
        mesh=fine,
        in_specs=(
            P(None, dp, None),
            P(None, dp, None),
            P(None, dp, None),
            P("section", None, dp, None),
            P(),
            P("section", dp, None),
            P("section", dp, None),
            P("section", dp, None),
            P("section", dp),
            P("section", dp),
            P("section", dp),
            P("section", dp, None, None),
            P("section", dp, None, None),
        ),
        out_specs=(
            P("section", None, dp, None),
            P("section", None, dp, None),
            P("section", dp, None),
            P("section", dp, None),
            P("section", dp, None),
            P("section", dp),
            P("section", dp),
            P("section", dp),
            P("section", dp, None, None),
            P("section", dp, None, None),
        ),
        check_vma=False,
    )
```
